32 devices in a mesh: freq: 8 (over y, x, core), chan: 4 (over z).
Axes of the slice: x: 2, y: 2, z: 4, core: 2. Of those that a mesh axis runs over, the one named last changes fastest.
Arguments:
- factor: bfloat16 [512, 2, 128, 128], P('freq', None, 'chan'), may hold values from -0.2 to 1.2, as said below
- spectrum: bfloat16 [512, 2, 128, 128], P('freq', None, 'chan'), may hold values from -2 to 5, as said below
- guess_scale: float32 [512], P('freq'), may hold values from 0.1 to 0.3
- lag_cutoff: int32 [1], replicated, may hold values from 64 to 255
Outputs:
- new_factor: float32 [512, 2, 128, 128], P('freq', None, None, 'chan')
The draws below stay inside these ranges and needn't reach their ends.
Inputs may be any that keep to these rules, and one draw needn't show every extreme that they name: The real part of factor is the identity plus independent entries of spread about 0.35 / sqrt(128). At every frequency spectrum is Hermitian: its real part symmetric, its imaginary part antisymmetric with a zero diagonal; it is positive definite.
All inputs are finite; a program needn't handle non-finite values.
Results may differ from the reference program's by a relative error of at most 0.00105.
Values may be sent and summed in bfloat16 or wider, within the bound.
No kernel may reach another device: no remote copies, remote signals or barrier semaphores. Data moves between devices by JAX's collectives and lax.ppermute only.
A program may use at most 128 MiB of HBM per device.

```python
import math
import jax
import jax.numpy as jnp
from jax import lax

C = 128
F = 512
ITERS = 8


def noise_pair(key, shape):
    key_a = jax.random.fold_in(key, 17)
    key_b = jax.random.fold_in(key, 29)
    first_noise = jnp.clip(jax.random.normal(key_a, shape, jnp.float32), -4.0, 4.0)
    second_noise = jnp.clip(jax.random.normal(key_b, shape, jnp.float32), -4.0, 4.0)
    return (first_noise, second_noise)


def draw_factor(key, part):
    first_noise, second_noise = noise_pair(key, (F, C, C))
    spread = 0.35 / math.sqrt(C)
    part_re = jnp.eye(C, dtype=jnp.float32)[None] + spread * first_noise
    part_im = spread * second_noise
    return jnp.stack([part_re, part_im], axis=1).astype(jnp.bfloat16)


def draw_spectrum(key, part):
    first_noise, second_noise = noise_pair(key, (F, C, C))
    spread = 0.25 / math.sqrt(C)
    part_re = spread * (first_noise + jnp.swapaxes(first_noise, 1, 2)) + 1.5 * jnp.eye(C, dtype=jnp.float32)[None]
    part_im = spread * (second_noise - jnp.swapaxes(second_noise, 1, 2))
    logs = jax.random.uniform(jax.random.fold_in(key, 41), (F, C), jnp.float32, math.log(0.5), math.log(2.0))
    roots = jnp.exp(0.5 * logs)
    outer_scale = roots[:, :, None] * roots[:, None, :]
    return jnp.stack([part_re * outer_scale, part_im * outer_scale], axis=1).astype(jnp.bfloat16)


def levels(own_key, shape, cuts, low, high):
    def one(position, shards_of):
        steps = jax.random.uniform(jax.random.fold_in(jax.random.fold_in(own_key, 6), position), (shards_of,), jnp.float32, low / len(cuts), high / len(cuts))
        return jnp.repeat(jnp.exp(steps), shape[position] // shards_of).reshape((-1,) + (1,) * (len(shape) - position - 1))

    level = one(*cuts[0])
    for cut in cuts[1:]:
        level = level * one(*cut)
    return level


def setup_inputs(seed: int = 0) -> dict:
    key_of = jax.random.split(jax.random.key(seed), 5)
    return {
        "factor": draw_factor(jax.random.fold_in(key_of[4], 71), 0),
        "spectrum": draw_spectrum(jax.random.fold_in(key_of[4], 71), 0),
        "guess_scale": jnp.clip(jnp.exp(math.log(0.3) - 1.0986123 * jax.random.uniform(key_of[2], (F,), jnp.float32) ** levels(key_of[2], (F,), ((0, 8),), -0.2, 0.2)), 0.1, 0.3),
        "lag_cutoff": jax.random.randint(key_of[3], (1,), F // 8, F // 2).astype(jnp.int32),
    }


def matmul(matrix_a, matrix_b):
    return jnp.einsum("fij,fjk->fik", matrix_a, matrix_b, precision=lax.Precision.HIGHEST)


def complex_product(left, right):
    left_re, left_im = left[:, 0], left[:, 1]
    right_re, right_im = right[:, 0], right[:, 1]
    part_re = matmul(left_re, right_re) - matmul(left_im, right_im)
    part_im = matmul(left_re, right_im) + matmul(left_im, right_re)
    return jnp.stack([part_re, part_im], axis=1)


def adjoint(matrix):
    return jnp.stack([jnp.swapaxes(matrix[:, 0], -1, -2), -jnp.swapaxes(matrix[:, 1], -1, -2)], axis=1)


def reference(factor, spectrum, guess_scale, lag_cutoff):
    factor_f = factor.astype(jnp.float32)
    spectrum_f = spectrum.astype(jnp.float32)
    inverse = guess_scale.astype(jnp.float32)[:, None, None, None] * adjoint(factor_f)
    for iteration in range(ITERS):
        inverse = 2.0 * inverse - complex_product(complex_product(inverse, factor_f), inverse)
    middle = complex_product(complex_product(inverse, spectrum_f), adjoint(inverse))
    middle = middle.at[:, 0].add(jnp.eye(C, dtype=jnp.float32))
    complex_g = lax.complex(middle[:, 0], middle[:, 1])
    lag_terms = jnp.fft.ifft(complex_g, axis=0)
    lag_index = jnp.arange(F, dtype=jnp.int32)
    keep = jnp.where(lag_index == 0, 0.5, jnp.where((lag_index >= 1) & (lag_index <= lag_cutoff[0]), 1.0, 0.0))
    projected = jnp.fft.fft(lag_terms * keep[:, None, None], axis=0)
    causal = jnp.stack([jnp.real(projected), jnp.imag(projected)], axis=1).astype(jnp.float32)
    return complex_product(factor_f, causal)
```

```python
import functools
import math

import jax
import jax.numpy as jnp
from jax import lax
from jax.experimental import pallas as pl
from jax.experimental.pallas import tpu as pltpu
from jax.sharding import PartitionSpec as P

ITERS = 8
F32 = jnp.float32
BF16 = jnp.bfloat16
MIB = 1024 * 1024
NN = (((1,), (0,)), ((), ()))
NT = (((1,), (1,)), ((), ()))
TN = (((0,), (0,)), ((), ()))


def dot(left, right, dims=NN):
    return lax.dot_general(left, right, dims, preferred_element_type=F32)


def split(value):
    high = value.astype(BF16)
    return high, (value - high.astype(F32)).astype(BF16)


def cat(parts, axis):
    return jnp.concatenate(parts, axis=axis)


def dot3(left_high, left_low, right_high, right_low, dims=NN):
    rows = left_high.shape[0]
    both = dot(cat([left_high, left_low], 0), right_high, dims)
    return both[:rows] + (both[rows:] + dot(left_high, right_low, dims))


def eye(size):
    rows = lax.broadcasted_iota(jnp.int32, (size, size), 0)
    columns = lax.broadcasted_iota(jnp.int32, (size, size), 1)
    return jnp.where(rows == columns, 1.0, 0.0).astype(F32)


def newton_kernel(scale_ref, psi_ref, out_ref):
    bins = psi_ref.shape[1]
    size = psi_ref.shape[4]
    identity = eye(size)
    state = []
    for item in range(bins):
        re = psi_ref[:, item, 0].reshape(size, size)
        im = psi_ref[:, item, 1].reshape(size, size)
        scale = scale_ref[pl.program_id(0) * bins + item]
        gram = dot(cat([re, im], 0), cat([cat([re, im], 1), cat([im, -re], 1)], 0), TN)
        sym = identity - scale * gram[:, :size]
        anti = -scale * gram[:, size:]
        state.append((sym, anti, None))
    for step in range(ITERS):
        after = []
        for sym, anti, total in state:
            left_high, left_low = split(cat([sym, anti], 1))
            if step == 0:
                total = identity + (sym + anti)
                right = cat([sym + anti, sym - anti], 0)
            elif step < ITERS - 1:
                right = cat([cat([sym + anti, total], 1), cat([sym - anti, total.T], 1)], 0)
            else:
                right = cat([total, total.T], 0)
            product = dot3(left_high, left_low, *split(right))
            if step > 0:
                total = total + product[:, -size:]
            if step < ITERS - 1:
                square = product[:, :size]
                square_t = square.T
                sym = 0.5 * (square + square_t)
                anti = 0.5 * (square - square_t)
            after.append((sym, anti, total))
        state = after
    for item in range(bins):
        total = state[item][2]
        total_t = total.T
        re = psi_ref[:, item, 0].reshape(size, size)
        im = psi_ref[:, item, 1].reshape(size, size)
        scale = scale_ref[pl.program_id(0) * bins + item]
        half = (0.5 * scale) * cat([total + total_t, total - total_t], 1)
        high, low = split(half)
        both = dot(cat([high, low], 0), cat([cat([re, im], 1), cat([-im, re], 1)], 0), NT)
        high, low = split(both[:size] + both[size:])
        out_ref[item, 0] = high
        out_ref[item, 1] = low


def middle_kernel(inverse_ref, spectrum_ref, out_ref):
    bins, size = inverse_ref.shape[0], inverse_ref.shape[2]
    total_bins = pl.num_programs(0) * bins
    identity = eye(size)
    for item in range(bins):
        re = spectrum_ref[:, item, 0].reshape(size, size)
        im = spectrum_ref[:, item, 1].reshape(size, size)
        high, low = inverse_ref[item, 0], inverse_ref[item, 1]
        both = dot(cat([high, low], 0), cat([cat([re, im], 1), cat([-im, re], 1)], 0))
        left_high, left_low = split(both[:size] + both[size:])

        def swapped(value):
            return cat([value, cat([value[:, size:], -value[:, :size]], 1)], 0)

        middle = dot3(left_high, left_low, swapped(high), swapped(low), NT)
        place = pl.program_id(0) * bins + item
        out_ref[pl.ds(place, size, stride=2 * total_bins), :] = middle[:, :size] + identity
        out_ref[pl.ds(total_bins + place, size, stride=2 * total_bins), :] = middle[:, size:]


def causal_kernel(table_ref, values_ref, out_ref, table_high, table_low):
    count = table_ref.shape[1]
    lanes = values_ref.shape[-1]

    @pl.when(pl.program_id(0) == 0)
    def _():
        for part in range(2):
            high, low = split(table_ref[part])
            table_high[part * count : (part + 1) * count] = high
            table_low[part * count : (part + 1) * count] = low

    values = cat(
        [
            values_ref[:, 0, 0].reshape(count, lanes),
            values_ref[:, 0, 1].reshape(count, lanes),
        ],
        1,
    )
    high, low = split(values)
    whole = dot(table_high[...], high) + (dot(table_high[...], low) + dot(table_low[...], high))
    real, imag = whole[:count], whole[count:]
    shape = (out_ref.shape[0], out_ref.shape[3], lanes)
    out_ref[:, 0, 0] = (real[:, :lanes] - imag[:, lanes:]).reshape(shape)
    out_ref[:, 0, 1] = (real[:, lanes:] + imag[:, :lanes]).reshape(shape)


def product_kernel(causal_ref, psi_ref, out_ref):
    bins, size = psi_ref.shape[2], psi_ref.shape[5]
    columns = out_ref.shape[2]
    total_bins = causal_ref.shape[0] // (2 * columns)
    base = (pl.program_id(0) * pl.num_programs(1) + pl.program_id(1)) * bins
    for item in range(bins):
        re = psi_ref[0, :, item, 0].reshape(size, size)
        im = psi_ref[0, :, item, 1].reshape(size, size)
        place = base + item
        left = cat(
            [
                causal_ref[pl.ds(place, columns, stride=2 * total_bins), :],
                causal_ref[pl.ds(total_bins + place, columns, stride=2 * total_bins), :],
            ],
            1,
        )
        high, low = split(left)
        both = dot(cat([high, low], 0), cat([cat([re, -im], 1), cat([im, re], 1)], 0), NT)
        result = both[:columns] + both[columns:]
        out_ref[item, 0] = result[:, :size]
        out_ref[item, 1] = result[:, size:]


def projection_table(lag_limit, count, freq_size, chan_size):
    own = count // (freq_size * chan_size)
    shape = (count, count)
    row = lax.broadcasted_iota(jnp.int32, shape, 0)
    column = lax.broadcasted_iota(jnp.int32, shape, 1)
    bins = (
        (column // own) % freq_size * (own * chan_size)
        + column // (own * freq_size) * own
        + column % own
    )
    shift = bins - row
    unit = math.pi / count
    half_angle = shift.astype(F32) * unit
    turned = ((2 * lag_limit + 1) * shift) % (2 * count)
    turned = jnp.where(turned >= count, turned - 2 * count, turned)
    last_angle = turned.astype(F32) * unit
    below = jnp.where(shift == 0, 1.0, 2.0 * count * jnp.sin(half_angle))
    real = jnp.where(shift == 0, (lag_limit.astype(F32) + 0.5) / count, jnp.sin(last_angle) / below)
    imag = jnp.where(shift == 0, 0.0, (jnp.cos(half_angle) - jnp.cos(last_angle)) / below)
    return jnp.stack([real, imag])


def params(limit):
    return pltpu.CompilerParams(vmem_limit_bytes=limit * MIB)


def cost(flops, moved):
    return pl.CostEstimate(flops=flops, bytes_accessed=moved, transcendentals=0)


def shards(freq_size, chan_size, factor, spectrum, guess_scale, lag_cutoff):
    group_bins, _, rows, size = factor.shape
    own = group_bins // chan_size
    count = group_bins * freq_size
    step = math.gcd(own, 4)
    column_parts = min(freq_size, rows)
    lane_parts = freq_size // column_parts
    kept = rows // column_parts
    lanes = size // lane_parts

    factor_own = lax.all_to_all(factor, "chan", 0, 0, tiled=True)
    factor_own = factor_own.reshape(chan_size, own, 2, rows, size)
    spectrum_own = lax.all_to_all(spectrum, "chan", 0, 0, tiled=True)
    spectrum_own = spectrum_own.reshape(chan_size, own, 2, rows, size)
    factor_all = lax.all_gather(factor_own, "chan", axis=0, tiled=False)
    scale_own = lax.dynamic_slice_in_dim(guess_scale, lax.axis_index("chan") * own, own, 0)
    table = projection_table(lag_cutoff[0], count, freq_size, chan_size)

    panel_block = pl.BlockSpec((chan_size, step, 2, rows, size), lambda i: (0, i, 0, 0, 0))
    inverse_block = pl.BlockSpec((step, 2, size, 2 * size), lambda i: (i, 0, 0, 0))
    inverse = pl.pallas_call(
        newton_kernel,
        grid=(own // step,),
        in_specs=[pl.BlockSpec(memory_space=pltpu.SMEM), panel_block],
        out_specs=inverse_block,
        out_shape=jax.ShapeDtypeStruct((own, 2, size, 2 * size), BF16),
        compiler_params=params(16),
        cost_estimate=cost(own * 64 * 2 * 4 * size**3, own * 6 * 4 * size * size),
    )(scale_own, factor_own)
    middle = pl.pallas_call(
        middle_kernel,
        grid=(own // step,),
        in_specs=[inverse_block, panel_block],
        out_specs=pl.BlockSpec((size * 2 * own, size), lambda i: (0, 0)),
        out_shape=jax.ShapeDtypeStruct((size * 2 * own, size), F32),
        compiler_params=params(16),
        cost_estimate=cost(own * 10 * 2 * 4 * size**3, own * 6 * 4 * size * size),
    )(inverse, spectrum_own)

    sent = middle.astype(jnp.float16)
    if lane_parts > 1:
        sent = sent.reshape(size, 2, own, lane_parts, lanes)
        sent = sent.transpose(0, 3, 1, 2, 4)
    sent = sent.reshape(chan_size * freq_size, kept, 2, own, lanes)
    values = lax.all_to_all(sent, ("chan", "freq"), 0, 0, tiled=True).astype(F32)
    sources = chan_size * freq_size
    if own % 8:
        values = values.transpose(1, 2, 0, 3, 4).reshape(1, kept, 2, count, lanes)
        sources, own_rows = 1, count
    else:
        own_rows = own
    causal = pl.pallas_call(
        causal_kernel,
        grid=(kept,),
        in_specs=[
            pl.BlockSpec((2, count, count), lambda i: (0, 0, 0)),
            pl.BlockSpec((sources, 1, 2, own_rows, lanes), lambda i: (0, i, 0, 0, 0)),
        ],
        out_specs=pl.BlockSpec((freq_size, 1, 2, group_bins, lanes), lambda i: (0, i, 0, 0, 0)),
        out_shape=jax.ShapeDtypeStruct((freq_size, kept, 2, group_bins, lanes), F32),
        scratch_shapes=[pltpu.VMEM((2 * count, count), BF16), pltpu.VMEM((2 * count, count), BF16)],
        compiler_params=params(24),
        cost_estimate=cost(kept * 24 * count * count * lanes, 8 * kept * 2 * count * lanes),
    )(table, values)
    back = lax.all_to_all(causal.astype(jnp.float16), "freq", 0, 0, tiled=True).astype(F32)
    if lane_parts > 1:
        back = back.reshape(column_parts, lane_parts, kept, 2, group_bins, lanes)
        back = back.transpose(0, 2, 3, 4, 1, 5)
    back = back.reshape(rows * 2 * group_bins, size)
    result = pl.pallas_call(
        product_kernel,
        grid=(chan_size, own // step),
        in_specs=[
            pl.BlockSpec((rows * 2 * group_bins, size), lambda i, j: (0, 0)),
            pl.BlockSpec((1, chan_size, step, 2, rows, size), lambda i, j: (i, 0, j, 0, 0, 0)),
        ],
        out_specs=pl.BlockSpec((step, 2, rows, size), lambda i, j: (i * (own // step) + j, 0, 0, 0)),
        out_shape=jax.ShapeDtypeStruct((group_bins, 2, rows, size), F32),
        compiler_params=params(16),
        cost_estimate=cost(group_bins * 4 * 4 * size * size * rows, 8 * MIB),
    )(back, factor_all)
    return jnp.swapaxes(result, 2, 3)


def solution(mesh):
    in_specs = (P("freq", None, "chan", None), P("freq", None, "chan", None), P("freq"), P())
    out_specs = P("freq", None, None, "chan")
    body = functools.partial(shards, mesh.shape["freq"], mesh.shape["chan"])
    return jax.shard_map(body, mesh=mesh, in_specs=in_specs, out_specs=out_specs, check_vma=False)
```

```python
import functools
import math

import jax
import jax.numpy as jnp
from jax import lax
from jax.experimental import pallas as pl
from jax.experimental.pallas import tpu as pltpu
from jax.sharding import PartitionSpec as P

ITERS = 8
SCALE = 16.0
CHUNKS = 1
F32 = jnp.float32
BF16 = jnp.bfloat16
MIB = 1024 * 1024
NN = (((1,), (0,)), ((), ()))
NT = (((1,), (1,)), ((), ()))
TN = (((0,), (0,)), ((), ()))


def dot(left, right, dims=NN):
    return lax.dot_general(left, right, dims, preferred_element_type=F32)


def split(value):
    high = value.astype(BF16)
    return high, (value - high.astype(F32)).astype(BF16)


def cat(parts, axis):
    return jnp.concatenate(parts, axis=axis)


def dot3(left_high, left_low, right_high, right_low, dims=NN):
    rows = left_high.shape[0]
    both = dot(cat([left_high, left_low], 0), right_high, dims)
    return both[:rows] + (both[rows:] + dot(left_high, right_low, dims))


def eye(size):
    rows = lax.broadcasted_iota(jnp.int32, (size, size), 0)
    columns = lax.broadcasted_iota(jnp.int32, (size, size), 1)
    return jnp.where(rows == columns, 1.0, 0.0).astype(F32)


def newton_kernel(scale_ref, psi_ref, out_ref):
    bins = psi_ref.shape[1]
    size = psi_ref.shape[4]
    identity = eye(size)
    state = []
    for item in range(bins):
        re = psi_ref[:, item, 0].reshape(size, size)
        im = psi_ref[:, item, 1].reshape(size, size)
        scale = scale_ref[pl.program_id(0) * bins + item]
        gram = dot(cat([re, im], 0), cat([cat([re, im], 1), cat([im, -re], 1)], 0), TN)
        sym = identity - scale * gram[:, :size]
        anti = -scale * gram[:, size:]
        state.append((sym, anti, None))
    for step in range(ITERS):
        after = []
        for sym, anti, total in state:
            left_high, left_low = split(cat([sym, anti], 1))
            if step == 0:
                total = identity + (sym + anti)
                right = cat([sym + anti, sym - anti], 0)
            elif step < ITERS - 1:
                right = cat([cat([sym + anti, total], 1), cat([sym - anti, total.T], 1)], 0)
            else:
                right = cat([total, total.T], 0)
            product = dot3(left_high, left_low, *split(right))
            if step > 0:
                total = total + product[:, -size:]
            if step < ITERS - 1:
                square = product[:, :size]
                square_t = square.T
                sym = 0.5 * (square + square_t)
                anti = 0.5 * (square - square_t)
            after.append((sym, anti, total))
        state = after
    for item in range(bins):
        total = state[item][2]
        total_t = total.T
        re = psi_ref[:, item, 0].reshape(size, size)
        im = psi_ref[:, item, 1].reshape(size, size)
        scale = scale_ref[pl.program_id(0) * bins + item]
        half = (0.5 * scale) * cat([total + total_t, total - total_t], 1)
        high, low = split(half)
        both = dot(cat([high, low], 0), cat([cat([re, im], 1), cat([-im, re], 1)], 0), NT)
        high, low = split(both[:size] + both[size:])
        out_ref[item, 0] = high
        out_ref[item, 1] = low


def middle_kernel(inverse_ref, packed_ref, out_ref):
    bins, size = inverse_ref.shape[0], inverse_ref.shape[2]
    total_bins = pl.num_programs(0) * bins
    identity = eye(size)
    rows = lax.broadcasted_iota(jnp.int32, (size, size), 0)
    columns = lax.broadcasted_iota(jnp.int32, (size, size), 1)
    for item in range(bins):
        packed = packed_ref[:, item].reshape(size, size).astype(F32)
        packed_t = packed.T
        re = jnp.where(columns >= rows, packed, packed_t).astype(BF16)
        im = jnp.where(columns == rows, 0.0, jnp.where(columns < rows, packed, -packed_t)).astype(BF16)
        high, low = inverse_ref[item, 0], inverse_ref[item, 1]
        both = dot(cat([high, low], 0), cat([cat([re, im], 1), cat([-im, re], 1)], 0))
        left = both[:size] + both[size:]
        left_re, left_im = left[:, :size], left[:, size:]
        left_high, left_low = split(cat([left_re + left_im, left_im - left_re], 1))
        middle = dot3(left_high, left_low, high, low, NT)
        place = pl.program_id(0) * bins + item
        out_ref[pl.ds(place, size, stride=total_bins), :] = (middle + identity) * (1.0 / SCALE)


def causal_kernel(table_ref, values_ref, out_ref, table_high, table_low):
    count = table_ref.shape[1]
    sources, kept, own, lanes = values_ref.shape

    @pl.when(pl.program_id(0) == 0)
    def _():
        for part in range(2):
            high, low = split(table_ref[part])
            table_high[part * count : (part + 1) * count] = high
            table_low[part * count : (part + 1) * count] = low

    values = cat([values_ref[:, item].reshape(count, lanes) for item in range(kept)], 1)
    high, low = split(values)
    whole = dot(table_high[...], high) + (dot(table_high[...], low) + dot(table_low[...], high))
    for item in range(kept):
        for part in range(2):
            piece = whole[part * count : (part + 1) * count, item * lanes : (item + 1) * lanes]
            out_ref[:, item, part] = piece.reshape(sources, own, lanes)


def product_kernel(causal_ref, psi_ref, out_ref):
    bins, size = psi_ref.shape[1], psi_ref.shape[4]
    total_bins = causal_ref.shape[0] // (2 * size)
    for item in range(bins):
        re = psi_ref[:, item, 0].reshape(size, size)
        im = psi_ref[:, item, 1].reshape(size, size)
        place = pl.program_id(0) * bins + item
        part_re = causal_ref[pl.ds(place, size, stride=2 * total_bins), :]
        part_im = causal_ref[pl.ds(total_bins + place, size, stride=2 * total_bins), :]
        added, taken = part_re + part_im, part_re - part_im
        high, low = split(0.5 * cat([taken.T + added, added.T - taken], 1))
        both = dot(cat([high, low], 0), cat([cat([re, -im], 1), cat([im, re], 1)], 0), NT)
        result = both[:size] + both[size:]
        shape = (psi_ref.shape[0], psi_ref.shape[3], size)
        out_ref[:, item, 0] = result[:, :size].reshape(shape)
        out_ref[:, item, 1] = result[:, size:].reshape(shape)


def owned_bins(index, own, freq_size, chan_size, chunks):
    part = own // chunks
    inner = index % own
    group = index // own % freq_size
    member = index // (own * freq_size)
    return group * (own * chan_size) + inner // part * (part * chan_size) + member * part + inner % part


def projection_table(lag_limit, count, freq_size, chan_size, chunks):
    own = count // (freq_size * chan_size)
    rows = lax.broadcasted_iota(jnp.int32, (count, 1), 0)
    columns = lax.broadcasted_iota(jnp.int32, (1, count), 1)
    shift = owned_bins(columns, own, freq_size, chan_size, chunks) - owned_bins(
        rows, own, freq_size, chan_size, chunks
    )
    unit = math.pi / count
    half_angle = shift.astype(F32) * unit
    turned = ((2 * lag_limit + 1) * shift) % (2 * count)
    turned = jnp.where(turned >= count, turned - 2 * count, turned)
    last_angle = turned.astype(F32) * unit
    below = jnp.where(shift == 0, 1.0, 2.0 * count * jnp.sin(half_angle))
    real = jnp.where(shift == 0, (lag_limit.astype(F32) + 0.5) / count, jnp.sin(last_angle) / below)
    imag = jnp.where(shift == 0, 0.0, (jnp.cos(half_angle) - jnp.cos(last_angle)) / below)
    return jnp.stack([real, imag])


def params(limit):
    return pltpu.CompilerParams(vmem_limit_bytes=limit * MIB)


def cost(flops, moved):
    return pl.CostEstimate(flops=flops, bytes_accessed=moved, transcendentals=0)


def shards(freq_size, chan_size, factor, spectrum, guess_scale, lag_cutoff):
    group_bins, _, rows, size = factor.shape
    own = group_bins // chan_size
    count = group_bins * freq_size
    chunks = CHUNKS if own % (8 * CHUNKS) == 0 else 1
    part = own // chunks
    step = math.gcd(part, 4)
    column_parts = min(freq_size, rows)
    lane_parts = freq_size // column_parts
    kept = rows // column_parts
    lanes = size // lane_parts
    member = lax.axis_index("chan")
    devices = chan_size * freq_size

    panel_block = pl.BlockSpec((chan_size, step, 2, rows, size), lambda i: (0, i, 0, 0, 0))
    inverse_block = pl.BlockSpec((step, 2, size, 2 * size), lambda i: (i, 0, 0, 0))

    owned = []
    for chunk in range(chunks):
        piece = factor[chunk * part * chan_size : (chunk + 1) * part * chan_size]
        if owned:
            piece, owned[-1] = lax.optimization_barrier((piece, owned[-1]))
        piece = lax.all_to_all(piece, "chan", 0, 0, tiled=True)
        owned.append(piece.reshape(chan_size, part, 2, rows, size))
    row_index = lax.broadcasted_iota(jnp.int32, (rows, size), 0) + member * rows
    column_index = lax.broadcasted_iota(jnp.int32, (rows, size), 1)
    packed = jnp.where(column_index >= row_index, spectrum[:, 0], spectrum[:, 1])
    packed, owned[-1] = lax.optimization_barrier((packed, owned[-1]))
    if chunks > 1:
        packed = packed.reshape(chunks, chan_size, part, rows, size).transpose(1, 0, 2, 3, 4)
    packed = packed.reshape(group_bins, rows, size)
    packed = lax.all_to_all(packed, "chan", 0, 0, tiled=True)
    packed = packed.reshape(chan_size, own, rows, size)
    table = projection_table(lag_cutoff[0], count, freq_size, chan_size, chunks)

    middles = []
    for chunk in range(chunks):
        scale = lax.dynamic_slice_in_dim(
            guess_scale, chunk * part * chan_size + member * part, part, 0
        )
        inverse = pl.pallas_call(
            newton_kernel,
            grid=(part // step,),
            in_specs=[pl.BlockSpec(memory_space=pltpu.SMEM), panel_block],
            out_specs=inverse_block,
            out_shape=jax.ShapeDtypeStruct((part, 2, size, 2 * size), BF16),
            compiler_params=params(16),
            cost_estimate=cost(part * 64 * 2 * 4 * size**3, part * 6 * 4 * size * size),
        )(scale, owned[chunk])
        offset = chunk * (part // step)
        middles.append(
            pl.pallas_call(
                middle_kernel,
                grid=(part // step,),
                in_specs=[
                    inverse_block,
                    pl.BlockSpec(
                        (chan_size, step, rows, size), lambda i, offset=offset: (0, i + offset, 0, 0)
                    ),
                ],
                out_specs=pl.BlockSpec((size * part, size), lambda i: (0, 0)),
                out_shape=jax.ShapeDtypeStruct((size * part, size), F32),
                compiler_params=params(16),
                cost_estimate=cost(part * 10 * 2 * 4 * size**3, part * 6 * 4 * size * size),
            )(inverse, packed)
        )

    middles = [middle.astype(jnp.float16).reshape(size, part, size) for middle in middles]
    sent = cat(middles, 1) if chunks > 1 else middles[0]
    if lane_parts > 1:
        sent = sent.reshape(size, own, lane_parts, lanes).transpose(0, 2, 1, 3)
    sent = sent.reshape(devices, kept, own, lanes)
    values = lax.all_to_all(sent, ("chan", "freq"), 0, 0, tiled=True).astype(F32)
    sources, own_rows = devices, own
    if own % 8:
        values = values.transpose(1, 0, 2, 3).reshape(1, kept, count, lanes)
        sources, own_rows = 1, count
    pair = math.gcd(kept, 2)
    causal = pl.pallas_call(
        causal_kernel,
        grid=(kept // pair,),
        in_specs=[
            pl.BlockSpec((2, count, count), lambda i: (0, 0, 0)),
            pl.BlockSpec((sources, pair, own_rows, lanes), lambda i: (0, i, 0, 0)),
        ],
        out_specs=pl.BlockSpec((sources, pair, 2, own_rows, lanes), lambda i: (0, i, 0, 0, 0)),
        out_shape=jax.ShapeDtypeStruct((sources, kept, 2, own_rows, lanes), F32),
        scratch_shapes=[pltpu.VMEM((2 * count, count), BF16), pltpu.VMEM((2 * count, count), BF16)],
        compiler_params=params(24),
        cost_estimate=cost(kept * 12 * count * count * lanes, 12 * kept * count * lanes),
    )(table, values)
    causal = causal.astype(jnp.float16)
    if own % 8:
        causal = causal.reshape(kept, 2, devices, own, lanes).transpose(2, 0, 1, 3, 4)

    pieces = []
    for chunk in range(chunks):
        back = causal[:, :, :, chunk * part : (chunk + 1) * part]
        back = lax.all_to_all(back, ("chan", "freq"), 0, 0, tiled=True).astype(F32)
        if lane_parts > 1:
            back = back.reshape(chan_size * column_parts, lane_parts, kept, 2, part, lanes)
            back = back.transpose(0, 2, 3, 4, 1, 5)
        back = back.reshape(size * 2 * part, size)
        result = pl.pallas_call(
            product_kernel,
            grid=(part // step,),
            in_specs=[pl.BlockSpec((size * 2 * part, size), lambda i: (0, 0)), panel_block],
            out_specs=panel_block,
            out_shape=jax.ShapeDtypeStruct((chan_size, part, 2, rows, size), F32),
            compiler_params=params(16),
            cost_estimate=cost(part * 4 * 4 * size**3, part * 5 * 4 * size * size),
        )(back, owned[chunk])
        result = lax.all_to_all(result.astype(jnp.float16), "chan", 0, 0, tiled=True)
        pieces.append(result.reshape(chan_size * part, 2, rows, size))
    whole = cat(pieces, 0) if chunks > 1 else pieces[0]
    return jnp.swapaxes(whole.astype(F32) * SCALE, 2, 3)


def solution(mesh):
    in_specs = (P("freq", None, "chan", None), P("freq", None, "chan", None), P("freq"), P())
    out_specs = P("freq", None, None, "chan")
    body = functools.partial(shards, mesh.shape["freq"], mesh.shape["chan"])
    return jax.shard_map(body, mesh=mesh, in_specs=in_specs, out_specs=out_specs, check_vma=False)
```

```python
import functools
import math

import jax
import jax.numpy as jnp
from jax import lax
from jax.experimental import pallas as pl
from jax.experimental.pallas import tpu as pltpu
from jax.sharding import PartitionSpec as P

ITERS = 8
SCALE = 16.0
CHUNKS = 2
F32 = jnp.float32
BF16 = jnp.bfloat16
MIB = 1024 * 1024
NN = (((1,), (0,)), ((), ()))
NT = (((1,), (1,)), ((), ()))
TN = (((0,), (0,)), ((), ()))


def dot(left, right, dims=NN):
    return lax.dot_general(left, right, dims, preferred_element_type=F32)


def split(value):
    high = value.astype(BF16)
    return high, (value - high.astype(F32)).astype(BF16)


def cat(parts, axis):
    return jnp.concatenate(parts, axis=axis)


def dot3(left_high, left_low, right_high, right_low, dims=NN):
    rows = left_high.shape[0]
    both = dot(cat([left_high, left_low], 0), right_high, dims)
    return both[:rows] + (both[rows:] + dot(left_high, right_low, dims))


def eye(size):
    rows = lax.broadcasted_iota(jnp.int32, (size, size), 0)
    columns = lax.broadcasted_iota(jnp.int32, (size, size), 1)
    return jnp.where(rows == columns, 1.0, 0.0).astype(F32)


def newton_kernel(scale_ref, psi_ref, out_ref):
    bins = psi_ref.shape[1]
    size = psi_ref.shape[4]
    identity = eye(size)
    state = []
    for item in range(bins):
        re = psi_ref[:, item, 0].reshape(size, size)
        im = psi_ref[:, item, 1].reshape(size, size)
        scale = scale_ref[pl.program_id(0) * bins + item]
        gram = dot(cat([re, im], 0), cat([cat([re, im], 1), cat([im, -re], 1)], 0), TN)
        sym = identity - scale * gram[:, :size]
        anti = -scale * gram[:, size:]
        state.append((sym, anti, None))
    for step in range(ITERS):
        after = []
        for sym, anti, total in state:
            left_high, left_low = split(cat([sym, anti], 1))
            if step == 0:
                total = identity + (sym + anti)
                right = cat([sym + anti, sym - anti], 0)
            elif step < ITERS - 1:
                right = cat([cat([sym + anti, total], 1), cat([sym - anti, total.T], 1)], 0)
            else:
                right = cat([total, total.T], 0)
            product = dot3(left_high, left_low, *split(right))
            if step > 0:
                total = total + product[:, -size:]
            if step < ITERS - 1:
                square = product[:, :size]
                square_t = square.T
                sym = 0.5 * (square + square_t)
                anti = 0.5 * (square - square_t)
            after.append((sym, anti, total))
        state = after
    for item in range(bins):
        total = state[item][2]
        total_t = total.T
        re = psi_ref[:, item, 0].reshape(size, size)
        im = psi_ref[:, item, 1].reshape(size, size)
        scale = scale_ref[pl.program_id(0) * bins + item]
        half = (0.5 * scale) * cat([total + total_t, total - total_t], 1)
        high, low = split(half)
        both = dot(cat([high, low], 0), cat([cat([re, im], 1), cat([-im, re], 1)], 0), NT)
        high, low = split(both[:size] + both[size:])
        out_ref[item, 0] = high
        out_ref[item, 1] = low


def middle_kernel(inverse_ref, packed_ref, out_ref):
    bins, size = inverse_ref.shape[0], inverse_ref.shape[2]
    total_bins = pl.num_programs(0) * bins
    identity = eye(size)
    rows = lax.broadcasted_iota(jnp.int32, (size, size), 0)
    columns = lax.broadcasted_iota(jnp.int32, (size, size), 1)
    for item in range(bins):
        packed = packed_ref[:, item].reshape(size, size).astype(F32)
        packed_t = packed.T
        re = jnp.where(columns >= rows, packed, packed_t).astype(BF16)
        im = jnp.where(columns == rows, 0.0, jnp.where(columns < rows, packed, -packed_t)).astype(BF16)
        high, low = inverse_ref[item, 0], inverse_ref[item, 1]
        both = dot(cat([high, low], 0), cat([cat([re, im], 1), cat([-im, re], 1)], 0))
        left = both[:size] + both[size:]
        left_re, left_im = left[:, :size], left[:, size:]
        left_high, left_low = split(cat([left_re + left_im, left_im - left_re], 1))
        middle = dot3(left_high, left_low, high, low, NT)
        place = pl.program_id(0) * bins + item
        out_ref[pl.ds(place, size, stride=total_bins), :] = (middle + identity) * (1.0 / SCALE)


def causal_kernel(table_ref, values_ref, out_ref, table_high, table_low):
    count = table_ref.shape[1]
    sources, kept, own, lanes = values_ref.shape

    @pl.when(pl.program_id(0) == 0)
    def _():
        for part in range(2):
            high, low = split(table_ref[part])
            table_high[part * count : (part + 1) * count] = high
            table_low[part * count : (part + 1) * count] = low

    values = cat([values_ref[:, item].reshape(count, lanes) for item in range(kept)], 1)
    high, low = split(values)
    whole = dot(table_high[...], high) + (dot(table_high[...], low) + dot(table_low[...], high))
    for item in range(kept):
        for part in range(2):
            piece = whole[part * count : (part + 1) * count, item * lanes : (item + 1) * lanes]
            out_ref[:, item, part] = piece.reshape(sources, own, lanes)


def product_kernel(causal_ref, psi_ref, out_ref):
    bins, size = psi_ref.shape[1], psi_ref.shape[4]
    total_bins = causal_ref.shape[0] // (2 * size)
    for item in range(bins):
        re = psi_ref[:, item, 0].reshape(size, size)
        im = psi_ref[:, item, 1].reshape(size, size)
        place = pl.program_id(0) * bins + item
        part_re = causal_ref[pl.ds(place, size, stride=2 * total_bins), :]
        part_im = causal_ref[pl.ds(total_bins + place, size, stride=2 * total_bins), :]
        added, taken = part_re + part_im, part_re - part_im
        high, low = split(0.5 * cat([taken.T + added, added.T - taken], 1))
        both = dot(cat([high, low], 0), cat([cat([re, -im], 1), cat([im, re], 1)], 0), NT)
        result = both[:size] + both[size:]
        shape = (psi_ref.shape[0], psi_ref.shape[3], size)
        out_ref[:, item, 0] = result[:, :size].reshape(shape)
        out_ref[:, item, 1] = result[:, size:].reshape(shape)


def owned_bins(index, own, freq_size, chan_size, chunks):
    part = own // chunks
    inner = index % own
    group = index // own % freq_size
    member = index // (own * freq_size)
    return group * (own * chan_size) + inner // part * (part * chan_size) + member * part + inner % part


def projection_table(lag_limit, count, freq_size, chan_size, chunks):
    own = count // (freq_size * chan_size)
    rows = lax.broadcasted_iota(jnp.int32, (count, 1), 0)
    columns = lax.broadcasted_iota(jnp.int32, (1, count), 1)
    shift = owned_bins(columns, own, freq_size, chan_size, chunks) - owned_bins(
        rows, own, freq_size, chan_size, chunks
    )
    unit = math.pi / count
    half_angle = shift.astype(F32) * unit
    turned = ((2 * lag_limit + 1) * shift) % (2 * count)
    turned = jnp.where(turned >= count, turned - 2 * count, turned)
    last_angle = turned.astype(F32) * unit
    below = jnp.where(shift == 0, 1.0, 2.0 * count * jnp.sin(half_angle))
    real = jnp.where(shift == 0, (lag_limit.astype(F32) + 0.5) / count, jnp.sin(last_angle) / below)
    imag = jnp.where(shift == 0, 0.0, (jnp.cos(half_angle) - jnp.cos(last_angle)) / below)
    return jnp.stack([real, imag])


def params(limit):
    return pltpu.CompilerParams(vmem_limit_bytes=limit * MIB)


def cost(flops, moved):
    return pl.CostEstimate(flops=flops, bytes_accessed=moved, transcendentals=0)


def shards(freq_size, chan_size, factor, spectrum, guess_scale, lag_cutoff):
    group_bins, _, rows, size = factor.shape
    own = group_bins // chan_size
    count = group_bins * freq_size
    chunks = CHUNKS if own % (8 * CHUNKS) == 0 else 1
    part = own // chunks
    step = math.gcd(part, 4)
    column_parts = min(freq_size, rows)
    lane_parts = freq_size // column_parts
    kept = rows // column_parts
    lanes = size // lane_parts
    member = lax.axis_index("chan")
    devices = chan_size * freq_size

    panel_block = pl.BlockSpec((chan_size, step, 2, rows, size), lambda i: (0, i, 0, 0, 0))
    inverse_block = pl.BlockSpec((step, 2, size, 2 * size), lambda i: (i, 0, 0, 0))

    owned = []
    for chunk in range(chunks):
        piece = factor[chunk * part * chan_size : (chunk + 1) * part * chan_size]
        if owned:
            piece, owned[-1] = lax.optimization_barrier((piece, owned[-1]))
        piece = lax.all_to_all(piece, "chan", 0, 0, tiled=True)
        owned.append(piece.reshape(chan_size, part, 2, rows, size))
    row_index = lax.broadcasted_iota(jnp.int32, (rows, size), 0) + member * rows
    column_index = lax.broadcasted_iota(jnp.int32, (rows, size), 1)
    packed = jnp.where(column_index >= row_index, spectrum[:, 0], spectrum[:, 1])
    packed, owned[-1] = lax.optimization_barrier((packed, owned[-1]))
    if chunks > 1:
        packed = packed.reshape(chunks, chan_size, part, rows, size).transpose(1, 0, 2, 3, 4)
    packed = packed.reshape(group_bins, rows, size)
    packed = lax.all_to_all(packed, "chan", 0, 0, tiled=True)
    packed = packed.reshape(chan_size, own, rows, size)
    table = projection_table(lag_cutoff[0], count, freq_size, chan_size, chunks)

    middles = []
    for chunk in range(chunks):
        scale = lax.dynamic_slice_in_dim(
            guess_scale, chunk * part * chan_size + member * part, part, 0
        )
        inverse = pl.pallas_call(
            newton_kernel,
            grid=(part // step,),
            in_specs=[pl.BlockSpec(memory_space=pltpu.SMEM), panel_block],
            out_specs=inverse_block,
            out_shape=jax.ShapeDtypeStruct((part, 2, size, 2 * size), BF16),
            compiler_params=params(16),
            cost_estimate=cost(part * 64 * 2 * 4 * size**3, part * 6 * 4 * size * size),
        )(scale, owned[chunk])
        offset = chunk * (part // step)
        middles.append(
            pl.pallas_call(
                middle_kernel,
                grid=(part // step,),
                in_specs=[
                    inverse_block,
                    pl.BlockSpec(
                        (chan_size, step, rows, size), lambda i, offset=offset: (0, i + offset, 0, 0)
                    ),
                ],
                out_specs=pl.BlockSpec((size * part, size), lambda i: (0, 0)),
                out_shape=jax.ShapeDtypeStruct((size * part, size), F32),
                compiler_params=params(16),
                cost_estimate=cost(part * 10 * 2 * 4 * size**3, part * 6 * 4 * size * size),
            )(inverse, packed)
        )

    middles = [middle.astype(jnp.float16).reshape(size, part, size) for middle in middles]
    sent = cat(middles, 1) if chunks > 1 else middles[0]
    if lane_parts > 1:
        sent = sent.reshape(size, own, lane_parts, lanes).transpose(0, 2, 1, 3)
    sent = sent.reshape(devices, kept, own, lanes)
    values = lax.all_to_all(sent, ("chan", "freq"), 0, 0, tiled=True).astype(F32)
    sources, own_rows = devices, own
    if own % 8:
        values = values.transpose(1, 0, 2, 3).reshape(1, kept, count, lanes)
        sources, own_rows = 1, count
    pair = math.gcd(kept, 2)
    causal = pl.pallas_call(
        causal_kernel,
        grid=(kept // pair,),
        in_specs=[
            pl.BlockSpec((2, count, count), lambda i: (0, 0, 0)),
            pl.BlockSpec((sources, pair, own_rows, lanes), lambda i: (0, i, 0, 0)),
        ],
        out_specs=pl.BlockSpec((sources, pair, 2, own_rows, lanes), lambda i: (0, i, 0, 0, 0)),
        out_shape=jax.ShapeDtypeStruct((sources, kept, 2, own_rows, lanes), F32),
        scratch_shapes=[pltpu.VMEM((2 * count, count), BF16), pltpu.VMEM((2 * count, count), BF16)],
        compiler_params=params(24),
        cost_estimate=cost(kept * 12 * count * count * lanes, 12 * kept * count * lanes),
    )(table, values)
    causal = causal.astype(jnp.float16)
    if own % 8:
        causal = causal.reshape(kept, 2, devices, own, lanes).transpose(2, 0, 1, 3, 4)

    pieces = []
    for chunk in range(chunks):
        back = causal[:, :, :, chunk * part : (chunk + 1) * part]
        back = lax.all_to_all(back, ("chan", "freq"), 0, 0, tiled=True).astype(F32)
        if lane_parts > 1:
            back = back.reshape(chan_size * column_parts, lane_parts, kept, 2, part, lanes)
            back = back.transpose(0, 2, 3, 4, 1, 5)
        back = back.reshape(size * 2 * part, size)
        result = pl.pallas_call(
            product_kernel,
            grid=(part // step,),
            in_specs=[pl.BlockSpec((size * 2 * part, size), lambda i: (0, 0)), panel_block],
            out_specs=panel_block,
            out_shape=jax.ShapeDtypeStruct((chan_size, part, 2, rows, size), F32),
            compiler_params=params(16),
            cost_estimate=cost(part * 4 * 4 * size**3, part * 5 * 4 * size * size),
        )(back, owned[chunk])
        result = lax.all_to_all(result.astype(jnp.float16), "chan", 0, 0, tiled=True)
        pieces.append(result.reshape(chan_size * part, 2, rows, size))
    whole = cat(pieces, 0) if chunks > 1 else pieces[0]
    return jnp.swapaxes(whole.astype(F32) * SCALE, 2, 3)


def solution(mesh):
    in_specs = (P("freq", None, "chan", None), P("freq", None, "chan", None), P("freq"), P())
    out_specs = P("freq", None, None, "chan")
    body = functools.partial(shards, mesh.shape["freq"], mesh.shape["chan"])
    return jax.shard_map(body, mesh=mesh, in_specs=in_specs, out_specs=out_specs, check_vma=False)
```

```python
import functools
import math

import jax
import jax.numpy as jnp
from jax import lax
from jax.experimental import pallas as pl
from jax.experimental.pallas import tpu as pltpu
from jax.sharding import PartitionSpec as P

ITERS = 8
SCALE = 16.0
F32 = jnp.float32
BF16 = jnp.bfloat16
MIB = 1024 * 1024
NN = (((1,), (0,)), ((), ()))
NT = (((1,), (1,)), ((), ()))
TN = (((0,), (0,)), ((), ()))


def dot(left, right, dims=NN):
    return lax.dot_general(left, right, dims, preferred_element_type=F32)


def split(value):
    high = value.astype(BF16)
    return high, (value - high.astype(F32)).astype(BF16)


def cat(parts, axis):
    return jnp.concatenate(parts, axis=axis)


def dot3(left_high, left_low, right_high, right_low, dims=NN):
    rows = left_high.shape[0]
    both = dot(cat([left_high, left_low], 0), right_high, dims)
    return both[:rows] + (both[rows:] + dot(left_high, right_low, dims))


def eye(size):
    rows = lax.broadcasted_iota(jnp.int32, (size, size), 0)
    columns = lax.broadcasted_iota(jnp.int32, (size, size), 1)
    return jnp.where(rows == columns, 1.0, 0.0).astype(F32)


def newton_kernel(scale_ref, psi_ref, out_ref):
    bins = psi_ref.shape[1]
    size = psi_ref.shape[4]
    identity = eye(size)
    state = []
    for item in range(bins):
        re = psi_ref[:, item, 0].reshape(size, size)
        im = psi_ref[:, item, 1].reshape(size, size)
        scale = scale_ref[pl.program_id(0) * bins + item]
        gram = dot(cat([re, im], 0), cat([cat([re, im], 1), cat([im, -re], 1)], 0), TN)
        sym = identity - scale * gram[:, :size]
        anti = -scale * gram[:, size:]
        state.append((sym, anti, None))
    for step in range(ITERS):
        after = []
        for sym, anti, total in state:
            left_high, left_low = split(cat([sym, anti], 1))
            if step == 0:
                total = identity + (sym + anti)
                right = cat([sym + anti, sym - anti], 0)
            elif step < ITERS - 1:
                right = cat([cat([sym + anti, total], 1), cat([sym - anti, total.T], 1)], 0)
            else:
                right = cat([total, total.T], 0)
            product = dot3(left_high, left_low, *split(right))
            if step > 0:
                total = total + product[:, -size:]
            if step < ITERS - 1:
                square = product[:, :size]
                square_t = square.T
                sym = 0.5 * (square + square_t)
                anti = 0.5 * (square - square_t)
            after.append((sym, anti, total))
        state = after
    for item in range(bins):
        total = state[item][2]
        total_t = total.T
        re = psi_ref[:, item, 0].reshape(size, size)
        im = psi_ref[:, item, 1].reshape(size, size)
        scale = scale_ref[pl.program_id(0) * bins + item]
        half = (0.5 * scale) * cat([total + total_t, total - total_t], 1)
        high, low = split(half)
        both = dot(cat([high, low], 0), cat([cat([re, im], 1), cat([-im, re], 1)], 0), NT)
        high, low = split(both[:size] + both[size:])
        out_ref[item, 0] = high
        out_ref[item, 1] = low


def middle_kernel(inverse_ref, packed_ref, out_ref):
    bins, size = inverse_ref.shape[0], inverse_ref.shape[2]
    total_bins = pl.num_programs(0) * bins
    identity = eye(size) * (1.0 / SCALE)
    rows = lax.broadcasted_iota(jnp.int32, (size, size), 0)
    columns = lax.broadcasted_iota(jnp.int32, (size, size), 1)

    def swapped(value):
        return cat([value, cat([value[:, size:], -value[:, :size]], 1)], 0)

    for item in range(bins):
        packed = packed_ref[:, item].reshape(size, size).astype(F32)
        packed_t = packed.T
        re = jnp.where(columns >= rows, packed, packed_t).astype(BF16)
        im = jnp.where(columns == rows, 0.0, jnp.where(columns < rows, packed, -packed_t)).astype(BF16)
        high, low = inverse_ref[item, 0], inverse_ref[item, 1]
        both = dot(cat([high, low], 0), cat([cat([re, im], 1), cat([-im, re], 1)], 0))
        left_high, left_low = split(both[:size] + both[size:])
        middle = dot3(left_high, left_low, swapped(high), swapped(low), NT) * (1.0 / SCALE)
        place = pl.program_id(0) * bins + item
        out_ref[pl.ds(place, size, stride=2 * total_bins), :] = middle[:, :size] + identity
        out_ref[pl.ds(total_bins + place, size, stride=2 * total_bins), :] = middle[:, size:]


def causal_kernel(table_ref, values_ref, out_ref, table_high, table_low):
    count = table_ref.shape[1]
    lanes = values_ref.shape[-1]

    @pl.when(pl.program_id(0) == 0)
    def _():
        for part in range(2):
            high, low = split(table_ref[part])
            table_high[part * count : (part + 1) * count] = high
            table_low[part * count : (part + 1) * count] = low

    values = cat([values_ref[:, 0, part].reshape(count, lanes) for part in range(2)], 1)
    high, low = split(values)
    whole = dot(table_high[...], high) + (dot(table_high[...], low) + dot(table_low[...], high))
    real, imag = whole[:count], whole[count:]
    shape = (out_ref.shape[0], out_ref.shape[3], lanes)
    out_ref[:, 0, 0] = (real[:, :lanes] - imag[:, lanes:]).reshape(shape)
    out_ref[:, 0, 1] = (real[:, lanes:] + imag[:, :lanes]).reshape(shape)


def product_kernel(causal_ref, psi_ref, out_ref):
    bins, size = psi_ref.shape[2], psi_ref.shape[5]
    panels, _, _, rows, _ = out_ref.shape
    columns = panels * rows
    total_bins = causal_ref.shape[0] // (2 * columns)
    base = (pl.program_id(0) * pl.num_programs(1) + pl.program_id(1)) * bins
    for item in range(bins):
        re = psi_ref[0, :, item, 0].reshape(size, size)
        im = psi_ref[0, :, item, 1].reshape(size, size)
        place = base + item
        part_re = causal_ref[pl.ds(place, columns, stride=2 * total_bins), :]
        part_im = causal_ref[pl.ds(total_bins + place, columns, stride=2 * total_bins), :]
        high, low = split(cat([part_re, part_im], 1))
        both = dot(cat([high, low], 0), cat([cat([re, -im], 1), cat([im, re], 1)], 0), NT)
        result = both[:columns] + both[columns:]
        out_ref[:, item, 0] = result[:, :size].reshape(panels, rows, size)
        out_ref[:, item, 1] = result[:, size:].reshape(panels, rows, size)


def projection_table(lag_limit, count, freq_size, pairs):
    own = count // (freq_size * 2 * pairs)
    row = lax.broadcasted_iota(jnp.int32, (count, 1), 0)
    column = lax.broadcasted_iota(jnp.int32, (1, count), 1)
    column_bins = (
        (column // own) % freq_size * (own * 2 * pairs) + column // (own * freq_size) * own + column % own
    )
    holder = row // (2 * own)
    row_bins = (
        holder % freq_size * (own * 2 * pairs)
        + (row // own % 2 * pairs + holder // freq_size) * own
        + row % own
    )
    shift = column_bins - row_bins
    unit = math.pi / count
    half_angle = shift.astype(F32) * unit
    turned = ((2 * lag_limit + 1) * shift) % (2 * count)
    turned = jnp.where(turned >= count, turned - 2 * count, turned)
    last_angle = turned.astype(F32) * unit
    below = jnp.where(shift == 0, 1.0, 2.0 * count * jnp.sin(half_angle))
    real = jnp.where(shift == 0, (lag_limit.astype(F32) + 0.5) / count, jnp.sin(last_angle) / below)
    imag = jnp.where(shift == 0, 0.0, (jnp.cos(half_angle) - jnp.cos(last_angle)) / below)
    return jnp.stack([real, imag])


def params(limit):
    return pltpu.CompilerParams(vmem_limit_bytes=limit * MIB)


def cost(flops, moved):
    return pl.CostEstimate(flops=flops, bytes_accessed=moved, transcendentals=0)


def after(value, *earlier):
    return lax.optimization_barrier((value,) + earlier)[0]


SWAP = ((0, 1), (1, 0))


def shards(freq_size, pairs, factor, spectrum, guess_scale, lag_cutoff):
    chan = ("side", "pair")
    chan_size = 2 * pairs
    group_bins, _, rows, size = factor.shape
    own = group_bins // chan_size
    count = group_bins * freq_size
    step = math.gcd(own, 4)
    column_parts = min(freq_size, rows)
    lane_parts = freq_size // column_parts
    kept = rows // column_parts
    lanes = size // lane_parts
    side, pair = lax.axis_index("side"), lax.axis_index("pair")
    member = side * pairs + pair
    devices = chan_size * freq_size

    panel_block = pl.BlockSpec((chan_size, step, 2, rows, size), lambda i: (0, i, 0, 0, 0))
    inverse_block = pl.BlockSpec((step, 2, size, 2 * size), lambda i: (i, 0, 0, 0))

    factor_own = lax.all_to_all(factor, chan, 0, 0, tiled=True)
    factor_own = factor_own.reshape(chan_size, own, 2, rows, size)
    row_index = lax.broadcasted_iota(jnp.int32, (rows, size), 0) + member * rows
    column_index = lax.broadcasted_iota(jnp.int32, (rows, size), 1)
    packed = jnp.where(column_index >= row_index, spectrum[:, 0], spectrum[:, 1])
    packed = lax.all_to_all(after(packed, factor_own), chan, 0, 0, tiled=True)
    packed = packed.reshape(chan_size, own, rows, size)
    table = projection_table(lag_cutoff[0], count, freq_size, pairs)
    scale = lax.dynamic_slice_in_dim(guess_scale, member * own, own, 0)

    inverse = pl.pallas_call(
        newton_kernel,
        grid=(own // step,),
        in_specs=[pl.BlockSpec(memory_space=pltpu.SMEM), panel_block],
        out_specs=inverse_block,
        out_shape=jax.ShapeDtypeStruct((own, 2, size, 2 * size), BF16),
        compiler_params=params(16),
        cost_estimate=cost(own * 64 * 2 * 4 * size**3, own * 6 * 4 * size * size),
    )(scale, factor_own)
    middle = pl.pallas_call(
        middle_kernel,
        grid=(own // step,),
        in_specs=[
            inverse_block,
            pl.BlockSpec((chan_size, step, rows, size), lambda i: (0, i, 0, 0)),
        ],
        out_specs=pl.BlockSpec((size * 2 * own, size), lambda i: (0, 0)),
        out_shape=jax.ShapeDtypeStruct((size * 2 * own, size), F32),
        compiler_params=params(16),
        cost_estimate=cost(own * 10 * 2 * 4 * size**3, own * 6 * 4 * size * size),
    )(inverse, packed)

    sent = middle.astype(jnp.float16)
    if lane_parts > 1:
        sent = sent.reshape(size, 2, own, lane_parts, lanes).transpose(0, 3, 1, 2, 4)
    sent = sent.reshape(devices, kept, 2, own, lanes)
    arrived = lax.all_to_all(sent, chan + ("freq",), 0, 0, tiled=True)

    across = lax.dynamic_slice_in_dim(factor_own, side * pairs, pairs, 0)
    across = lax.ppermute(after(across, arrived), "side", SWAP)
    far = (1 - side) * pairs
    beside = lax.dynamic_slice_in_dim(factor, (far + 1 - pair) * own, own, 0)
    beside = lax.ppermute(after(beside, arrived), "pair", SWAP)
    here = lax.dynamic_slice_in_dim(factor, (far + pair) * own, own, 0)
    panels = []
    for owner in range(2):
        for panel in range(chan_size):
            near = jnp.where(panel % pairs == pair, here, beside)
            other = jnp.where(panel // pairs == side, near, across[panel % pairs])
            panels.append(jnp.where(owner == side, factor_own[panel], other))
    psi = jnp.stack(panels).reshape(2, chan_size, own, 2, rows, size)

    values = arrived.astype(F32)
    sources, own_rows = devices, own
    if own % 8:
        values = values.transpose(1, 2, 0, 3, 4).reshape(1, kept, 2, count, lanes)
        sources, own_rows = 1, count
    holders, held = pairs * freq_size, 2 * own
    if held % 8:
        holders, held = 1, count
    causal = pl.pallas_call(
        causal_kernel,
        grid=(kept,),
        in_specs=[
            pl.BlockSpec((2, count, count), lambda i: (0, 0, 0)),
            pl.BlockSpec((sources, 1, 2, own_rows, lanes), lambda i: (0, i, 0, 0, 0)),
        ],
        out_specs=pl.BlockSpec((holders, 1, 2, held, lanes), lambda i: (0, i, 0, 0, 0)),
        out_shape=jax.ShapeDtypeStruct((holders, kept, 2, held, lanes), F32),
        scratch_shapes=[pltpu.VMEM((2 * count, count), BF16), pltpu.VMEM((2 * count, count), BF16)],
        compiler_params=params(24),
        cost_estimate=cost(kept * 24 * count * count * lanes, 16 * kept * count * lanes),
    )(table, values)
    causal = causal.astype(jnp.float16)
    if holders == 1:
        causal = causal.reshape(kept, 2, pairs * freq_size, 2 * own, lanes)
        causal = causal.transpose(2, 0, 1, 3, 4)
    back = lax.all_to_all(causal, ("pair", "freq"), 0, 0, tiled=True).astype(F32)
    if lane_parts > 1:
        back = back.reshape(pairs * column_parts, lane_parts, kept, 2, 2 * own, lanes)
        back = back.transpose(0, 2, 3, 4, 1, 5)
    back = back.reshape(pairs * rows * 2 * 2 * own, size)

    steps = own // step
    result = pl.pallas_call(
        product_kernel,
        grid=(2, steps),
        in_specs=[
            pl.BlockSpec(back.shape, lambda i, j: (0, 0)),
            pl.BlockSpec((1, chan_size, step, 2, rows, size), lambda i, j: (i, 0, j, 0, 0, 0)),
        ],
        out_specs=pl.BlockSpec((pairs, step, 2, rows, size), lambda i, j: (0, i * steps + j, 0, 0, 0)),
        out_shape=jax.ShapeDtypeStruct((pairs, 2 * own, 2, rows, size), F32),
        compiler_params=params(16),
        cost_estimate=cost(own * 4 * 4 * size**3, own * 5 * 4 * size * size),
    )(back, psi)
    given = lax.dynamic_index_in_dim(result, 1 - pair, 0, keepdims=False)
    given = lax.ppermute(given.astype(jnp.float16), "pair", SWAP).astype(F32)
    kept_here = lax.dynamic_index_in_dim(result, pair, 0, keepdims=False)
    given = given.reshape(2, 1, own, 2, rows, size)
    kept_here = kept_here.reshape(2, 1, own, 2, rows, size)
    first = jnp.where(pair == 0, kept_here, given)
    second = jnp.where(pair == 0, given, kept_here)
    whole = cat([first, second], 1).reshape(group_bins, 2, rows, size) * SCALE
    return jnp.swapaxes(whole, 2, 3)


def solution(mesh):
    freq_size, pairs = mesh.shape["freq"], mesh.shape["chan"] // 2
    split_mesh = jax.sharding.Mesh(
        mesh.devices.reshape(freq_size, 2, pairs), ("freq", "side", "pair")
    )
    in_specs = (
        P("freq", None, ("side", "pair"), None),
        P("freq", None, ("side", "pair"), None),
        P("freq"),
        P(),
    )
    out_specs = P("freq", None, None, ("side", "pair"))
    body = functools.partial(shards, freq_size, pairs)
    return jax.shard_map(
        body, mesh=split_mesh, in_specs=in_specs, out_specs=out_specs, check_vma=False
    )
```

```python
import functools
import math

import jax
import jax.numpy as jnp
from jax import lax
from jax.experimental import pallas as pl
from jax.experimental.pallas import tpu as pltpu
from jax.sharding import PartitionSpec as P

ITERS = 8
SCALE = 16.0
CHUNKS = 2
F32 = jnp.float32
BF16 = jnp.bfloat16
MIB = 1024 * 1024
NN = (((1,), (0,)), ((), ()))
NT = (((1,), (1,)), ((), ()))
TN = (((0,), (0,)), ((), ()))


def dot(left, right, dims=NN):
    return lax.dot_general(left, right, dims, preferred_element_type=F32)


def split(value):
    high = value.astype(BF16)
    return high, (value - high.astype(F32)).astype(BF16)


def cat(parts, axis):
    return jnp.concatenate(parts, axis=axis)


def dot3(left_high, left_low, right_high, right_low, dims=NN):
    rows = left_high.shape[0]
    both = dot(cat([left_high, left_low], 0), right_high, dims)
    return both[:rows] + (both[rows:] + dot(left_high, right_low, dims))


def eye(size):
    rows = lax.broadcasted_iota(jnp.int32, (size, size), 0)
    columns = lax.broadcasted_iota(jnp.int32, (size, size), 1)
    return jnp.where(rows == columns, 1.0, 0.0).astype(F32)


def place_rows(member, panels, out_ref):
    rows = panels[0].shape[-2]
    for index, panel in enumerate(panels):
        start = pl.multiple_of((member ^ index) * rows, rows)
        out_ref[..., pl.ds(start, rows), :] = panel[...]


def newton_kernel(member_ref, scale_ref, own_ref, one_ref, two_ref, three_ref, out_ref, psi_ref):
    bins, _, size, _ = psi_ref.shape
    place_rows(member_ref[0], [own_ref.at[0], one_ref, two_ref, three_ref], psi_ref)
    identity = eye(size)
    state = []
    for item in range(bins):
        re, im = psi_ref[item, 0], psi_ref[item, 1]
        scale = scale_ref[pl.program_id(0) * bins + item]
        gram = dot(cat([re, im], 0), cat([cat([re, im], 1), cat([im, -re], 1)], 0), TN)
        sym = identity - scale * gram[:, :size]
        anti = -scale * gram[:, size:]
        state.append((sym, anti, None))
    for step in range(ITERS):
        after = []
        for sym, anti, total in state:
            left_high, left_low = split(cat([sym, anti], 1))
            if step == 0:
                total = identity + (sym + anti)
                right = cat([sym + anti, sym - anti], 0)
            elif step < ITERS - 1:
                right = cat([cat([sym + anti, total], 1), cat([sym - anti, total.T], 1)], 0)
            else:
                right = cat([total, total.T], 0)
            product = dot3(left_high, left_low, *split(right))
            if step > 0:
                total = total + product[:, -size:]
            if step < ITERS - 1:
                square = product[:, :size]
                square_t = square.T
                sym = 0.5 * (square + square_t)
                anti = 0.5 * (square - square_t)
            after.append((sym, anti, total))
        state = after
    for item in range(bins):
        total = state[item][2]
        total_t = total.T
        re, im = psi_ref[item, 0], psi_ref[item, 1]
        scale = scale_ref[pl.program_id(0) * bins + item]
        half = (0.5 * scale) * cat([total + total_t, total - total_t], 1)
        high, low = split(half)
        both = dot(cat([high, low], 0), cat([cat([re, im], 1), cat([-im, re], 1)], 0), NT)
        high, low = split(both[:size] + both[size:])
        out_ref[item, 0] = high
        out_ref[item, 1] = low


def middle_kernel(member_ref, inverse_ref, own_ref, one_ref, two_ref, three_ref, out_ref, packed_ref):
    bins, size = inverse_ref.shape[0], inverse_ref.shape[2]
    total_bins = pl.num_programs(0) * bins
    place_rows(member_ref[0], [own_ref.at[0], one_ref, two_ref, three_ref], packed_ref)
    identity = eye(size) * (1.0 / SCALE)
    rows = lax.broadcasted_iota(jnp.int32, (size, size), 0)
    columns = lax.broadcasted_iota(jnp.int32, (size, size), 1)

    def swapped(value):
        return cat([value, cat([value[:, size:], -value[:, :size]], 1)], 0)

    for item in range(bins):
        packed = packed_ref[item].astype(F32)
        packed_t = packed.T
        re = jnp.where(columns >= rows, packed, packed_t).astype(BF16)
        im = jnp.where(columns == rows, 0.0, jnp.where(columns < rows, packed, -packed_t)).astype(BF16)
        high, low = inverse_ref[item, 0], inverse_ref[item, 1]
        both = dot(cat([high, low], 0), cat([cat([re, im], 1), cat([-im, re], 1)], 0))
        left_high, left_low = split(both[:size] + both[size:])
        middle = dot3(left_high, left_low, swapped(high), swapped(low), NT) * (1.0 / SCALE)
        place = pl.program_id(0) * bins + item
        out_ref[pl.ds(place, size, stride=2 * total_bins), :] = middle[:, :size] + identity
        out_ref[pl.ds(total_bins + place, size, stride=2 * total_bins), :] = middle[:, size:]


def causal_kernel(real_ref, imag_ref, values_ref, out_ref, table_high, table_low):
    count = real_ref.shape[1]
    lanes = values_ref.shape[-1]

    @pl.when(pl.program_id(0) == 0)
    def _():
        for part, table_ref in enumerate((real_ref, imag_ref)):
            high, low = split(table_ref[...])
            table_high[part * count : (part + 1) * count] = high
            table_low[part * count : (part + 1) * count] = low

    values = cat([values_ref[:, 0, part].reshape(count, lanes) for part in range(2)], 1)
    high, low = split(values)
    whole = dot(table_high[...], high) + (dot(table_high[...], low) + dot(table_low[...], high))
    real, imag = whole[:count], whole[count:]
    shape = (out_ref.shape[0], out_ref.shape[3], lanes)
    out_ref[:, 0, 0] = (real[:, :lanes] - imag[:, lanes:]).reshape(shape)
    out_ref[:, 0, 1] = (real[:, lanes:] + imag[:, :lanes]).reshape(shape)


def product(causal_ref, psi_ref, out_ref, first):
    bins, _, size, _ = psi_ref.shape
    panels, _, _, rows, _ = out_ref.shape
    columns = panels * rows
    total_bins = causal_ref.shape[0] // (2 * columns)
    for item in range(bins):
        re, im = psi_ref[item, 0], psi_ref[item, 1]
        place = first + pl.program_id(0) * bins + item
        part_re = causal_ref[pl.ds(place, columns, stride=2 * total_bins), :]
        part_im = causal_ref[pl.ds(total_bins + place, columns, stride=2 * total_bins), :]
        high, low = split(cat([part_re, part_im], 1))
        both = dot(cat([high, low], 0), cat([cat([re, -im], 1), cat([im, re], 1)], 0), NT)
        result = both[:columns] + both[columns:]
        out_ref[:, item, 0] = result[:, :size].reshape(panels, rows, size)
        out_ref[:, item, 1] = result[:, size:].reshape(panels, rows, size)


def near_kernel(causal_ref, psi_ref, out_ref):
    product(causal_ref, psi_ref, out_ref, 0)


def far_kernel(member_ref, causal_ref, own_ref, one_ref, two_ref, three_ref, out_ref, psi_ref):
    place_rows(member_ref[0], [own_ref.at[0], one_ref, two_ref, three_ref], psi_ref)
    product(causal_ref, psi_ref, out_ref, pl.num_programs(0) * psi_ref.shape[0])


def projection_table(lag_limit, count, freq_size, pairs, side):
    own = count // (freq_size * 2 * pairs)
    row = lax.broadcasted_iota(jnp.int32, (count, 1), 0)
    column = lax.broadcasted_iota(jnp.int32, (1, count), 1)
    column_bins = (
        (column // own) % freq_size * (own * 2 * pairs) + column // (own * freq_size) * own + column % own
    )
    holder = row // (2 * own)
    row_bins = (
        holder % freq_size * (own * 2 * pairs)
        + ((row // own % 2 ^ side) * pairs + holder // freq_size) * own
        + row % own
    )
    shift = column_bins - row_bins
    unit = math.pi / count
    half_angle = shift.astype(F32) * unit
    turned = ((2 * lag_limit + 1) * shift) % (2 * count)
    turned = jnp.where(turned >= count, turned - 2 * count, turned)
    last_angle = turned.astype(F32) * unit
    below = jnp.where(shift == 0, 1.0, 2.0 * count * jnp.sin(half_angle))
    real = jnp.where(shift == 0, (lag_limit.astype(F32) + 0.5) / count, jnp.sin(last_angle) / below)
    imag = jnp.where(shift == 0, 0.0, (jnp.cos(half_angle) - jnp.cos(last_angle)) / below)
    return real, imag


def params(limit):
    return pltpu.CompilerParams(vmem_limit_bytes=limit * MIB)


def cost(flops, moved):
    return pl.CostEstimate(flops=flops, bytes_accessed=moved, transcendentals=0)


def after(value, *earlier):
    return lax.optimization_barrier((value,) + earlier)[0]


SWAP = ((0, 1), (1, 0))
FLIP = ((0, 3), (1, 2), (2, 1), (3, 0))


def swap(value, distance):
    if distance == 1:
        return lax.ppermute(value, "pair", SWAP)
    if distance == 2:
        return lax.ppermute(value, "side", SWAP)
    return lax.ppermute(value, ("side", "pair"), FLIP)


def call(kernel, steps, in_specs, out_specs, out_shape, scratch, flops, moved):
    return pl.pallas_call(
        kernel,
        grid_spec=pltpu.PrefetchScalarGridSpec(
            num_scalar_prefetch=1,
            grid=(steps,),
            in_specs=in_specs,
            out_specs=out_specs,
            scratch_shapes=scratch,
        ),
        out_shape=out_shape,
        compiler_params=params(16),
        cost_estimate=cost(flops, moved),
    )


def shards(freq_size, pairs, factor, spectrum, guess_scale, lag_cutoff):
    chan = ("side", "pair")
    chan_size = 2 * pairs
    group_bins, _, rows, size = factor.shape
    own = group_bins // chan_size
    count = group_bins * freq_size
    chunks = CHUNKS if own % (4 * CHUNKS) == 0 else 1
    part = own // chunks
    step = math.gcd(part, 4)
    column_parts = min(freq_size, rows)
    lane_parts = freq_size // column_parts
    kept = rows // column_parts
    lanes = size // lane_parts
    side, pair = lax.axis_index("side"), lax.axis_index("pair")
    member = side * pairs + pair
    members = member.reshape(1)
    devices = chan_size * freq_size
    distances = range(1, chan_size)

    factors = factor.reshape(chan_size, own, 2, rows, size)

    def rows_for(owner, first, length):
        return lax.dynamic_slice(
            factors, (owner, first, 0, 0, 0), (1, length, 2, rows, size)
        ).reshape(length, 2, rows, size)

    arrived = []
    for chunk in range(chunks):
        pieces = [rows_for(member ^ d, chunk * part, part) for d in distances]
        if arrived:
            pieces = lax.optimization_barrier(tuple(pieces) + tuple(arrived[-1]))[: len(pieces)]
        arrived.append([swap(piece, d) for piece, d in zip(pieces, distances)])
    row_index = lax.broadcasted_iota(jnp.int32, (rows, size), 0) + member * rows
    column_index = lax.broadcasted_iota(jnp.int32, (rows, size), 1)
    packed = jnp.where(column_index >= row_index, spectrum[:, 0], spectrum[:, 1])
    packed = packed.reshape(chan_size, own, rows, size)
    pieces = [lax.dynamic_index_in_dim(packed, member ^ d, 0, keepdims=False) for d in distances]
    pieces = lax.optimization_barrier(tuple(pieces) + tuple(arrived[-1]))[: len(pieces)]
    packed_arrived = [swap(piece, d) for piece, d in zip(pieces, distances)]
    table_re, table_im = projection_table(lag_cutoff[0], count, freq_size, pairs, side)

    local_block = lambda first: pl.BlockSpec(
        (1, step, 2, rows, size), lambda i, m: (m[0], i + first, 0, 0, 0)
    )
    other_block = pl.BlockSpec((step, 2, rows, size), lambda i, m: (i, 0, 0, 0))
    whole_block = pl.BlockSpec((step, 2, size, size), lambda i, m: (i, 0, 0, 0))
    inverse_block = pl.BlockSpec((step, 2, size, 2 * size), lambda i, m: (i, 0, 0, 0))
    inverses, psis, middles = [], [], []
    for chunk in range(chunks):
        scale = lax.dynamic_slice_in_dim(guess_scale, member * own + chunk * part, part, 0)
        inverse, psi = call(
            newton_kernel,
            part // step,
            [pl.BlockSpec(memory_space=pltpu.SMEM), local_block(chunk * part // step)] + [other_block] * 3,
            [inverse_block, whole_block],
            [
                jax.ShapeDtypeStruct((part, 2, size, 2 * size), BF16),
                jax.ShapeDtypeStruct((part, 2, size, size), BF16),
            ],
            [],
            part * 64 * 2 * 4 * size**3,
            part * 6 * 4 * size * size,
        )(members, scale, factors, *arrived[chunk])
        inverses.append(inverse)
        psis.append(psi)
    for chunk in range(chunks):
        first = chunk * part // step
        other = pl.BlockSpec((step, rows, size), lambda i, m, first=first: (i + first, 0, 0))
        middles.append(
            call(
                middle_kernel,
                part // step,
                [
                    inverse_block,
                    pl.BlockSpec(
                        (1, step, rows, size), lambda i, m, first=first: (m[0], i + first, 0, 0)
                    ),
                ]
                + [other] * 3,
                pl.BlockSpec((size * 2 * part, size), lambda i, m: (0, 0)),
                jax.ShapeDtypeStruct((size * 2 * part, size), F32),
                [pltpu.VMEM((step, size, size), BF16)],
                part * 10 * 2 * 4 * size**3,
                part * 6 * 4 * size * size,
            )(members, inverses[chunk], packed, *packed_arrived)
        )
    middles = [value.astype(jnp.float16).reshape(size, 2, part, size) for value in middles]
    sent = cat(middles, 2) if chunks > 1 else middles[0]
    if lane_parts > 1:
        sent = sent.reshape(size, 2, own, lane_parts, lanes).transpose(0, 3, 1, 2, 4)
    sent = sent.reshape(devices, kept, 2, own, lanes)
    gathered = lax.all_to_all(sent, chan + ("freq",), 0, 0, tiled=True)

    across = swap(after(rows_for(member, 0, own), packed_arrived[0]), 2)
    across_pair = cat([piece[0] for piece in arrived], 0) if chunks > 1 else arrived[0][0]
    across_pair = swap(after(across_pair, gathered), 2)
    beside = swap(after(rows_for(member ^ 3, 0, own), packed_arrived[0]), 1)

    values = gathered.astype(F32)
    sources, own_rows = devices, own
    if own % 8:
        values = values.transpose(1, 2, 0, 3, 4).reshape(1, kept, 2, count, lanes)
        sources, own_rows = 1, count
    holders, held = pairs * freq_size, 2 * own
    if held % 8:
        holders, held = 1, count
    table_block = pl.BlockSpec((count, count), lambda i: (0, 0))
    causal = pl.pallas_call(
        causal_kernel,
        grid=(kept,),
        in_specs=[
            table_block,
            table_block,
            pl.BlockSpec((sources, 1, 2, own_rows, lanes), lambda i: (0, i, 0, 0, 0)),
        ],
        out_specs=pl.BlockSpec((holders, 1, 2, held, lanes), lambda i: (0, i, 0, 0, 0)),
        out_shape=jax.ShapeDtypeStruct((holders, kept, 2, held, lanes), F32),
        scratch_shapes=[pltpu.VMEM((2 * count, count), BF16), pltpu.VMEM((2 * count, count), BF16)],
        compiler_params=params(24),
        cost_estimate=cost(kept * 24 * count * count * lanes, 16 * kept * count * lanes),
    )(table_re, table_im, values)
    causal = causal.astype(jnp.float16)
    if holders == 1:
        causal = causal.reshape(kept, 2, pairs * freq_size, 2 * own, lanes)
        causal = causal.transpose(2, 0, 1, 3, 4)
    back = lax.all_to_all(causal, ("pair", "freq"), 0, 0, tiled=True).astype(F32)
    if lane_parts > 1:
        back = back.reshape(pairs * column_parts, lane_parts, kept, 2, 2 * own, lanes)
        back = back.transpose(0, 2, 3, 4, 1, 5)
    back = back.reshape(pairs * rows * 2 * 2 * own, size)

    back_block = pl.BlockSpec(back.shape, lambda i, m: (0, 0))
    result_block = pl.BlockSpec((pairs, step, 2, rows, size), lambda i, m: (0, i, 0, 0, 0))
    result_shape = jax.ShapeDtypeStruct((pairs, own, 2, rows, size), F32)
    flops, moved = own * 2 * 4 * size**3, own * 4 * 4 * size * size
    psi = cat(psis, 0) if chunks > 1 else psis[0]
    near = pl.pallas_call(
        near_kernel,
        grid=(own // step,),
        in_specs=[
            pl.BlockSpec(back.shape, lambda i: (0, 0)),
            pl.BlockSpec((step, 2, size, size), lambda i: (i, 0, 0, 0)),
        ],
        out_specs=pl.BlockSpec((pairs, step, 2, rows, size), lambda i: (0, i, 0, 0, 0)),
        out_shape=result_shape,
        compiler_params=params(16),
        cost_estimate=cost(flops, moved),
    )(back, psi)
    far = call(
        far_kernel,
        own // step,
        [
            back_block,
            pl.BlockSpec((1, step, 2, rows, size), lambda i, m: (m[0] ^ 2, i, 0, 0, 0)),
        ]
        + [other_block] * 3,
        result_block,
        result_shape,
        [pltpu.VMEM((step, 2, size, size), BF16)],
        flops,
        moved,
    )(members, back, factors, beside, across, across_pair)

    blocks = [None] * chan_size
    for distance, result in ((0, near), (2, far)):
        given = lax.dynamic_index_in_dim(result, 1 - pair, 0, keepdims=False)
        blocks[distance] = lax.dynamic_index_in_dim(result, pair, 0, keepdims=False)
        blocks[distance + 1] = swap(given.astype(jnp.float16), 1).astype(F32)
    ordered = []
    for owner in range(chan_size):
        distance = member ^ owner
        low = jnp.where(distance % 2 == 0, blocks[0], blocks[1])
        high = jnp.where(distance % 2 == 0, blocks[2], blocks[3])
        ordered.append(jnp.where(distance < 2, low, high))
    whole = cat(ordered, 0) * SCALE
    return jnp.swapaxes(whole, 2, 3)


def solution(mesh):
    freq_size, pairs = mesh.shape["freq"], mesh.shape["chan"] // 2
    split_mesh = jax.sharding.Mesh(
        mesh.devices.reshape(freq_size, 2, pairs), ("freq", "side", "pair")
    )
    in_specs = (
        P("freq", None, ("side", "pair"), None),
        P("freq", None, ("side", "pair"), None),
        P("freq"),
        P(),
    )
    out_specs = P("freq", None, None, ("side", "pair"))
    body = functools.partial(shards, freq_size, pairs)
    return jax.shard_map(
        body, mesh=split_mesh, in_specs=in_specs, out_specs=out_specs, check_vma=False
    )
```

```python
import functools
import math

import jax
import jax.numpy as jnp
from jax import lax
from jax.experimental import pallas as pl
from jax.experimental.pallas import tpu as pltpu
from jax.sharding import PartitionSpec as P

ITERS = 8
SCALE = 16.0
CHUNKS = 2
F32 = jnp.float32
BF16 = jnp.bfloat16
MIB = 1024 * 1024
NN = (((1,), (0,)), ((), ()))
NT = (((1,), (1,)), ((), ()))
TN = (((0,), (0,)), ((), ()))


def dot(left, right, dims=NN):
    return lax.dot_general(left, right, dims, preferred_element_type=F32)


def split(value):
    high = value.astype(BF16)
    return high, (value - high.astype(F32)).astype(BF16)


def cat(parts, axis):
    return jnp.concatenate(parts, axis=axis)


def dot3(left_high, left_low, right_high, right_low, dims=NN):
    rows = left_high.shape[0]
    both = dot(cat([left_high, left_low], 0), right_high, dims)
    return both[:rows] + (both[rows:] + dot(left_high, right_low, dims))


def eye(size):
    rows = lax.broadcasted_iota(jnp.int32, (size, size), 0)
    columns = lax.broadcasted_iota(jnp.int32, (size, size), 1)
    return jnp.where(rows == columns, 1.0, 0.0).astype(F32)


def place_rows(member, panels, out_ref):
    rows = panels[0].shape[-2]
    for index, panel in enumerate(panels):
        start = pl.multiple_of((member ^ index) * rows, rows)
        out_ref[..., pl.ds(start, rows), :] = panel[...]


def newton_kernel(member_ref, scale_ref, own_ref, one_ref, two_ref, three_ref, out_ref, psi_ref):
    bins, _, size, _ = psi_ref.shape
    place_rows(member_ref[0], [own_ref.at[0], one_ref, two_ref, three_ref], psi_ref)
    identity = eye(size)
    state = []
    for item in range(bins):
        re, im = psi_ref[item, 0], psi_ref[item, 1]
        scale = scale_ref[pl.program_id(0) * bins + item]
        gram = dot(cat([re, im], 0), cat([cat([re, im], 1), cat([im, -re], 1)], 0), TN)
        sym = identity - scale * gram[:, :size]
        anti = -scale * gram[:, size:]
        state.append((sym, anti, None))
    for step in range(ITERS):
        after = []
        for sym, anti, total in state:
            left_high, left_low = split(cat([sym, anti], 1))
            if step == 0:
                total = identity + (sym + anti)
                right = cat([sym + anti, sym - anti], 0)
            elif step < ITERS - 1:
                right = cat([cat([sym + anti, total], 1), cat([sym - anti, total.T], 1)], 0)
            else:
                right = cat([total, total.T], 0)
            product = dot3(left_high, left_low, *split(right))
            if step > 0:
                total = total + product[:, -size:]
            if step < ITERS - 1:
                square = product[:, :size]
                square_t = square.T
                sym = 0.5 * (square + square_t)
                anti = 0.5 * (square - square_t)
            after.append((sym, anti, total))
        state = after
    for item in range(bins):
        total = state[item][2]
        total_t = total.T
        re, im = psi_ref[item, 0], psi_ref[item, 1]
        scale = scale_ref[pl.program_id(0) * bins + item]
        half = (0.5 * scale) * cat([total + total_t, total - total_t], 1)
        high, low = split(half)
        both = dot(cat([high, low], 0), cat([cat([re, im], 1), cat([-im, re], 1)], 0), NT)
        high, low = split(both[:size] + both[size:])
        out_ref[item, 0] = high
        out_ref[item, 1] = low


def middle_kernel(member_ref, inverse_ref, own_ref, one_ref, two_ref, three_ref, out_ref, packed_ref):
    bins, size = inverse_ref.shape[0], inverse_ref.shape[2]
    total_bins = pl.num_programs(0) * bins
    place_rows(member_ref[0], [own_ref.at[0], one_ref, two_ref, three_ref], packed_ref)
    identity = eye(size) * (1.0 / SCALE)
    rows = lax.broadcasted_iota(jnp.int32, (size, size), 0)
    columns = lax.broadcasted_iota(jnp.int32, (size, size), 1)

    def swapped(value):
        return cat([value, cat([value[:, size:], -value[:, :size]], 1)], 0)

    for item in range(bins):
        packed = packed_ref[item].astype(F32)
        packed_t = packed.T
        re = jnp.where(columns >= rows, packed, packed_t).astype(BF16)
        im = jnp.where(columns == rows, 0.0, jnp.where(columns < rows, packed, -packed_t)).astype(BF16)
        high, low = inverse_ref[item, 0], inverse_ref[item, 1]
        both = dot(cat([high, low], 0), cat([cat([re, im], 1), cat([-im, re], 1)], 0))
        left_high, left_low = split(both[:size] + both[size:])
        middle = dot3(left_high, left_low, swapped(high), swapped(low), NT) * (1.0 / SCALE)
        place = pl.program_id(0) * bins + item
        out_ref[pl.ds(place, size, stride=2 * total_bins), :] = middle[:, :size] + identity
        out_ref[pl.ds(total_bins + place, size, stride=2 * total_bins), :] = middle[:, size:]


def causal_kernel(real_ref, imag_ref, values_ref, out_ref, table_high, table_low):
    count = real_ref.shape[1]
    lanes = values_ref.shape[-1]

    @pl.when(pl.program_id(0) == 0)
    def _():
        for part, table_ref in enumerate((real_ref, imag_ref)):
            high, low = split(table_ref[...])
            table_high[part * count : (part + 1) * count] = high
            table_low[part * count : (part + 1) * count] = low

    values = cat([values_ref[:, 0, part].reshape(count, lanes) for part in range(2)], 1)
    high, low = split(values)
    whole = dot(table_high[...], high) + (dot(table_high[...], low) + dot(table_low[...], high))
    real, imag = whole[:count], whole[count:]
    shape = (out_ref.shape[0], out_ref.shape[3], lanes)
    out_ref[:, 0, 0] = (real[:, :lanes] - imag[:, lanes:]).reshape(shape)
    out_ref[:, 0, 1] = (real[:, lanes:] + imag[:, :lanes]).reshape(shape)


def product(member_ref, causal_ref, psi_ref, out_ref, distance):
    bins, _, size, _ = psi_ref.shape
    rows = out_ref.shape[2]
    total_bins = causal_ref.shape[0] // (2 * rows)
    first = (member_ref[0] ^ distance) * (pl.num_programs(0) * bins) + pl.program_id(0) * bins
    for item in range(bins):
        re, im = psi_ref[item, 0], psi_ref[item, 1]
        place = first + item
        part_re = causal_ref[pl.ds(place, rows, stride=2 * total_bins), :]
        part_im = causal_ref[pl.ds(total_bins + place, rows, stride=2 * total_bins), :]
        high, low = split(cat([part_re, part_im], 1))
        both = dot(cat([high, low], 0), cat([cat([re, -im], 1), cat([im, re], 1)], 0), NT)
        result = (both[:rows] + both[rows:]) * SCALE
        out_ref[item, 0] = result[:, :size]
        out_ref[item, 1] = result[:, size:]


def near_kernel(member_ref, causal_ref, psi_ref, out_ref):
    product(member_ref, causal_ref, psi_ref, out_ref, 0)


def far_kernel(distance, member_ref, causal_ref, own_ref, one_ref, two_ref, three_ref, done_ref, out_ref, psi_ref):
    place_rows(member_ref[0], [own_ref.at[0], one_ref, two_ref, three_ref], psi_ref)
    product(member_ref, causal_ref, psi_ref, out_ref, distance)


def projection_table(lag_limit, count, freq_size, pairs):
    own = count // (freq_size * 2 * pairs)
    row = lax.broadcasted_iota(jnp.int32, (count, 1), 0)
    column = lax.broadcasted_iota(jnp.int32, (1, count), 1)
    column_bins = (
        (column // own) % freq_size * (own * 2 * pairs) + column // (own * freq_size) * own + column % own
    )
    shift = column_bins - row
    unit = math.pi / count
    half_angle = shift.astype(F32) * unit
    turned = ((2 * lag_limit + 1) * shift) % (2 * count)
    turned = jnp.where(turned >= count, turned - 2 * count, turned)
    last_angle = turned.astype(F32) * unit
    below = jnp.where(shift == 0, 1.0, 2.0 * count * jnp.sin(half_angle))
    real = jnp.where(shift == 0, (lag_limit.astype(F32) + 0.5) / count, jnp.sin(last_angle) / below)
    imag = jnp.where(shift == 0, 0.0, (jnp.cos(half_angle) - jnp.cos(last_angle)) / below)
    return real, imag


def params(limit):
    return pltpu.CompilerParams(vmem_limit_bytes=limit * MIB)


def cost(flops, moved):
    return pl.CostEstimate(flops=flops, bytes_accessed=moved, transcendentals=0)


def after(value, *earlier):
    return lax.optimization_barrier((value,) + earlier)[0]


SWAP = ((0, 1), (1, 0))
FLIP = ((0, 3), (1, 2), (2, 1), (3, 0))


def swap(value, distance):
    if distance == 1:
        return lax.ppermute(value, "pair", SWAP)
    if distance == 2:
        return lax.ppermute(value, "side", SWAP)
    return lax.ppermute(value, ("side", "pair"), FLIP)


def call(kernel, steps, in_specs, out_specs, out_shape, scratch, flops, moved, aliases={}):
    return pl.pallas_call(
        kernel,
        grid_spec=pltpu.PrefetchScalarGridSpec(
            num_scalar_prefetch=1,
            grid=(steps,),
            in_specs=in_specs,
            out_specs=out_specs,
            scratch_shapes=scratch,
        ),
        out_shape=out_shape,
        input_output_aliases=aliases,
        compiler_params=params(16),
        cost_estimate=cost(flops, moved),
    )


def shards(freq_size, pairs, factor, spectrum, guess_scale, lag_cutoff):
    chan = ("side", "pair")
    chan_size = 2 * pairs
    group_bins, _, rows, size = factor.shape
    own = group_bins // chan_size
    count = group_bins * freq_size
    chunks = CHUNKS if own % (4 * CHUNKS) == 0 else 1
    part = own // chunks
    step = math.gcd(part, 4)
    column_parts = min(freq_size, rows)
    lane_parts = freq_size // column_parts
    kept = rows // column_parts
    lanes = size // lane_parts
    side, pair = lax.axis_index("side"), lax.axis_index("pair")
    member = side * pairs + pair
    members = member.reshape(1)
    devices = chan_size * freq_size
    distances = range(1, chan_size)

    factors = factor.reshape(chan_size, own, 2, rows, size)

    def rows_for(owner, first, length):
        return lax.dynamic_slice(
            factors, (owner, first, 0, 0, 0), (1, length, 2, rows, size)
        ).reshape(length, 2, rows, size)

    arrived, beside = [], []
    for chunk in range(chunks):
        pieces = [rows_for(member ^ d, chunk * part, part) for d in distances]
        if arrived:
            pieces = lax.optimization_barrier(tuple(pieces) + tuple(arrived[-1]))[: len(pieces)]
        arrived.append([swap(piece, d) for piece, d in zip(pieces, distances)])
    row_index = lax.broadcasted_iota(jnp.int32, (rows, size), 0) + member * rows
    column_index = lax.broadcasted_iota(jnp.int32, (rows, size), 1)
    packed = jnp.where(column_index >= row_index, spectrum[:, 0], spectrum[:, 1])
    packed = packed.reshape(chan_size, own, rows, size)
    pieces = [lax.dynamic_index_in_dim(packed, member ^ d, 0, keepdims=False) for d in distances]
    pieces = lax.optimization_barrier(tuple(pieces) + tuple(arrived[-1]))[: len(pieces)]
    beside.append(swap(after(rows_for(member, 0, own), arrived[0][2]), 1))
    beside.append(swap(after(rows_for(member ^ 2, 0, own), arrived[-1][2]), 1))
    packed_arrived = [swap(piece, d) for piece, d in zip(pieces, distances)]
    table_re, table_im = projection_table(lag_cutoff[0], count, freq_size, pairs)

    local_block = lambda first: pl.BlockSpec(
        (1, step, 2, rows, size), lambda i, m: (m[0], i + first, 0, 0, 0)
    )
    other_block = pl.BlockSpec((step, 2, rows, size), lambda i, m: (i, 0, 0, 0))
    whole_block = pl.BlockSpec((step, 2, size, size), lambda i, m: (i, 0, 0, 0))
    inverse_block = pl.BlockSpec((step, 2, size, 2 * size), lambda i, m: (i, 0, 0, 0))
    inverses, psis, middles = [], [], []
    for chunk in range(chunks):
        scale = lax.dynamic_slice_in_dim(guess_scale, member * own + chunk * part, part, 0)
        inverse, psi = call(
            newton_kernel,
            part // step,
            [pl.BlockSpec(memory_space=pltpu.SMEM), local_block(chunk * part // step)] + [other_block] * 3,
            [inverse_block, whole_block],
            [
                jax.ShapeDtypeStruct((part, 2, size, 2 * size), BF16),
                jax.ShapeDtypeStruct((part, 2, size, size), BF16),
            ],
            [],
            part * 64 * 2 * 4 * size**3,
            part * 6 * 4 * size * size,
        )(members, scale, factors, *arrived[chunk])
        inverses.append(inverse)
        psis.append(psi)
    for chunk in range(chunks):
        first = chunk * part // step
        other = pl.BlockSpec((step, rows, size), lambda i, m, first=first: (i + first, 0, 0))
        middles.append(
            call(
                middle_kernel,
                part // step,
                [
                    inverse_block,
                    pl.BlockSpec(
                        (1, step, rows, size), lambda i, m, first=first: (m[0], i + first, 0, 0)
                    ),
                ]
                + [other] * 3,
                pl.BlockSpec((size * 2 * part, size), lambda i, m: (0, 0)),
                jax.ShapeDtypeStruct((size * 2 * part, size), F32),
                [pltpu.VMEM((step, size, size), BF16)],
                part * 10 * 2 * 4 * size**3,
                part * 6 * 4 * size * size,
            )(members, inverses[chunk], packed, *packed_arrived)
        )
    middles = [value.astype(jnp.float16).reshape(size, 2, part, size) for value in middles]
    sent = cat(middles, 2) if chunks > 1 else middles[0]
    if lane_parts > 1:
        sent = sent.reshape(size, 2, own, lane_parts, lanes).transpose(0, 3, 1, 2, 4)
    sent = sent.reshape(devices, kept, 2, own, lanes)
    gathered = lax.all_to_all(sent, chan + ("freq",), 0, 0, tiled=True)

    def both_chunks(distance):
        pieces = [piece[distance - 1] for piece in arrived]
        return cat(pieces, 0) if chunks > 1 else pieces[0]

    across = [swap(after(rows_for(member, 0, own), packed_arrived[2]), 2)]
    across += [swap(after(rows_for(member ^ 1, 0, own), packed_arrived[2]), 2)]
    beside += [swap(after(rows_for(member ^ 3, 0, own), packed_arrived[2]), 1)]
    rest = [swap(after(both_chunks(d), packed_arrived[2]), 1) for d in (2, 3)]
    passed = [swap(value, 1) for value in across]

    values = gathered.astype(F32)
    sources, own_rows = devices, own
    if own % 8:
        values = values.transpose(1, 2, 0, 3, 4).reshape(1, kept, 2, count, lanes)
        sources, own_rows = 1, count
    holders, held = freq_size, group_bins
    if held % 8:
        holders, held = 1, count
    table_block = pl.BlockSpec((count, count), lambda i: (0, 0))
    causal = pl.pallas_call(
        causal_kernel,
        grid=(kept,),
        in_specs=[
            table_block,
            table_block,
            pl.BlockSpec((sources, 1, 2, own_rows, lanes), lambda i: (0, i, 0, 0, 0)),
        ],
        out_specs=pl.BlockSpec((holders, 1, 2, held, lanes), lambda i: (0, i, 0, 0, 0)),
        out_shape=jax.ShapeDtypeStruct((holders, kept, 2, held, lanes), F32),
        scratch_shapes=[pltpu.VMEM((2 * count, count), BF16), pltpu.VMEM((2 * count, count), BF16)],
        compiler_params=params(24),
        cost_estimate=cost(kept * 24 * count * count * lanes, 16 * kept * count * lanes),
    )(table_re, table_im, values)
    causal = causal.astype(jnp.float16)
    if holders == 1:
        causal = causal.reshape(kept, 2, freq_size, group_bins, lanes)
        causal = causal.transpose(2, 0, 1, 3, 4)
    back = lax.all_to_all(causal, "freq", 0, 0, tiled=True).astype(F32)
    if lane_parts > 1:
        back = back.reshape(column_parts, lane_parts, kept, 2, group_bins, lanes)
        back = back.transpose(0, 2, 3, 4, 1, 5)
    back = back.reshape(rows * 2 * group_bins, size)

    steps = own // step
    back_block = pl.BlockSpec(back.shape, lambda i, m: (0, 0))
    result_shape = jax.ShapeDtypeStruct((group_bins, 2, rows, size), F32)
    flops, moved = own * 4 * size**3, own * 4 * 4 * size * size
    psi = cat(psis, 0) if chunks > 1 else psis[0]

    def result_block(distance):
        return pl.BlockSpec(
            (step, 2, rows, size), lambda i, m: ((m[0] ^ distance) * steps + i, 0, 0, 0)
        )

    whole = call(
        near_kernel, steps, [back_block, whole_block], result_block(0), result_shape, [], flops, moved
    )(members, back, psi)
    for distance, one, two, three in (
        (1, beside[0], rest[1], rest[0]),
        (2, beside[2], across[0], passed[1]),
        (3, beside[1], across[1], passed[0]),
    ):
        whole = call(
            functools.partial(far_kernel, distance),
            steps,
            [
                back_block,
                pl.BlockSpec(
                    (1, step, 2, rows, size),
                    lambda i, m, distance=distance: (m[0] ^ distance, i, 0, 0, 0),
                ),
            ]
            + [other_block] * 3
            + [pl.BlockSpec(memory_space=pl.ANY)],
            result_block(distance),
            result_shape,
            [pltpu.VMEM((step, 2, size, size), BF16)],
            flops,
            moved,
            {6: 0},
        )(members, back, factors, one, two, three, whole)
    return jnp.swapaxes(whole, 2, 3)


def solution(mesh):
    freq_size, pairs = mesh.shape["freq"], mesh.shape["chan"] // 2
    split_mesh = jax.sharding.Mesh(
        mesh.devices.reshape(freq_size, 2, pairs), ("freq", "side", "pair")
    )
    in_specs = (
        P("freq", None, ("side", "pair"), None),
        P("freq", None, ("side", "pair"), None),
        P("freq"),
        P(),
    )
    out_specs = P("freq", None, None, ("side", "pair"))
    body = functools.partial(shards, freq_size, pairs)
    return jax.shard_map(
        body, mesh=split_mesh, in_specs=in_specs, out_specs=out_specs, check_vma=False
    )
```

```python
import functools
import math

import jax
import jax.numpy as jnp
from jax import lax
from jax.experimental import pallas as pl
from jax.experimental.pallas import tpu as pltpu
from jax.sharding import PartitionSpec as P

ITERS = 8
SCALE = 16.0
CHUNKS = 2
F32 = jnp.float32
BF16 = jnp.bfloat16
MIB = 1024 * 1024
NN = (((1,), (0,)), ((), ()))
NT = (((1,), (1,)), ((), ()))
TN = (((0,), (0,)), ((), ()))


def dot(left, right, dims=NN):
    return lax.dot_general(left, right, dims, preferred_element_type=F32)


def split(value):
    high = value.astype(BF16)
    return high, (value - high.astype(F32)).astype(BF16)


def cat(parts, axis):
    return jnp.concatenate(parts, axis=axis)


def dot3(left_high, left_low, right_high, right_low, dims=NN):
    rows = left_high.shape[0]
    both = dot(cat([left_high, left_low], 0), right_high, dims)
    return both[:rows] + (both[rows:] + dot(left_high, right_low, dims))


def eye(size):
    rows = lax.broadcasted_iota(jnp.int32, (size, size), 0)
    columns = lax.broadcasted_iota(jnp.int32, (size, size), 1)
    return jnp.where(rows == columns, 1.0, 0.0).astype(F32)


def place_rows(member, panels, out_ref):
    rows = panels[0].shape[-2]
    for index, panel in enumerate(panels):
        start = pl.multiple_of((member ^ index) * rows, rows)
        out_ref[..., pl.ds(start, rows), :] = panel[...]


def newton_kernel(member_ref, scale_ref, own_ref, one_ref, two_ref, three_ref, out_ref, psi_ref):
    bins, _, size, _ = psi_ref.shape
    place_rows(member_ref[0], [own_ref.at[0], one_ref, two_ref, three_ref], psi_ref)
    identity = eye(size)
    state = []
    for item in range(bins):
        re, im = psi_ref[item, 0], psi_ref[item, 1]
        scale = scale_ref[pl.program_id(0) * bins + item]
        gram = dot(cat([re, im], 0), cat([cat([re, im], 1), cat([im, -re], 1)], 0), TN)
        sym = identity - scale * gram[:, :size]
        anti = -scale * gram[:, size:]
        state.append((sym, anti, None))
    for step in range(ITERS):
        after = []
        for sym, anti, total in state:
            left_high, left_low = split(cat([sym, anti], 1))
            if step == 0:
                total = identity + (sym + anti)
                right = cat([sym + anti, sym - anti], 0)
            elif step < ITERS - 1:
                right = cat([cat([sym + anti, total], 1), cat([sym - anti, total.T], 1)], 0)
            else:
                right = cat([total, total.T], 0)
            product = dot3(left_high, left_low, *split(right))
            if step > 0:
                total = total + product[:, -size:]
            if step < ITERS - 1:
                square = product[:, :size]
                square_t = square.T
                sym = 0.5 * (square + square_t)
                anti = 0.5 * (square - square_t)
            after.append((sym, anti, total))
        state = after
    for item in range(bins):
        total = state[item][2]
        total_t = total.T
        re, im = psi_ref[item, 0], psi_ref[item, 1]
        scale = scale_ref[pl.program_id(0) * bins + item]
        half = (0.5 * scale) * cat([total + total_t, total - total_t], 1)
        high, low = split(half)
        both = dot(cat([high, low], 0), cat([cat([re, im], 1), cat([-im, re], 1)], 0), NT)
        high, low = split(both[:size] + both[size:])
        out_ref[item, 0] = high
        out_ref[item, 1] = low


def middle_kernel(member_ref, inverse_ref, own_ref, one_ref, two_ref, three_ref, out_ref, packed_ref):
    bins, size = inverse_ref.shape[0], inverse_ref.shape[2]
    total_bins = pl.num_programs(0) * bins
    place_rows(member_ref[0], [own_ref.at[0], one_ref, two_ref, three_ref], packed_ref)
    identity = eye(size)
    rows = lax.broadcasted_iota(jnp.int32, (size, size), 0)
    columns = lax.broadcasted_iota(jnp.int32, (size, size), 1)
    for item in range(bins):
        packed = packed_ref[item].astype(F32)
        packed_t = packed.T
        re = jnp.where(columns >= rows, packed, packed_t).astype(BF16)
        im = jnp.where(columns == rows, 0.0, jnp.where(columns < rows, packed, -packed_t)).astype(BF16)
        high, low = inverse_ref[item, 0], inverse_ref[item, 1]
        both = dot(cat([high, low], 0), cat([cat([re, im], 1), cat([-im, re], 1)], 0))
        left = both[:size] + both[size:]
        left_re, left_im = left[:, :size], left[:, size:]
        left_high, left_low = split(cat([left_re + left_im, left_im - left_re], 1))
        middle = dot3(left_high, left_low, high, low, NT)
        place = pl.program_id(0) * bins + item
        out_ref[pl.ds(place, size, stride=total_bins), :] = (middle + identity) * (1.0 / SCALE)


def causal_kernel(real_ref, imag_ref, values_ref, *refs):
    *out_refs, table_high, table_low = refs
    count = real_ref.shape[1]
    sources, kept, own, lanes = values_ref.shape

    @pl.when(pl.program_id(0) == 0)
    def _():
        for part, table_ref in enumerate((real_ref, imag_ref)):
            high, low = split(table_ref[...])
            table_high[part * count : (part + 1) * count] = high
            table_low[part * count : (part + 1) * count] = low

    values = cat([values_ref[:, item].reshape(count, lanes) for item in range(kept)], 1)
    high, low = split(values)
    whole = dot(table_high[...], high) + (dot(table_high[...], low) + dot(table_low[...], high))
    for item in range(kept):
        for part in range(2):
            piece = whole[part * count : (part + 1) * count, item * lanes : (item + 1) * lanes]
            piece = piece.reshape(sources, own, lanes)
            step = own // len(out_refs)
            for chunk, out_ref in enumerate(out_refs):
                out_ref[:, item, part] = piece[:, chunk * step : (chunk + 1) * step]


def product_kernel(causal_ref, psi_ref, out_ref):
    bins, _, size, _ = psi_ref.shape
    total_bins = causal_ref.shape[0] // (2 * size)
    shape = (out_ref.shape[0], out_ref.shape[3], size)
    for item in range(bins):
        re, im = psi_ref[item, 0], psi_ref[item, 1]
        place = pl.program_id(0) * bins + item
        part_re = causal_ref[pl.ds(place, size, stride=2 * total_bins), :]
        part_im = causal_ref[pl.ds(total_bins + place, size, stride=2 * total_bins), :]
        added, taken = part_re + part_im, part_re - part_im
        high, low = split(0.5 * cat([taken.T + added, added.T - taken], 1))
        both = dot(cat([high, low], 0), cat([cat([re, -im], 1), cat([im, re], 1)], 0), NT)
        result = both[:size] + both[size:]
        out_ref[:, item, 0] = result[:, :size].reshape(shape)
        out_ref[:, item, 1] = result[:, size:].reshape(shape)


def projection_table(lag_limit, count, freq_size, pairs, chunks):
    own = count // (freq_size * 2 * pairs)

    def bins(index):
        part = own // chunks
        group, holder, inner = index // own % freq_size, index // (own * freq_size), index % own
        return (group * chunks + inner // part) * (part * 2 * pairs) + holder * part + inner % part

    row = lax.broadcasted_iota(jnp.int32, (count, 1), 0)
    column = lax.broadcasted_iota(jnp.int32, (1, count), 1)
    shift = bins(column) - bins(row)
    unit = math.pi / count
    half_angle = shift.astype(F32) * unit
    turned = ((2 * lag_limit + 1) * shift) % (2 * count)
    turned = jnp.where(turned >= count, turned - 2 * count, turned)
    last_angle = turned.astype(F32) * unit
    below = jnp.where(shift == 0, 1.0, 2.0 * count * jnp.sin(half_angle))
    real = jnp.where(shift == 0, (lag_limit.astype(F32) + 0.5) / count, jnp.sin(last_angle) / below)
    imag = jnp.where(shift == 0, 0.0, (jnp.cos(half_angle) - jnp.cos(last_angle)) / below)
    return real, imag


def params(limit):
    return pltpu.CompilerParams(vmem_limit_bytes=limit * MIB)


def cost(flops, moved):
    return pl.CostEstimate(flops=flops, bytes_accessed=moved, transcendentals=0)


def after(value, *earlier):
    return lax.optimization_barrier((value,) + earlier)[0]


SWAP = ((0, 1), (1, 0))
FLIP = ((0, 3), (1, 2), (2, 1), (3, 0))


def swap(value, distance):
    if distance == 1:
        return lax.ppermute(value, "pair", SWAP)
    if distance == 2:
        return lax.ppermute(value, "side", SWAP)
    return lax.ppermute(value, ("side", "pair"), FLIP)


def call(kernel, steps, in_specs, out_specs, out_shape, scratch, flops, moved):
    return pl.pallas_call(
        kernel,
        grid_spec=pltpu.PrefetchScalarGridSpec(
            num_scalar_prefetch=1,
            grid=(steps,),
            in_specs=in_specs,
            out_specs=out_specs,
            scratch_shapes=scratch,
        ),
        out_shape=out_shape,
        compiler_params=params(16),
        cost_estimate=cost(flops, moved),
    )


def shards(freq_size, pairs, factor, spectrum, guess_scale, lag_cutoff):
    chan = ("side", "pair")
    chan_size = 2 * pairs
    group_bins, _, rows, size = factor.shape
    own = group_bins // chan_size
    count = group_bins * freq_size
    chunks = CHUNKS if own % (4 * CHUNKS) == 0 else 1
    part = own // chunks
    step = math.gcd(part, 4)
    column_parts = min(freq_size, rows)
    lane_parts = freq_size // column_parts
    kept = rows // column_parts
    lanes = size // lane_parts
    side, pair = lax.axis_index("side"), lax.axis_index("pair")
    member = side * pairs + pair
    members = member.reshape(1)
    devices = chan_size * freq_size
    distances = range(1, chan_size)

    factors = factor.reshape(chunks, chan_size, part, 2, rows, size)

    arrived = []
    for chunk in range(chunks):
        pieces = [
            lax.dynamic_index_in_dim(factors[chunk], member ^ d, 0, keepdims=False)
            for d in distances
        ]
        if arrived:
            pieces = lax.optimization_barrier(tuple(pieces) + tuple(arrived[-1]))[: len(pieces)]
        arrived.append([swap(piece, d) for piece, d in zip(pieces, distances)])
    row_index = lax.broadcasted_iota(jnp.int32, (rows, size), 0) + member * rows
    column_index = lax.broadcasted_iota(jnp.int32, (rows, size), 1)
    packed = jnp.where(column_index >= row_index, spectrum[:, 0], spectrum[:, 1])
    packed = packed.reshape(chunks, chan_size, part, rows, size)
    pieces = [
        lax.dynamic_index_in_dim(packed, member ^ d, 1, keepdims=False).reshape(own, rows, size)
        for d in distances
    ]
    pieces = lax.optimization_barrier(tuple(pieces) + tuple(arrived[-1]))[: len(pieces)]
    packed_arrived = [swap(piece, d) for piece, d in zip(pieces, distances)]
    table_re, table_im = projection_table(lag_cutoff[0], count, freq_size, pairs, chunks)

    local_block = lambda chunk: pl.BlockSpec(
        (pl.squeezed, 1, step, 2, rows, size), lambda i, m: (chunk, m[0], i, 0, 0, 0)
    )
    other_block = pl.BlockSpec((step, 2, rows, size), lambda i, m: (i, 0, 0, 0))
    whole_block = pl.BlockSpec((step, 2, size, size), lambda i, m: (i, 0, 0, 0))
    inverse_block = pl.BlockSpec((step, 2, size, 2 * size), lambda i, m: (i, 0, 0, 0))
    inverses, psis, middles = [], [], []
    for chunk in range(chunks):
        scale = lax.dynamic_slice_in_dim(guess_scale, (chunk * chan_size + member) * part, part, 0)
        inverse, psi = call(
            newton_kernel,
            part // step,
            [pl.BlockSpec(memory_space=pltpu.SMEM), local_block(chunk)] + [other_block] * 3,
            [inverse_block, whole_block],
            [
                jax.ShapeDtypeStruct((part, 2, size, 2 * size), BF16),
                jax.ShapeDtypeStruct((part, 2, size, size), BF16),
            ],
            [],
            part * 64 * 2 * 4 * size**3,
            part * 6 * 4 * size * size,
        )(members, scale, factors, *arrived[chunk])
        inverses.append(inverse)
        psis.append(psi)
    for chunk in range(chunks):
        first = chunk * part // step
        other = pl.BlockSpec((step, rows, size), lambda i, m, first=first: (i + first, 0, 0))
        middles.append(
            call(
                middle_kernel,
                part // step,
                [
                    inverse_block,
                    pl.BlockSpec(
                        (pl.squeezed, 1, step, rows, size),
                        lambda i, m, chunk=chunk: (chunk, m[0], i, 0, 0),
                    ),
                ]
                + [other] * 3,
                pl.BlockSpec((size * part, size), lambda i, m: (0, 0)),
                jax.ShapeDtypeStruct((size * part, size), F32),
                [pltpu.VMEM((step, size, size), BF16)],
                part * 10 * 2 * 4 * size**3,
                part * 6 * 4 * size * size,
            )(members, inverses[chunk], packed, *packed_arrived)
        )
    middles = [value.astype(jnp.float16).reshape(size, part, size) for value in middles]
    sent = cat(middles, 1) if chunks > 1 else middles[0]
    if lane_parts > 1:
        sent = sent.reshape(size, own, lane_parts, lanes).transpose(0, 2, 1, 3)
    sent = sent.reshape(devices, kept, own, lanes)
    values = lax.all_to_all(sent, chan + ("freq",), 0, 0, tiled=True).astype(F32)
    sources, own_rows, parts = devices, own, chunks
    if own % 8:
        values = values.transpose(1, 0, 2, 3).reshape(1, kept, count, lanes)
        sources, own_rows = 1, count
    twice = math.gcd(kept, 2)
    table_block = pl.BlockSpec((count, count), lambda i: (0, 0))
    causal = pl.pallas_call(
        causal_kernel,
        grid=(kept // twice,),
        in_specs=[
            table_block,
            table_block,
            pl.BlockSpec((sources, twice, own_rows, lanes), lambda i: (0, i, 0, 0)),
        ],
        out_specs=[
            pl.BlockSpec((sources, twice, 2, own_rows // chunks, lanes), lambda i: (0, i, 0, 0, 0))
        ]
        * chunks,
        out_shape=[jax.ShapeDtypeStruct((sources, kept, 2, own_rows // chunks, lanes), F32)] * chunks,
        scratch_shapes=[pltpu.VMEM((2 * count, count), BF16), pltpu.VMEM((2 * count, count), BF16)],
        compiler_params=params(24),
        cost_estimate=cost(kept * 12 * count * count * lanes, 12 * kept * count * lanes),
    )(table_re, table_im, values)

    blocks = []
    for chunk in range(chunks):
        back = causal[chunk].astype(jnp.float16)
        if own % 8:
            back = back.reshape(kept, 2, devices, own, lanes).transpose(2, 0, 1, 3, 4)
        if blocks:
            back = after(back, backs)
        back = lax.all_to_all(back, chan + ("freq",), 0, 0, tiled=True)
        backs = back
        if blocks:
            back = after(back, *blocks[-1][1:])
        back = back.astype(F32)
        if lane_parts > 1:
            back = back.reshape(chan_size * column_parts, lane_parts, kept, 2, part, lanes)
            back = back.transpose(0, 2, 3, 4, 1, 5)
        back = back.reshape(size * 2 * part, size)
        result = pl.pallas_call(
            product_kernel,
            grid=(part // step,),
            in_specs=[
                pl.BlockSpec(back.shape, lambda i: (0, 0)),
                pl.BlockSpec((step, 2, size, size), lambda i: (i, 0, 0, 0)),
            ],
            out_specs=pl.BlockSpec((chan_size, step, 2, rows, size), lambda i: (0, i, 0, 0, 0)),
            out_shape=jax.ShapeDtypeStruct((chan_size, part, 2, rows, size), F32),
            compiler_params=params(16),
            cost_estimate=cost(part * 4 * 4 * size**3, part * 5 * 4 * size * size),
        )(back, psis[chunk])
        panels = [
            lax.dynamic_index_in_dim(result, member ^ d, 0, keepdims=False) for d in range(chan_size)
        ]
        blocks.append(panels[:1] + [swap(panels[d].astype(jnp.float16), d) for d in distances])
    ordered = []
    for chunk in range(chunks):
        pieces = [piece.astype(F32) for piece in blocks[chunk]]
        owners = []
        for owner in range(chan_size):
            distance = member ^ owner
            low = jnp.where(distance % 2 == 0, pieces[0], pieces[1])
            high = jnp.where(distance % 2 == 0, pieces[2], pieces[3])
            owners.append(jnp.where(distance < 2, low, high) * SCALE)
        if chunk < chunks - 1:
            owners = [lax.optimization_barrier(cat(owners, 0))]
        ordered += owners
    return jnp.swapaxes(cat(ordered, 0), 2, 3)


def solution(mesh):
    freq_size, pairs = mesh.shape["freq"], mesh.shape["chan"] // 2
    split_mesh = jax.sharding.Mesh(
        mesh.devices.reshape(freq_size, 2, pairs), ("freq", "side", "pair")
    )
    in_specs = (
        P("freq", None, ("side", "pair"), None),
        P("freq", None, ("side", "pair"), None),
        P("freq"),
        P(),
    )
    out_specs = P("freq", None, None, ("side", "pair"))
    body = functools.partial(shards, freq_size, pairs)
    return jax.shard_map(
        body, mesh=split_mesh, in_specs=in_specs, out_specs=out_specs, check_vma=False
    )
```

```python
import functools
import math

import jax
import jax.numpy as jnp
from jax import lax
from jax.experimental import pallas as pl
from jax.experimental.pallas import tpu as pltpu
from jax.sharding import PartitionSpec as P

ITERS = 8
SCALE = 16.0
CHUNKS = 2
F32 = jnp.float32
BF16 = jnp.bfloat16
MIB = 1024 * 1024
NN = (((1,), (0,)), ((), ()))
NT = (((1,), (1,)), ((), ()))
TN = (((0,), (0,)), ((), ()))


def dot(left, right, dims=NN):
    return lax.dot_general(left, right, dims, preferred_element_type=F32)


def split(value):
    high = value.astype(BF16)
    return high, (value - high.astype(F32)).astype(BF16)


def cat(parts, axis):
    return jnp.concatenate(parts, axis=axis)


def dot3(left_high, left_low, right_high, right_low, dims=NN):
    rows = left_high.shape[0]
    both = dot(cat([left_high, left_low], 0), right_high, dims)
    return both[:rows] + (both[rows:] + dot(left_high, right_low, dims))


def eye(size):
    rows = lax.broadcasted_iota(jnp.int32, (size, size), 0)
    columns = lax.broadcasted_iota(jnp.int32, (size, size), 1)
    return jnp.where(rows == columns, 1.0, 0.0).astype(F32)


def place_rows(member, panels, out_ref):
    rows = panels[0].shape[-2]
    for index, panel in enumerate(panels):
        start = pl.multiple_of((member ^ index) * rows, rows)
        out_ref[..., pl.ds(start, rows), :] = panel[...]


def newton_kernel(member_ref, scale_ref, own_ref, one_ref, two_ref, three_ref, *refs):
    out_ref, psi_ref = refs[-2:]
    bins, _, size, _ = psi_ref.shape
    place_rows(member_ref[0], [own_ref.at[0], one_ref, two_ref, three_ref], psi_ref)
    identity = eye(size)
    state = []
    for item in range(bins):
        re, im = psi_ref[item, 0], psi_ref[item, 1]
        scale = scale_ref[pl.program_id(0) * bins + item]
        gram = dot(cat([re, im], 0), cat([cat([re, im], 1), cat([im, -re], 1)], 0), TN)
        sym = identity - scale * gram[:, :size]
        anti = -scale * gram[:, size:]
        state.append((sym, anti, None))
    for step in range(ITERS):
        after = []
        for sym, anti, total in state:
            left_high, left_low = split(cat([sym, anti], 1))
            if step == 0:
                total = identity + (sym + anti)
                right = cat([sym + anti, sym - anti], 0)
            elif step < ITERS - 1:
                right = cat([cat([sym + anti, total], 1), cat([sym - anti, total.T], 1)], 0)
            else:
                right = cat([total, total.T], 0)
            product = dot3(left_high, left_low, *split(right))
            if step > 0:
                total = total + product[:, -size:]
            if step < ITERS - 1:
                square = product[:, :size]
                square_t = square.T
                sym = 0.5 * (square + square_t)
                anti = 0.5 * (square - square_t)
            after.append((sym, anti, total))
        state = after
    for item in range(bins):
        total = state[item][2]
        total_t = total.T
        re, im = psi_ref[item, 0], psi_ref[item, 1]
        scale = scale_ref[pl.program_id(0) * bins + item]
        half = (0.5 * scale) * cat([total + total_t, total - total_t], 1)
        high, low = split(half)
        both = dot(cat([high, low], 0), cat([cat([re, im], 1), cat([-im, re], 1)], 0), NT)
        high, low = split(both[:size] + both[size:])
        out_ref[item, 0] = high
        out_ref[item, 1] = low


def middle_kernel(member_ref, inverse_ref, own_ref, one_ref, two_ref, three_ref, out_ref, packed_ref):
    bins, size = inverse_ref.shape[0], inverse_ref.shape[2]
    total_bins = pl.num_programs(0) * bins
    place_rows(member_ref[0], [own_ref.at[0], one_ref, two_ref, three_ref], packed_ref)
    identity = eye(size) * (1.0 / SCALE)
    rows = lax.broadcasted_iota(jnp.int32, (size, size), 0)
    columns = lax.broadcasted_iota(jnp.int32, (size, size), 1)

    def swapped(value):
        return cat([value, cat([value[:, size:], -value[:, :size]], 1)], 0)

    for item in range(bins):
        packed = packed_ref[item].astype(F32)
        packed_t = packed.T
        re = jnp.where(columns >= rows, packed, packed_t).astype(BF16)
        im = jnp.where(columns == rows, 0.0, jnp.where(columns < rows, packed, -packed_t)).astype(BF16)
        high, low = inverse_ref[item, 0], inverse_ref[item, 1]
        both = dot(cat([high, low], 0), cat([cat([re, im], 1), cat([-im, re], 1)], 0))
        left_high, left_low = split(both[:size] + both[size:])
        middle = dot3(left_high, left_low, swapped(high), swapped(low), NT) * (1.0 / SCALE)
        place = pl.program_id(0) * bins + item
        out_ref[pl.ds(place, size, stride=2 * total_bins), :] = middle[:, :size] + identity
        out_ref[pl.ds(total_bins + place, size, stride=2 * total_bins), :] = middle[:, size:]


def causal_kernel(real_ref, imag_ref, values_ref, out_ref, table_high, table_low):
    count = real_ref.shape[1]
    lanes = values_ref.shape[-1]

    @pl.when(pl.program_id(0) == 0)
    def _():
        for part, table_ref in enumerate((real_ref, imag_ref)):
            high, low = split(table_ref[...])
            table_high[part * count : (part + 1) * count] = high
            table_low[part * count : (part + 1) * count] = low

    values = cat([values_ref[:, 0, part].reshape(count, lanes) for part in range(2)], 1)
    high, low = split(values)
    whole = dot(table_high[...], high) + (dot(table_high[...], low) + dot(table_low[...], high))
    real, imag = whole[:count], whole[count:]
    shape = (out_ref.shape[0], out_ref.shape[3], lanes)
    out_ref[:, 0, 0] = (real[:, :lanes] - imag[:, lanes:]).reshape(shape)
    out_ref[:, 0, 1] = (real[:, lanes:] + imag[:, :lanes]).reshape(shape)


def place_kernel(member_ref, own_ref, one_ref, two_ref, three_ref, out_ref):
    place_rows(member_ref[0], [own_ref.at[0], one_ref, two_ref, three_ref], out_ref)


def product_kernel(first, member_ref, causal_ref, psi_ref, out_ref):
    bins, _, size, _ = psi_ref.shape
    rows = out_ref.shape[2]
    total_bins = causal_ref.shape[0] // (2 * rows)
    for item in range(bins):
        re, im = psi_ref[item, 0], psi_ref[item, 1]
        place = first + pl.program_id(0) * bins + item
        part_re = causal_ref[pl.ds(place, rows, stride=2 * total_bins), :]
        part_im = causal_ref[pl.ds(total_bins + place, rows, stride=2 * total_bins), :]
        high, low = split(cat([part_re, part_im], 1))
        both = dot(cat([high, low], 0), cat([cat([re, -im], 1), cat([im, re], 1)], 0), NT)
        result = both[:rows] + both[rows:]
        out_ref[item, 0] = result[:, :size]
        out_ref[item, 1] = result[:, size:]


def projection_table(lag_limit, count, freq_size, pairs, side):
    own = count // (freq_size * 2 * pairs)
    row = lax.broadcasted_iota(jnp.int32, (count, 1), 0)
    column = lax.broadcasted_iota(jnp.int32, (1, count), 1)
    column_bins = (
        (column // own) % freq_size * (own * 2 * pairs) + column // (own * freq_size) * own + column % own
    )
    holder = row // (2 * own)
    row_bins = (
        holder % freq_size * (own * 2 * pairs)
        + ((row // own % 2 ^ side) * pairs + holder // freq_size) * own
        + row % own
    )
    shift = column_bins - row_bins
    unit = math.pi / count
    half_angle = shift.astype(F32) * unit
    turned = ((2 * lag_limit + 1) * shift) % (2 * count)
    turned = jnp.where(turned >= count, turned - 2 * count, turned)
    last_angle = turned.astype(F32) * unit
    below = jnp.where(shift == 0, 1.0, 2.0 * count * jnp.sin(half_angle))
    real = jnp.where(shift == 0, (lag_limit.astype(F32) + 0.5) / count, jnp.sin(last_angle) / below)
    imag = jnp.where(shift == 0, 0.0, (jnp.cos(half_angle) - jnp.cos(last_angle)) / below)
    return real, imag


def params(limit):
    return pltpu.CompilerParams(vmem_limit_bytes=limit * MIB)


def cost(flops, moved):
    return pl.CostEstimate(flops=flops, bytes_accessed=moved, transcendentals=0)


def after(value, *earlier):
    return lax.optimization_barrier((value,) + earlier)[0]


SWAP = ((0, 1), (1, 0))
FLIP = ((0, 3), (1, 2), (2, 1), (3, 0))


def swap(value, distance):
    if distance == 1:
        return lax.ppermute(value, "pair", SWAP)
    if distance == 2:
        return lax.ppermute(value, "side", SWAP)
    return lax.ppermute(value, ("side", "pair"), FLIP)


def call(kernel, steps, in_specs, out_specs, out_shape, scratch, flops, moved, aliases={}):
    return pl.pallas_call(
        kernel,
        grid_spec=pltpu.PrefetchScalarGridSpec(
            num_scalar_prefetch=1,
            grid=(steps,),
            in_specs=in_specs,
            out_specs=out_specs,
            scratch_shapes=scratch,
        ),
        out_shape=out_shape,
        input_output_aliases=aliases,
        compiler_params=params(16),
        cost_estimate=cost(flops, moved),
    )


def shards(freq_size, pairs, factor, spectrum, guess_scale, lag_cutoff):
    chan = ("side", "pair")
    chan_size = 2 * pairs
    group_bins, _, rows, size = factor.shape
    own = group_bins // chan_size
    count = group_bins * freq_size
    chunks = CHUNKS if own % (4 * CHUNKS) == 0 else 1
    part = own // chunks
    step = math.gcd(part, 4)
    column_parts = min(freq_size, rows)
    lane_parts = freq_size // column_parts
    kept = rows // column_parts
    lanes = size // lane_parts
    side, pair = lax.axis_index("side"), lax.axis_index("pair")
    member = side * pairs + pair
    members = member.reshape(1)
    devices = chan_size * freq_size
    distances = range(1, chan_size)

    factors = factor.reshape(chan_size, own, 2, rows, size)

    def rows_for(owner, first, length):
        return lax.dynamic_slice(
            factors, (owner, first, 0, 0, 0), (1, length, 2, rows, size)
        ).reshape(length, 2, rows, size)

    arrived = []
    for chunk in range(chunks):
        pieces = [rows_for(member ^ d, chunk * part, part) for d in distances]
        if arrived:
            pieces = lax.optimization_barrier(tuple(pieces) + tuple(arrived[-1]))[: len(pieces)]
        arrived.append([swap(piece, d) for piece, d in zip(pieces, distances)])
    row_index = lax.broadcasted_iota(jnp.int32, (rows, size), 0) + member * rows
    column_index = lax.broadcasted_iota(jnp.int32, (rows, size), 1)
    packed = jnp.where(column_index >= row_index, spectrum[:, 0], spectrum[:, 1])
    packed = packed.reshape(chan_size, own, rows, size)
    pieces = [lax.dynamic_index_in_dim(packed, member ^ d, 0, keepdims=False) for d in distances]
    pieces = lax.optimization_barrier(tuple(pieces) + tuple(arrived[-1]))[: len(pieces)]
    packed_arrived = [swap(piece, d) for piece, d in zip(pieces, distances)]
    table_re, table_im = projection_table(lag_cutoff[0], count, freq_size, pairs, side)

    local_block = lambda first: pl.BlockSpec(
        (1, step, 2, rows, size), lambda i, m: (m[0], i + first, 0, 0, 0)
    )
    other_block = pl.BlockSpec((step, 2, rows, size), lambda i, m: (i, 0, 0, 0))
    whole_block = pl.BlockSpec((step, 2, size, size), lambda i, m: (i, 0, 0, 0))
    inverse_block = pl.BlockSpec((step, 2, size, 2 * size), lambda i, m: (i, 0, 0, 0))
    state = []
    for chunk in range(chunks):
        scale = lax.dynamic_slice_in_dim(guess_scale, member * own + chunk * part, part, 0)
        offset = chunk * part // step
        state = call(
            newton_kernel,
            part // step,
            [pl.BlockSpec(memory_space=pltpu.SMEM), local_block(offset)]
            + [other_block] * 3
            + [pl.BlockSpec(memory_space=pl.ANY)] * len(state),
            [
                pl.BlockSpec(
                    (step, 2, size, 2 * size), lambda i, m, offset=offset: (i + offset, 0, 0, 0)
                ),
                pl.BlockSpec(
                    (step, 2, size, size), lambda i, m, offset=offset: (i + offset, 0, 0, 0)
                ),
            ],
            [
                jax.ShapeDtypeStruct((own, 2, size, 2 * size), BF16),
                jax.ShapeDtypeStruct((own, 2, size, size), BF16),
            ],
            [],
            part * 64 * 2 * 4 * size**3,
            part * 6 * 4 * size * size,
            {6 + index: index for index in range(len(state))},
        )(members, scale, factors, *arrived[chunk], *state)
    inverse, psi = state

    def local_rows(chunk):
        return lax.dynamic_slice(
            factors, (member, chunk * part, 0, 0, 0), (1, part, 2, rows, size)
        ).reshape(part, 2, rows, size)

    across = [swap(after(local_rows(0), packed_arrived[2]), 2)]
    other = pl.BlockSpec((step, rows, size), lambda i, m: (i, 0, 0))
    middle = call(
        middle_kernel,
        own // step,
        [inverse_block, pl.BlockSpec((1, step, rows, size), lambda i, m: (m[0], i, 0, 0))]
        + [other] * 3,
        pl.BlockSpec((size * 2 * own, size), lambda i, m: (0, 0)),
        jax.ShapeDtypeStruct((size * 2 * own, size), F32),
        [pltpu.VMEM((step, size, size), BF16)],
        own * 40 * 2 * 4 * size**3,
        own * 6 * 4 * size * size,
    )(members, inverse, packed, *packed_arrived)
    sent = after(middle, across[0]).astype(jnp.float16)
    if lane_parts > 1:
        sent = sent.reshape(size, 2, own, lane_parts, lanes).transpose(0, 3, 1, 2, 4)
    sent = sent.reshape(devices, kept, 2, own, lanes)
    gathered = lax.all_to_all(sent, chan + ("freq",), 0, 0, tiled=True)

    beside = swap(after(rows_for(member ^ 3, 0, own), packed_arrived[2]), 1)
    gathered = after(gathered, beside)
    across += [swap(after(local_rows(chunk), gathered), 2) for chunk in range(1, chunks)]
    first = cat([piece[0] for piece in arrived], 0) if chunks > 1 else arrived[0][0]
    across_pair = swap(after(first, gathered), 2)

    values = gathered.astype(F32)
    sources, own_rows = devices, own
    if own % 8:
        values = values.transpose(1, 2, 0, 3, 4).reshape(1, kept, 2, count, lanes)
        sources, own_rows = 1, count
    holders, held = pairs * freq_size, 2 * own
    if held % 8:
        holders, held = 1, count
    table_block = pl.BlockSpec((count, count), lambda i: (0, 0))
    causal = pl.pallas_call(
        causal_kernel,
        grid=(kept,),
        in_specs=[
            table_block,
            table_block,
            pl.BlockSpec((sources, 1, 2, own_rows, lanes), lambda i: (0, i, 0, 0, 0)),
        ],
        out_specs=pl.BlockSpec((holders, 1, 2, held, lanes), lambda i: (0, i, 0, 0, 0)),
        out_shape=jax.ShapeDtypeStruct((holders, kept, 2, held, lanes), F32),
        scratch_shapes=[pltpu.VMEM((2 * count, count), BF16), pltpu.VMEM((2 * count, count), BF16)],
        compiler_params=params(24),
        cost_estimate=cost(kept * 96 * count * count * lanes, 16 * kept * count * lanes),
    )(table_re, table_im, values)
    causal = after(causal, *across[1:]).astype(jnp.float16)
    if holders == 1:
        causal = causal.reshape(kept, 2, pairs * freq_size, 2 * own, lanes)
        causal = causal.transpose(2, 0, 1, 3, 4)
    back = lax.all_to_all(causal, ("pair", "freq"), 0, 0, tiled=True).astype(F32)
    if lane_parts > 1:
        back = back.reshape(pairs * column_parts, lane_parts, kept, 2, 2 * own, lanes)
        back = back.transpose(0, 2, 3, 4, 1, 5)
    back = back.reshape(pairs * rows * 2 * 2 * own, size)

    across = cat(across, 0) if chunks > 1 else across[0]
    steps = own // step
    far = call(
        place_kernel,
        steps,
        [pl.BlockSpec((1, step, 2, rows, size), lambda i, m: (m[0] ^ 2, i, 0, 0, 0))]
        + [other_block] * 3,
        whole_block,
        jax.ShapeDtypeStruct((own, 2, size, size), BF16),
        [],
        own,
        own * 4 * 4 * size * size,
    )(members, factors, beside, across, across_pair)

    def products(column_panel, distance, factor_rows):
        return call(
            functools.partial(product_kernel, distance * own // 2),
            steps,
            [pl.BlockSpec((back.shape[0] // pairs, size), lambda i, m: (m[0], 0)), whole_block],
            other_block,
            jax.ShapeDtypeStruct((own, 2, rows, size), F32),
            [],
            own * 8 * size**3,
            own * 4 * 4 * size * size,
        )(column_panel.reshape(1), back, factor_rows)

    blocks = [None] * chan_size
    for distance, factor_rows in ((0, psi), (2, far)):
        given = products(1 - pair, distance, factor_rows).astype(jnp.float16)
        blocks[distance + 1] = swap(given, 1).astype(F32)
    for distance, factor_rows in ((0, psi), (2, far)):
        blocks[distance] = products(pair, distance, factor_rows)
    ordered = []
    for owner in range(chan_size):
        distance = member ^ owner
        low = jnp.where(distance % 2 == 0, blocks[0], blocks[1])
        high = jnp.where(distance % 2 == 0, blocks[2], blocks[3])
        ordered.append(jnp.where(distance < 2, low, high))
    whole = cat(ordered, 0) * SCALE
    return jnp.swapaxes(whole, 2, 3)


def solution(mesh):
    freq_size, pairs = mesh.shape["freq"], mesh.shape["chan"] // 2
    split_mesh = jax.sharding.Mesh(
        mesh.devices.reshape(freq_size, 2, pairs), ("freq", "side", "pair")
    )
    in_specs = (
        P("freq", None, ("side", "pair"), None),
        P("freq", None, ("side", "pair"), None),
        P("freq"),
        P(),
    )
    out_specs = P("freq", None, None, ("side", "pair"))
    body = functools.partial(shards, freq_size, pairs)
    return jax.shard_map(
        body, mesh=split_mesh, in_specs=in_specs, out_specs=out_specs, check_vma=False
    )
```

```python
import functools
import math

import jax
import jax.numpy as jnp
from jax import lax
from jax.experimental import pallas as pl
from jax.experimental.pallas import tpu as pltpu
from jax.sharding import PartitionSpec as P

ITERS = 8
SCALE = 16.0
CHUNKS = 2
F32 = jnp.float32
BF16 = jnp.bfloat16
MIB = 1024 * 1024
NN = (((1,), (0,)), ((), ()))
NT = (((1,), (1,)), ((), ()))
TN = (((0,), (0,)), ((), ()))


def dot(left, right, dims=NN):
    return lax.dot_general(left, right, dims, preferred_element_type=F32)


def split(value):
    high = value.astype(BF16)
    return high, (value - high.astype(F32)).astype(BF16)


def cat(parts, axis):
    return jnp.concatenate(parts, axis=axis)


def dot3(left_high, left_low, right_high, right_low, dims=NN):
    rows = left_high.shape[0]
    both = dot(cat([left_high, left_low], 0), right_high, dims)
    return both[:rows] + (both[rows:] + dot(left_high, right_low, dims))


def eye(size):
    rows = lax.broadcasted_iota(jnp.int32, (size, size), 0)
    columns = lax.broadcasted_iota(jnp.int32, (size, size), 1)
    return jnp.where(rows == columns, 1.0, 0.0).astype(F32)


def place_rows(member, panels, out_ref):
    rows = panels[0].shape[-2]
    for index, panel in enumerate(panels):
        start = pl.multiple_of((member ^ index) * rows, rows)
        out_ref[..., pl.ds(start, rows), :] = panel[...]


def newton_kernel(member_ref, scale_ref, own_ref, one_ref, two_ref, three_ref, *refs):
    out_ref, psi_ref = refs[-2:]
    bins, _, size, _ = psi_ref.shape
    place_rows(member_ref[0], [own_ref.at[0], one_ref, two_ref, three_ref], psi_ref)
    identity = eye(size)
    state = []
    for item in range(bins):
        re, im = psi_ref[item, 0], psi_ref[item, 1]
        scale = scale_ref[pl.program_id(0) * bins + item]
        gram = dot(cat([re, im], 0), cat([cat([re, im], 1), cat([im, -re], 1)], 0), TN)
        sym = identity - scale * gram[:, :size]
        anti = -scale * gram[:, size:]
        state.append((sym, anti, None))
    for step in range(ITERS):
        after = []
        for sym, anti, total in state:
            left_high, left_low = split(cat([sym, anti], 1))
            if step == 0:
                total = identity + (sym + anti)
                right = cat([sym + anti, sym - anti], 0)
            elif step < ITERS - 1:
                right = cat([cat([sym + anti, total], 1), cat([sym - anti, total.T], 1)], 0)
            else:
                right = cat([total, total.T], 0)
            product = dot3(left_high, left_low, *split(right))
            if step > 0:
                total = total + product[:, -size:]
            if step < ITERS - 1:
                square = product[:, :size]
                square_t = square.T
                sym = 0.5 * (square + square_t)
                anti = 0.5 * (square - square_t)
            after.append((sym, anti, total))
        state = after
    for item in range(bins):
        total = state[item][2]
        total_t = total.T
        re, im = psi_ref[item, 0], psi_ref[item, 1]
        scale = scale_ref[pl.program_id(0) * bins + item]
        half = (0.5 * scale) * cat([total + total_t, total - total_t], 1)
        high, low = split(half)
        both = dot(cat([high, low], 0), cat([cat([re, im], 1), cat([-im, re], 1)], 0), NT)
        high, low = split(both[:size] + both[size:])
        out_ref[item, 0] = high
        out_ref[item, 1] = low


def middle_kernel(member_ref, inverse_ref, own_ref, one_ref, two_ref, three_ref, out_ref, packed_ref):
    bins, size = inverse_ref.shape[0], inverse_ref.shape[2]
    total_bins = pl.num_programs(0) * bins
    place_rows(member_ref[0], [own_ref.at[0], one_ref, two_ref, three_ref], packed_ref)
    identity = eye(size)
    rows = lax.broadcasted_iota(jnp.int32, (size, size), 0)
    columns = lax.broadcasted_iota(jnp.int32, (size, size), 1)
    for item in range(bins):
        packed = packed_ref[item].astype(F32)
        packed_t = packed.T
        re = jnp.where(columns >= rows, packed, packed_t).astype(BF16)
        im = jnp.where(columns == rows, 0.0, jnp.where(columns < rows, packed, -packed_t)).astype(BF16)
        high, low = inverse_ref[item, 0], inverse_ref[item, 1]
        both = dot(cat([high, low], 0), cat([cat([re, im], 1), cat([-im, re], 1)], 0))
        left = both[:size] + both[size:]
        left_re, left_im = left[:, :size], left[:, size:]
        left_high, left_low = split(cat([left_re + left_im, left_im - left_re], 1))
        middle = dot3(left_high, left_low, high, low, NT)
        place = pl.program_id(0) * bins + item
        out_ref[pl.ds(place, size, stride=total_bins), :] = (middle + identity) * (1.0 / SCALE)


def causal_kernel(real_ref, imag_ref, values_ref, *refs):
    *out_refs, table_high, table_low = refs
    count = real_ref.shape[1]
    sources, kept, own, lanes = values_ref.shape

    @pl.when(pl.program_id(0) == 0)
    def _():
        for part, table_ref in enumerate((real_ref, imag_ref)):
            high, low = split(table_ref[...])
            table_high[part * count : (part + 1) * count] = high
            table_low[part * count : (part + 1) * count] = low

    values = cat([values_ref[:, item].reshape(count, lanes) for item in range(kept)], 1)
    high, low = split(values)
    whole = dot(table_high[...], high) + (dot(table_high[...], low) + dot(table_low[...], high))
    for item in range(kept):
        for part in range(2):
            piece = whole[part * count : (part + 1) * count, item * lanes : (item + 1) * lanes]
            piece = piece.reshape(sources, own, lanes)
            step = own // len(out_refs)
            for chunk, out_ref in enumerate(out_refs):
                out_ref[:, item, part] = piece[:, chunk * step : (chunk + 1) * step]


def product_kernel(causal_ref, psi_ref, out_ref):
    bins, _, size, _ = psi_ref.shape
    total_bins = causal_ref.shape[0] // (2 * size)
    shape = (out_ref.shape[0], out_ref.shape[3], size)
    for item in range(bins):
        re, im = psi_ref[item, 0], psi_ref[item, 1]
        place = pl.program_id(0) * bins + item
        part_re = causal_ref[pl.ds(place, size, stride=2 * total_bins), :]
        part_im = causal_ref[pl.ds(total_bins + place, size, stride=2 * total_bins), :]
        added, taken = part_re + part_im, part_re - part_im
        high, low = split(0.5 * cat([taken.T + added, added.T - taken], 1))
        both = dot(cat([high, low], 0), cat([cat([re, -im], 1), cat([im, re], 1)], 0), NT)
        result = both[:size] + both[size:]
        out_ref[:, item, 0] = result[:, :size].reshape(shape)
        out_ref[:, item, 1] = result[:, size:].reshape(shape)


def projection_table(lag_limit, count, freq_size, pairs):
    own = count // (freq_size * 2 * pairs)

    def bins(index):
        return index // own % freq_size * (own * 2 * pairs) + index // (own * freq_size) * own + index % own

    row = lax.broadcasted_iota(jnp.int32, (count, 1), 0)
    column = lax.broadcasted_iota(jnp.int32, (1, count), 1)
    shift = bins(column) - bins(row)
    unit = math.pi / count
    half_angle = shift.astype(F32) * unit
    turned = ((2 * lag_limit + 1) * shift) % (2 * count)
    turned = jnp.where(turned >= count, turned - 2 * count, turned)
    last_angle = turned.astype(F32) * unit
    below = jnp.where(shift == 0, 1.0, 2.0 * count * jnp.sin(half_angle))
    real = jnp.where(shift == 0, (lag_limit.astype(F32) + 0.5) / count, jnp.sin(last_angle) / below)
    imag = jnp.where(shift == 0, 0.0, (jnp.cos(half_angle) - jnp.cos(last_angle)) / below)
    return real, imag


def params(limit):
    return pltpu.CompilerParams(vmem_limit_bytes=limit * MIB)


def cost(flops, moved):
    return pl.CostEstimate(flops=flops, bytes_accessed=moved, transcendentals=0)


def after(value, *earlier):
    return lax.optimization_barrier((value,) + earlier)[0]


SWAP = ((0, 1), (1, 0))
FLIP = ((0, 3), (1, 2), (2, 1), (3, 0))


def swap(value, distance):
    if distance == 1:
        return lax.ppermute(value, "pair", SWAP)
    if distance == 2:
        return lax.ppermute(value, "side", SWAP)
    return lax.ppermute(value, ("side", "pair"), FLIP)


def call(kernel, steps, in_specs, out_specs, out_shape, scratch, flops, moved, aliases={}):
    return pl.pallas_call(
        kernel,
        grid_spec=pltpu.PrefetchScalarGridSpec(
            num_scalar_prefetch=1,
            grid=(steps,),
            in_specs=in_specs,
            out_specs=out_specs,
            scratch_shapes=scratch,
        ),
        out_shape=out_shape,
        input_output_aliases=aliases,
        compiler_params=params(16),
        cost_estimate=cost(flops, moved),
    )


def shards(freq_size, pairs, factor, spectrum, guess_scale, lag_cutoff):
    chan = ("side", "pair")
    chan_size = 2 * pairs
    group_bins, _, rows, size = factor.shape
    own = group_bins // chan_size
    count = group_bins * freq_size
    chunks = CHUNKS if own % (4 * CHUNKS) == 0 else 1
    part = own // chunks
    step = math.gcd(part, 4)
    column_parts = min(freq_size, rows)
    lane_parts = freq_size // column_parts
    kept = rows // column_parts
    lanes = size // lane_parts
    side, pair = lax.axis_index("side"), lax.axis_index("pair")
    member = side * pairs + pair
    members = member.reshape(1)
    devices = chan_size * freq_size
    distances = range(1, chan_size)

    factors = factor.reshape(chan_size, own, 2, rows, size)

    def rows_for(owner, first, length):
        return lax.dynamic_slice(
            factors, (owner, first, 0, 0, 0), (1, length, 2, rows, size)
        ).reshape(length, 2, rows, size)

    arrived = []
    for chunk in range(chunks):
        pieces = [rows_for(member ^ d, chunk * part, part) for d in distances]
        if arrived:
            pieces = lax.optimization_barrier(tuple(pieces) + tuple(arrived[-1]))[: len(pieces)]
        arrived.append([swap(piece, d) for piece, d in zip(pieces, distances)])
    row_index = lax.broadcasted_iota(jnp.int32, (rows, size), 0) + member * rows
    column_index = lax.broadcasted_iota(jnp.int32, (rows, size), 1)
    packed = jnp.where(column_index >= row_index, spectrum[:, 0], spectrum[:, 1])
    packed = packed.reshape(chan_size, own, rows, size)
    pieces = [lax.dynamic_index_in_dim(packed, member ^ d, 0, keepdims=False) for d in distances]
    pieces = lax.optimization_barrier(tuple(pieces) + tuple(arrived[-1]))[: len(pieces)]
    packed_arrived = [swap(piece, d) for piece, d in zip(pieces, distances)]
    table_re, table_im = projection_table(lag_cutoff[0], count, freq_size, pairs)

    local_block = lambda first: pl.BlockSpec(
        (1, step, 2, rows, size), lambda i, m: (m[0], i + first, 0, 0, 0)
    )
    other_block = pl.BlockSpec((step, 2, rows, size), lambda i, m: (i, 0, 0, 0))
    inverse_block = pl.BlockSpec((step, 2, size, 2 * size), lambda i, m: (i, 0, 0, 0))
    state = []
    for chunk in range(chunks):
        scale = lax.dynamic_slice_in_dim(guess_scale, member * own + chunk * part, part, 0)
        offset = chunk * part // step
        state = call(
            newton_kernel,
            part // step,
            [pl.BlockSpec(memory_space=pltpu.SMEM), local_block(offset)]
            + [other_block] * 3
            + [pl.BlockSpec(memory_space=pl.ANY)] * len(state),
            [
                pl.BlockSpec(
                    (step, 2, size, 2 * size), lambda i, m, offset=offset: (i + offset, 0, 0, 0)
                ),
                pl.BlockSpec(
                    (step, 2, size, size), lambda i, m, offset=offset: (i + offset, 0, 0, 0)
                ),
            ],
            [
                jax.ShapeDtypeStruct((own, 2, size, 2 * size), BF16),
                jax.ShapeDtypeStruct((own, 2, size, size), BF16),
            ],
            [],
            part * 64 * 2 * 4 * size**3,
            part * 6 * 4 * size * size,
            {6 + index: index for index in range(len(state))},
        )(members, scale, factors, *arrived[chunk], *state)
    inverse, psi = state

    other = pl.BlockSpec((step, rows, size), lambda i, m: (i, 0, 0))
    middle = call(
        middle_kernel,
        own // step,
        [inverse_block, pl.BlockSpec((1, step, rows, size), lambda i, m: (m[0], i, 0, 0))]
        + [other] * 3,
        pl.BlockSpec((size * own, size), lambda i, m: (0, 0)),
        jax.ShapeDtypeStruct((size * own, size), F32),
        [pltpu.VMEM((step, size, size), BF16)],
        own * 10 * 2 * 4 * size**3,
        own * 6 * 4 * size * size,
    )(members, inverse, packed, *packed_arrived)
    sent = middle.astype(jnp.float16)
    if lane_parts > 1:
        sent = sent.reshape(size, own, lane_parts, lanes).transpose(0, 2, 1, 3)
    sent = sent.reshape(devices, kept, own, lanes)
    values = lax.all_to_all(sent, chan + ("freq",), 0, 0, tiled=True).astype(F32)
    sources, own_rows = devices, own
    if own % 8:
        values = values.transpose(1, 0, 2, 3).reshape(1, kept, count, lanes)
        sources, own_rows = 1, count
    twice = math.gcd(kept, 2)
    table_block = pl.BlockSpec((count, count), lambda i: (0, 0))
    causal = pl.pallas_call(
        causal_kernel,
        grid=(kept // twice,),
        in_specs=[
            table_block,
            table_block,
            pl.BlockSpec((sources, twice, own_rows, lanes), lambda i: (0, i, 0, 0)),
        ],
        out_specs=[pl.BlockSpec((sources, twice, 2, own_rows, lanes), lambda i: (0, i, 0, 0, 0))],
        out_shape=[jax.ShapeDtypeStruct((sources, kept, 2, own_rows, lanes), F32)],
        scratch_shapes=[pltpu.VMEM((2 * count, count), BF16), pltpu.VMEM((2 * count, count), BF16)],
        compiler_params=params(24),
        cost_estimate=cost(kept * 12 * count * count * lanes, 12 * kept * count * lanes),
    )(table_re, table_im, values)[0].astype(jnp.float16)
    if own % 8:
        causal = causal.reshape(kept, 2, devices, own, lanes).transpose(2, 0, 1, 3, 4)
    back = lax.all_to_all(causal, chan + ("freq",), 0, 0, tiled=True).astype(F32)
    if lane_parts > 1:
        back = back.reshape(chan_size * column_parts, lane_parts, kept, 2, own, lanes)
        back = back.transpose(0, 2, 3, 4, 1, 5)
    back = back.reshape(size * 2 * own, size)
    result = pl.pallas_call(
        product_kernel,
        grid=(own // step,),
        in_specs=[
            pl.BlockSpec(back.shape, lambda i: (0, 0)),
            pl.BlockSpec((step, 2, size, size), lambda i: (i, 0, 0, 0)),
        ],
        out_specs=pl.BlockSpec((chan_size, step, 2, rows, size), lambda i: (0, i, 0, 0, 0)),
        out_shape=jax.ShapeDtypeStruct((chan_size, own, 2, rows, size), F32),
        compiler_params=params(16),
        cost_estimate=cost(own * 4 * 4 * size**3, own * 5 * 4 * size * size),
    )(back, psi)
    result = lax.all_to_all(result.astype(jnp.float16), chan, 0, 0, tiled=True)
    whole = result.reshape(group_bins, 2, rows, size).astype(F32) * SCALE
    return jnp.swapaxes(whole, 2, 3)


def solution(mesh):
    freq_size, pairs = mesh.shape["freq"], mesh.shape["chan"] // 2
    split_mesh = jax.sharding.Mesh(
        mesh.devices.reshape(freq_size, 2, pairs), ("freq", "side", "pair")
    )
    in_specs = (
        P("freq", None, ("side", "pair"), None),
        P("freq", None, ("side", "pair"), None),
        P("freq"),
        P(),
    )
    out_specs = P("freq", None, None, ("side", "pair"))
    body = functools.partial(shards, freq_size, pairs)
    return jax.shard_map(
        body, mesh=split_mesh, in_specs=in_specs, out_specs=out_specs, check_vma=False
    )
```

```python
import functools
import math

import jax
import jax.numpy as jnp
from jax import lax
from jax.experimental import pallas as pl
from jax.experimental.pallas import tpu as pltpu
from jax.sharding import PartitionSpec as P

ITERS = 8
SCALE = 16.0
CHUNKS = 2
F32 = jnp.float32
BF16 = jnp.bfloat16
MIB = 1024 * 1024
NN = (((1,), (0,)), ((), ()))
NT = (((1,), (1,)), ((), ()))
TN = (((0,), (0,)), ((), ()))


def dot(left, right, dims=NN):
    return lax.dot_general(left, right, dims, preferred_element_type=F32)


def split(value):
    high = value.astype(BF16)
    return high, (value - high.astype(F32)).astype(BF16)


def cat(parts, axis):
    return jnp.concatenate(parts, axis=axis)


def dot3(left_high, left_low, right_high, right_low, dims=NN):
    rows = left_high.shape[0]
    both = dot(cat([left_high, left_low], 0), right_high, dims)
    return both[:rows] + (both[rows:] + dot(left_high, right_low, dims))


def eye(size):
    rows = lax.broadcasted_iota(jnp.int32, (size, size), 0)
    columns = lax.broadcasted_iota(jnp.int32, (size, size), 1)
    return jnp.where(rows == columns, 1.0, 0.0).astype(F32)


def place_rows(member, panels, out_ref):
    rows = panels[0].shape[-2]
    for index, panel in enumerate(panels):
        start = pl.multiple_of((member ^ index) * rows, rows)
        out_ref[..., pl.ds(start, rows), :] = panel[...]


def newton_kernel(member_ref, scale_ref, own_ref, one_ref, two_ref, three_ref, *refs):
    out_ref, psi_ref = refs[-2:]
    bins, _, size, _ = psi_ref.shape
    place_rows(member_ref[0], [own_ref.at[0], one_ref, two_ref, three_ref], psi_ref)
    identity = eye(size)
    state = []
    for item in range(bins):
        re, im = psi_ref[item, 0], psi_ref[item, 1]
        scale = scale_ref[pl.program_id(0) * bins + item]
        gram = dot(cat([re, im], 0), cat([cat([re, im], 1), cat([im, -re], 1)], 0), TN)
        sym = identity - scale * gram[:, :size]
        anti = -scale * gram[:, size:]
        state.append((sym, anti, None))
    for step in range(ITERS):
        after = []
        for sym, anti, total in state:
            left_high, left_low = split(cat([sym, anti], 1))
            if step == 0:
                total = identity + (sym + anti)
                right = cat([sym + anti, sym - anti], 0)
            elif step < ITERS - 1:
                right = cat([cat([sym + anti, total], 1), cat([sym - anti, total.T], 1)], 0)
            else:
                right = cat([total, total.T], 0)
            product = dot3(left_high, left_low, *split(right))
            if step > 0:
                total = total + product[:, -size:]
            if step < ITERS - 1:
                square = product[:, :size]
                square_t = square.T
                sym = 0.5 * (square + square_t)
                anti = 0.5 * (square - square_t)
            after.append((sym, anti, total))
        state = after
    for item in range(bins):
        total = state[item][2]
        total_t = total.T
        re, im = psi_ref[item, 0], psi_ref[item, 1]
        scale = scale_ref[pl.program_id(0) * bins + item]
        half = (0.5 * scale) * cat([total + total_t, total - total_t], 1)
        high, low = split(half)
        both = dot(cat([high, low], 0), cat([cat([re, im], 1), cat([-im, re], 1)], 0), NT)
        high, low = split(both[:size] + both[size:])
        out_ref[item, 0] = high
        out_ref[item, 1] = low


def middle_kernel(member_ref, inverse_ref, own_ref, one_ref, two_ref, three_ref, out_ref, packed_ref):
    bins, size = inverse_ref.shape[0], inverse_ref.shape[2]
    total_bins = pl.num_programs(0) * bins
    place_rows(member_ref[0], [own_ref.at[0], one_ref, two_ref, three_ref], packed_ref)
    identity = eye(size)
    rows = lax.broadcasted_iota(jnp.int32, (size, size), 0)
    columns = lax.broadcasted_iota(jnp.int32, (size, size), 1)

    def swapped(value):
        return cat([value, cat([value[:, size:], -value[:, :size]], 1)], 0)

    for item in range(bins):
        packed = packed_ref[item].astype(F32)
        packed_t = packed.T
        re = jnp.where(columns >= rows, packed, packed_t).astype(BF16)
        im = jnp.where(columns == rows, 0.0, jnp.where(columns < rows, packed, -packed_t)).astype(BF16)
        high, low = inverse_ref[item, 0], inverse_ref[item, 1]
        both = dot(cat([high, low], 0), cat([cat([re, im], 1), cat([-im, re], 1)], 0))
        left_high, left_low = split(both[:size] + both[size:])
        middle = dot3(left_high, left_low, swapped(high), swapped(low), NT)
        middle = middle[:, :size] - middle[:, size:]
        place = pl.program_id(0) * bins + item
        out_ref[pl.ds(place, size, stride=total_bins), :] = (middle + identity) * (1.0 / SCALE)


def causal_kernel(real_ref, imag_ref, values_ref, *refs):
    *out_refs, table_high, table_low = refs
    count = real_ref.shape[1]
    sources, kept, own, lanes = values_ref.shape

    @pl.when(pl.program_id(0) == 0)
    def _():
        for part, table_ref in enumerate((real_ref, imag_ref)):
            high, low = split(table_ref[...])
            table_high[part * count : (part + 1) * count] = high
            table_low[part * count : (part + 1) * count] = low

    values = cat([values_ref[:, item].reshape(count, lanes) for item in range(kept)], 1)
    high, low = split(values)
    whole = dot(table_high[...], high) + (dot(table_high[...], low) + dot(table_low[...], high))
    for item in range(kept):
        for part in range(2):
            piece = whole[part * count : (part + 1) * count, item * lanes : (item + 1) * lanes]
            piece = piece.reshape(sources, own, lanes)
            step = own // len(out_refs)
            for chunk, out_ref in enumerate(out_refs):
                out_ref[:, item, part] = piece[:, chunk * step : (chunk + 1) * step]


def product_kernel(causal_ref, psi_ref, out_ref):
    bins, _, size, _ = psi_ref.shape
    total_bins = causal_ref.shape[0] // (2 * size)
    shape = (out_ref.shape[0], out_ref.shape[3], size)
    for item in range(bins):
        re, im = psi_ref[item, 0], psi_ref[item, 1]
        place = pl.program_id(0) * bins + item
        part_re = causal_ref[pl.ds(place, size, stride=2 * total_bins), :]
        part_im = causal_ref[pl.ds(total_bins + place, size, stride=2 * total_bins), :]
        added, taken = part_re + part_im, part_re - part_im
        high, low = split(0.5 * cat([taken.T + added, added.T - taken], 1))
        both = dot(cat([high, low], 0), cat([cat([re, -im], 1), cat([im, re], 1)], 0), NT)
        result = both[:size] + both[size:]
        out_ref[:, item, 0] = result[:, :size].reshape(shape)
        out_ref[:, item, 1] = result[:, size:].reshape(shape)


def projection_table(lag_limit, count, freq_size, pairs):
    own = count // (freq_size * 2 * pairs)

    def bins(index):
        return index // own % freq_size * (own * 2 * pairs) + index // (own * freq_size) * own + index % own

    row = lax.broadcasted_iota(jnp.int32, (count, 1), 0)
    column = lax.broadcasted_iota(jnp.int32, (1, count), 1)
    shift = bins(column) - bins(row)
    unit = math.pi / count
    half_angle = shift.astype(F32) * unit
    turned = ((2 * lag_limit + 1) * shift) % (2 * count)
    turned = jnp.where(turned >= count, turned - 2 * count, turned)
    last_angle = turned.astype(F32) * unit
    below = jnp.where(shift == 0, 1.0, 2.0 * count * jnp.sin(half_angle))
    real = jnp.where(shift == 0, (lag_limit.astype(F32) + 0.5) / count, jnp.sin(last_angle) / below)
    imag = jnp.where(shift == 0, 0.0, (jnp.cos(half_angle) - jnp.cos(last_angle)) / below)
    return real, imag


def params(limit):
    return pltpu.CompilerParams(vmem_limit_bytes=limit * MIB)


def cost(flops, moved):
    return pl.CostEstimate(flops=flops, bytes_accessed=moved, transcendentals=0)


def after(value, *earlier):
    return lax.optimization_barrier((value,) + earlier)[0]


SWAP = ((0, 1), (1, 0))
FLIP = ((0, 3), (1, 2), (2, 1), (3, 0))


def swap(value, distance):
    if distance == 1:
        return lax.ppermute(value, "pair", SWAP)
    if distance == 2:
        return lax.ppermute(value, "side", SWAP)
    return lax.ppermute(value, ("side", "pair"), FLIP)


def call(kernel, steps, in_specs, out_specs, out_shape, scratch, flops, moved, aliases={}):
    return pl.pallas_call(
        kernel,
        grid_spec=pltpu.PrefetchScalarGridSpec(
            num_scalar_prefetch=1,
            grid=(steps,),
            in_specs=in_specs,
            out_specs=out_specs,
            scratch_shapes=scratch,
        ),
        out_shape=out_shape,
        input_output_aliases=aliases,
        compiler_params=params(16),
        cost_estimate=cost(flops, moved),
    )


def shards(freq_size, pairs, factor, spectrum, guess_scale, lag_cutoff):
    chan = ("side", "pair")
    chan_size = 2 * pairs
    group_bins, _, rows, size = factor.shape
    own = group_bins // chan_size
    count = group_bins * freq_size
    chunks = CHUNKS if own % (4 * CHUNKS) == 0 else 1
    part = own // chunks
    step = math.gcd(part, 4)
    column_parts = min(freq_size, rows)
    lane_parts = freq_size // column_parts
    kept = rows // column_parts
    lanes = size // lane_parts
    side, pair = lax.axis_index("side"), lax.axis_index("pair")
    member = side * pairs + pair
    members = member.reshape(1)
    devices = chan_size * freq_size
    distances = range(1, chan_size)

    factors = factor.reshape(chan_size, own, 2, rows, size)

    def rows_for(owner, first, length):
        return lax.dynamic_slice(
            factors, (owner, first, 0, 0, 0), (1, length, 2, rows, size)
        ).reshape(length, 2, rows, size)

    arrived = []
    for chunk in range(chunks):
        pieces = [rows_for(member ^ d, chunk * part, part) for d in distances]
        arrived.append([swap(piece, d) for piece, d in zip(pieces, distances)])
    row_index = lax.broadcasted_iota(jnp.int32, (rows, size), 0) + member * rows
    column_index = lax.broadcasted_iota(jnp.int32, (rows, size), 1)
    packed = jnp.where(column_index >= row_index, spectrum[:, 0], spectrum[:, 1])
    packed = packed.reshape(chan_size, own, rows, size)
    pieces = [lax.dynamic_index_in_dim(packed, member ^ d, 0, keepdims=False) for d in distances]
    pieces = lax.optimization_barrier(tuple(pieces) + tuple(arrived[0]))[: len(pieces)]
    packed_arrived = [swap(piece, d) for piece, d in zip(pieces, distances)]
    table_re, table_im = projection_table(lag_cutoff[0], count, freq_size, pairs)

    local_block = lambda first: pl.BlockSpec(
        (1, step, 2, rows, size), lambda i, m: (m[0], i + first, 0, 0, 0)
    )
    other_block = pl.BlockSpec((step, 2, rows, size), lambda i, m: (i, 0, 0, 0))
    inverse_block = pl.BlockSpec((step, 2, size, 2 * size), lambda i, m: (i, 0, 0, 0))
    state = []
    for chunk in range(chunks):
        scale = lax.dynamic_slice_in_dim(guess_scale, member * own + chunk * part, part, 0)
        offset = chunk * part // step
        state = call(
            newton_kernel,
            part // step,
            [pl.BlockSpec(memory_space=pltpu.SMEM), local_block(offset)]
            + [other_block] * 3
            + [pl.BlockSpec(memory_space=pl.ANY)] * len(state),
            [
                pl.BlockSpec(
                    (step, 2, size, 2 * size), lambda i, m, offset=offset: (i + offset, 0, 0, 0)
                ),
                pl.BlockSpec(
                    (step, 2, size, size), lambda i, m, offset=offset: (i + offset, 0, 0, 0)
                ),
            ],
            [
                jax.ShapeDtypeStruct((own, 2, size, 2 * size), BF16),
                jax.ShapeDtypeStruct((own, 2, size, size), BF16),
            ],
            [],
            part * 64 * 2 * 4 * size**3,
            part * 6 * 4 * size * size,
            {6 + index: index for index in range(len(state))},
        )(members, scale, factors, *arrived[chunk], *state)
    inverse, psi = state

    other = pl.BlockSpec((step, rows, size), lambda i, m: (i, 0, 0))
    middle = call(
        middle_kernel,
        own // step,
        [inverse_block, pl.BlockSpec((1, step, rows, size), lambda i, m: (m[0], i, 0, 0))]
        + [other] * 3,
        pl.BlockSpec((size * own, size), lambda i, m: (0, 0)),
        jax.ShapeDtypeStruct((size * own, size), F32),
        [pltpu.VMEM((step, size, size), BF16)],
        own * 10 * 2 * 4 * size**3,
        own * 6 * 4 * size * size,
    )(members, inverse, packed, *packed_arrived)
    sent = middle.astype(jnp.float16)
    if lane_parts > 1:
        sent = sent.reshape(size, own, lane_parts, lanes).transpose(0, 2, 1, 3)
    sent = sent.reshape(devices, kept, own, lanes)
    values = lax.all_to_all(sent, chan + ("freq",), 0, 0, tiled=True).astype(F32)
    sources, own_rows = devices, own
    if own % 8:
        values = values.transpose(1, 0, 2, 3).reshape(1, kept, count, lanes)
        sources, own_rows = 1, count
    twice = math.gcd(kept, 2)
    table_block = pl.BlockSpec((count, count), lambda i: (0, 0))
    causal = pl.pallas_call(
        causal_kernel,
        grid=(kept // twice,),
        in_specs=[
            table_block,
            table_block,
            pl.BlockSpec((sources, twice, own_rows, lanes), lambda i: (0, i, 0, 0)),
        ],
        out_specs=[pl.BlockSpec((sources, twice, 2, own_rows, lanes), lambda i: (0, i, 0, 0, 0))],
        out_shape=[jax.ShapeDtypeStruct((sources, kept, 2, own_rows, lanes), F32)],
        scratch_shapes=[pltpu.VMEM((2 * count, count), BF16), pltpu.VMEM((2 * count, count), BF16)],
        compiler_params=params(24),
        cost_estimate=cost(kept * 12 * count * count * lanes, 12 * kept * count * lanes),
    )(table_re, table_im, values)[0].astype(jnp.float16)
    if own % 8:
        causal = causal.reshape(kept, 2, devices, own, lanes).transpose(2, 0, 1, 3, 4)
    back = lax.all_to_all(causal, chan + ("freq",), 0, 0, tiled=True).astype(F32)
    if lane_parts > 1:
        back = back.reshape(chan_size * column_parts, lane_parts, kept, 2, own, lanes)
        back = back.transpose(0, 2, 3, 4, 1, 5)
    back = back.reshape(size * 2 * own, size)
    result = pl.pallas_call(
        product_kernel,
        grid=(own // step,),
        in_specs=[
            pl.BlockSpec(back.shape, lambda i: (0, 0)),
            pl.BlockSpec((step, 2, size, size), lambda i: (i, 0, 0, 0)),
        ],
        out_specs=pl.BlockSpec((chan_size, step, 2, rows, size), lambda i: (0, i, 0, 0, 0)),
        out_shape=jax.ShapeDtypeStruct((chan_size, own, 2, rows, size), F32),
        compiler_params=params(16),
        cost_estimate=cost(own * 4 * 4 * size**3, own * 5 * 4 * size * size),
    )(back, psi)
    result = lax.all_to_all(result.astype(jnp.float16), chan, 0, 0, tiled=True)
    whole = result.reshape(group_bins, 2, rows, size).astype(F32) * SCALE
    return jnp.swapaxes(whole, 2, 3)


def solution(mesh):
    freq_size, pairs = mesh.shape["freq"], mesh.shape["chan"] // 2
    split_mesh = jax.sharding.Mesh(
        mesh.devices.reshape(freq_size, 2, pairs), ("freq", "side", "pair")
    )
    in_specs = (
        P("freq", None, ("side", "pair"), None),
        P("freq", None, ("side", "pair"), None),
        P("freq"),
        P(),
    )
    out_specs = P("freq", None, None, ("side", "pair"))
    body = functools.partial(shards, freq_size, pairs)
    return jax.shard_map(
        body, mesh=split_mesh, in_specs=in_specs, out_specs=out_specs, check_vma=False
    )
```

```python
import functools
import math

import jax
import jax.numpy as jnp
from jax import lax
from jax.experimental import pallas as pl
from jax.experimental.pallas import tpu as pltpu
from jax.sharding import PartitionSpec as P

ITERS = 8
SCALE = 16.0
CHUNKS = 2
F32 = jnp.float32
BF16 = jnp.bfloat16
MIB = 1024 * 1024
NN = (((1,), (0,)), ((), ()))
NT = (((1,), (1,)), ((), ()))
TN = (((0,), (0,)), ((), ()))


def dot(left, right, dims=NN):
    return lax.dot_general(left, right, dims, preferred_element_type=F32)


def split(value):
    high = value.astype(BF16)
    return high, (value - high.astype(F32)).astype(BF16)


def cat(parts, axis):
    return jnp.concatenate(parts, axis=axis)


def dot3(left_high, left_low, right_high, right_low, dims=NN):
    rows = left_high.shape[0]
    both = dot(cat([left_high, left_low], 0), right_high, dims)
    return both[:rows] + (both[rows:] + dot(left_high, right_low, dims))


def eye(size):
    rows = lax.broadcasted_iota(jnp.int32, (size, size), 0)
    columns = lax.broadcasted_iota(jnp.int32, (size, size), 1)
    return jnp.where(rows == columns, 1.0, 0.0).astype(F32)


def place_rows(member, panels, out_ref):
    rows = panels[0].shape[-2]
    for index, panel in enumerate(panels):
        start = pl.multiple_of((member ^ index) * rows, rows)
        out_ref[..., pl.ds(start, rows), :] = panel[...]


def newton_kernel(member_ref, scale_ref, own_ref, one_ref, two_ref, three_ref, *refs):
    out_ref, psi_ref = refs[-2:]
    bins, _, size, _ = psi_ref.shape
    place_rows(member_ref[0], [own_ref.at[0], one_ref, two_ref, three_ref], psi_ref)
    identity = eye(size)
    state = []
    for item in range(bins):
        re, im = psi_ref[item, 0], psi_ref[item, 1]
        scale = scale_ref[pl.program_id(0) * bins + item]
        gram = dot(cat([re, im], 0), cat([cat([re, im], 1), cat([im, -re], 1)], 0), TN)
        sym = identity - scale * gram[:, :size]
        anti = -scale * gram[:, size:]
        state.append((sym, anti, None))
    for step in range(ITERS):
        after = []
        for sym, anti, total in state:
            left_high, left_low = split(cat([sym, anti], 1))
            if step == 0:
                total = identity + (sym + anti)
                right = cat([sym + anti, sym - anti], 0)
            elif step < ITERS - 1:
                right = cat([cat([sym + anti, total], 1), cat([sym - anti, total.T], 1)], 0)
            else:
                right = cat([total, total.T], 0)
            product = dot3(left_high, left_low, *split(right))
            if step > 0:
                total = total + product[:, -size:]
            if step < ITERS - 1:
                square = product[:, :size]
                square_t = square.T
                sym = 0.5 * (square + square_t)
                anti = 0.5 * (square - square_t)
            after.append((sym, anti, total))
        state = after
    for item in range(bins):
        total = state[item][2]
        total_t = total.T
        re, im = psi_ref[item, 0], psi_ref[item, 1]
        scale = scale_ref[pl.program_id(0) * bins + item]
        half = (0.5 * scale) * cat([total + total_t, total - total_t], 1)
        high, low = split(half)
        both = dot(cat([high, low], 0), cat([cat([re, im], 1), cat([-im, re], 1)], 0), NT)
        high, low = split(both[:size] + both[size:])
        out_ref[item, 0] = high
        out_ref[item, 1] = low


def middle_kernel(member_ref, inverse_ref, own_ref, one_ref, two_ref, three_ref, out_ref, packed_ref):
    bins, size = inverse_ref.shape[0], inverse_ref.shape[2]
    total_bins = pl.num_programs(0) * bins
    place_rows(member_ref[0], [own_ref.at[0], one_ref, two_ref, three_ref], packed_ref)
    identity = eye(size)
    rows = lax.broadcasted_iota(jnp.int32, (size, size), 0)
    columns = lax.broadcasted_iota(jnp.int32, (size, size), 1)

    def swapped(value):
        return cat([value, cat([value[:, size:], -value[:, :size]], 1)], 0)

    for item in range(bins):
        packed = packed_ref[item].astype(F32)
        packed_t = packed.T
        re = jnp.where(columns >= rows, packed, packed_t).astype(BF16)
        im = jnp.where(columns == rows, 0.0, jnp.where(columns < rows, packed, -packed_t)).astype(BF16)
        high, low = inverse_ref[item, 0], inverse_ref[item, 1]
        both = dot(cat([high, low], 0), cat([cat([re, im], 1), cat([-im, re], 1)], 0))
        left_high, left_low = split(both[:size] + both[size:])
        middle = dot3(left_high, left_low, swapped(high), swapped(low), NT)
        middle = middle[:, :size] - middle[:, size:]
        place = pl.program_id(0) * bins + item
        out_ref[pl.ds(place, size, stride=total_bins), :] = (middle + identity) * (1.0 / SCALE)


def causal_kernel(real_ref, imag_ref, values_ref, *refs):
    *out_refs, table_high, table_low = refs
    count = real_ref.shape[1]
    sources, kept, own, lanes = values_ref.shape

    @pl.when(pl.program_id(0) == 0)
    def _():
        for part, table_ref in enumerate((real_ref, imag_ref)):
            high, low = split(table_ref[...])
            table_high[part * count : (part + 1) * count] = high
            table_low[part * count : (part + 1) * count] = low

    values = cat([values_ref[:, item].reshape(count, lanes) for item in range(kept)], 1)
    high, low = split(values)
    whole = dot(table_high[...], high) + (dot(table_high[...], low) + dot(table_low[...], high))
    for item in range(kept):
        for part in range(2):
            piece = whole[part * count : (part + 1) * count, item * lanes : (item + 1) * lanes]
            piece = piece.reshape(sources, own, lanes)
            step = own // len(out_refs)
            for chunk, out_ref in enumerate(out_refs):
                out_ref[:, item, part] = piece[:, chunk * step : (chunk + 1) * step]


def product_kernel(causal_ref, psi_ref, out_ref):
    bins, _, size, _ = psi_ref.shape
    total_bins = causal_ref.shape[0] // (2 * size)
    shape = (out_ref.shape[0], out_ref.shape[3], size)
    for item in range(bins):
        re, im = psi_ref[item, 0], psi_ref[item, 1]
        place = pl.program_id(0) * bins + item
        part_re = causal_ref[pl.ds(place, size, stride=2 * total_bins), :]
        part_im = causal_ref[pl.ds(total_bins + place, size, stride=2 * total_bins), :]
        added, taken = part_re + part_im, part_re - part_im
        high, low = split(0.5 * cat([taken.T + added, added.T - taken], 1))
        both = dot(cat([high, low], 0), cat([cat([re, -im], 1), cat([im, re], 1)], 0), NT)
        result = both[:size] + both[size:]
        out_ref[:, item, 0] = result[:, :size].reshape(shape)
        out_ref[:, item, 1] = result[:, size:].reshape(shape)


def projection_table(lag_limit, count, freq_size, pairs):
    own = count // (freq_size * 2 * pairs)

    def bins(index):
        return index // own % freq_size * (own * 2 * pairs) + index // (own * freq_size) * own + index % own

    row = lax.broadcasted_iota(jnp.int32, (count, 1), 0)
    column = lax.broadcasted_iota(jnp.int32, (1, count), 1)
    shift = bins(column) - bins(row)
    unit = math.pi / count
    half_angle = shift.astype(F32) * unit
    turned = ((2 * lag_limit + 1) * shift) % (2 * count)
    turned = jnp.where(turned >= count, turned - 2 * count, turned)
    last_angle = turned.astype(F32) * unit
    below = jnp.where(shift == 0, 1.0, 2.0 * count * jnp.sin(half_angle))
    real = jnp.where(shift == 0, (lag_limit.astype(F32) + 0.5) / count, jnp.sin(last_angle) / below)
    imag = jnp.where(shift == 0, 0.0, (jnp.cos(half_angle) - jnp.cos(last_angle)) / below)
    return real, imag


def params(limit):
    return pltpu.CompilerParams(vmem_limit_bytes=limit * MIB)


def cost(flops, moved):
    return pl.CostEstimate(flops=flops, bytes_accessed=moved, transcendentals=0)


def after(value, *earlier):
    return lax.optimization_barrier((value,) + earlier)[0]


SWAP = ((0, 1), (1, 0))
FLIP = ((0, 3), (1, 2), (2, 1), (3, 0))


def swap(value, distance):
    if distance == 1:
        return lax.ppermute(value, "pair", SWAP)
    if distance == 2:
        return lax.ppermute(value, "side", SWAP)
    return lax.ppermute(value, ("side", "pair"), FLIP)


def call(kernel, steps, in_specs, out_specs, out_shape, scratch, flops, moved, aliases={}):
    return pl.pallas_call(
        kernel,
        grid_spec=pltpu.PrefetchScalarGridSpec(
            num_scalar_prefetch=1,
            grid=(steps,),
            in_specs=in_specs,
            out_specs=out_specs,
            scratch_shapes=scratch,
        ),
        out_shape=out_shape,
        input_output_aliases=aliases,
        compiler_params=params(16),
        cost_estimate=cost(flops, moved),
    )


def shards(freq_size, pairs, factor, spectrum, guess_scale, lag_cutoff):
    chan = ("side", "pair")
    chan_size = 2 * pairs
    group_bins, _, rows, size = factor.shape
    own = group_bins // chan_size
    count = group_bins * freq_size
    chunks = CHUNKS if own % (4 * CHUNKS) == 0 else 1
    part = own // chunks
    step = math.gcd(part, 4)
    column_parts = min(freq_size, rows)
    lane_parts = freq_size // column_parts
    kept = rows // column_parts
    lanes = size // lane_parts
    side, pair = lax.axis_index("side"), lax.axis_index("pair")
    member = side * pairs + pair
    members = member.reshape(1)
    devices = chan_size * freq_size
    distances = range(1, chan_size)

    factors = factor.reshape(chan_size, own, 2, rows, size)

    def rows_for(owner, first, length):
        return lax.dynamic_slice(
            factors, (owner, first, 0, 0, 0), (1, length, 2, rows, size)
        ).reshape(length, 2, rows, size)

    arrived = []
    for chunk in range(chunks):
        pieces = [rows_for(member ^ d, chunk * part, part) for d in distances]
        arrived.append([swap(piece, d) for piece, d in zip(pieces, distances)])
    row_index = lax.broadcasted_iota(jnp.int32, (rows, size), 0) + member * rows
    column_index = lax.broadcasted_iota(jnp.int32, (rows, size), 1)
    packed = jnp.where(column_index >= row_index, spectrum[:, 0], spectrum[:, 1])
    packed = packed.reshape(chan_size, own, rows, size)
    pieces = [lax.dynamic_index_in_dim(packed, member ^ d, 0, keepdims=False) for d in distances]
    table_re, table_im = projection_table(lag_cutoff[0], count, freq_size, pairs)

    local_block = lambda first: pl.BlockSpec(
        (1, step, 2, rows, size), lambda i, m: (m[0], i + first, 0, 0, 0)
    )
    other_block = pl.BlockSpec((step, 2, rows, size), lambda i, m: (i, 0, 0, 0))
    inverse_block = pl.BlockSpec((step, 2, size, 2 * size), lambda i, m: (i, 0, 0, 0))
    state, packed_arrived = [], []
    for chunk in range(chunks):
        scale = lax.dynamic_slice_in_dim(guess_scale, member * own + chunk * part, part, 0)
        offset = chunk * part // step
        state = call(
            newton_kernel,
            part // step,
            [pl.BlockSpec(memory_space=pltpu.SMEM), local_block(offset)]
            + [other_block] * 3
            + [pl.BlockSpec(memory_space=pl.ANY)] * len(state),
            [
                pl.BlockSpec(
                    (step, 2, size, 2 * size), lambda i, m, offset=offset: (i + offset, 0, 0, 0)
                ),
                pl.BlockSpec(
                    (step, 2, size, size), lambda i, m, offset=offset: (i + offset, 0, 0, 0)
                ),
            ],
            [
                jax.ShapeDtypeStruct((own, 2, size, 2 * size), BF16),
                jax.ShapeDtypeStruct((own, 2, size, size), BF16),
            ],
            [],
            part * 64 * 2 * 4 * size**3,
            part * 6 * 4 * size * size,
            {6 + index: index for index in range(len(state))},
        )(members, scale, factors, *arrived[chunk], *state)
        if chunk == 0:
            held = lax.optimization_barrier(tuple(pieces) + tuple(state))
            state = held[len(pieces) :]
            packed_arrived = [swap(piece, d) for piece, d in zip(held, distances)]
    inverse, psi = state

    other = pl.BlockSpec((step, rows, size), lambda i, m: (i, 0, 0))
    middle = call(
        middle_kernel,
        own // step,
        [inverse_block, pl.BlockSpec((1, step, rows, size), lambda i, m: (m[0], i, 0, 0))]
        + [other] * 3,
        pl.BlockSpec((size * own, size), lambda i, m: (0, 0)),
        jax.ShapeDtypeStruct((size * own, size), F32),
        [pltpu.VMEM((step, size, size), BF16)],
        own * 10 * 2 * 4 * size**3,
        own * 6 * 4 * size * size,
    )(members, inverse, packed, *packed_arrived)
    sent = middle.astype(jnp.float16)
    if lane_parts > 1:
        sent = sent.reshape(size, own, lane_parts, lanes).transpose(0, 2, 1, 3)
    sent = sent.reshape(devices, kept, own, lanes)
    values = lax.all_to_all(sent, chan + ("freq",), 0, 0, tiled=True).astype(F32)
    sources, own_rows = devices, own
    if own % 8:
        values = values.transpose(1, 0, 2, 3).reshape(1, kept, count, lanes)
        sources, own_rows = 1, count
    twice = math.gcd(kept, 2)
    table_block = pl.BlockSpec((count, count), lambda i: (0, 0))
    causal = pl.pallas_call(
        causal_kernel,
        grid=(kept // twice,),
        in_specs=[
            table_block,
            table_block,
            pl.BlockSpec((sources, twice, own_rows, lanes), lambda i: (0, i, 0, 0)),
        ],
        out_specs=[pl.BlockSpec((sources, twice, 2, own_rows, lanes), lambda i: (0, i, 0, 0, 0))],
        out_shape=[jax.ShapeDtypeStruct((sources, kept, 2, own_rows, lanes), F32)],
        scratch_shapes=[pltpu.VMEM((2 * count, count), BF16), pltpu.VMEM((2 * count, count), BF16)],
        compiler_params=params(24),
        cost_estimate=cost(kept * 12 * count * count * lanes, 12 * kept * count * lanes),
    )(table_re, table_im, values)[0].astype(jnp.float16)
    if own % 8:
        causal = causal.reshape(kept, 2, devices, own, lanes).transpose(2, 0, 1, 3, 4)
    back = lax.all_to_all(causal, chan + ("freq",), 0, 0, tiled=True).astype(F32)
    if lane_parts > 1:
        back = back.reshape(chan_size * column_parts, lane_parts, kept, 2, own, lanes)
        back = back.transpose(0, 2, 3, 4, 1, 5)
    back = back.reshape(size * 2 * own, size)
    result = pl.pallas_call(
        product_kernel,
        grid=(own // step,),
        in_specs=[
            pl.BlockSpec(back.shape, lambda i: (0, 0)),
            pl.BlockSpec((step, 2, size, size), lambda i: (i, 0, 0, 0)),
        ],
        out_specs=pl.BlockSpec((chan_size, step, 2, rows, size), lambda i: (0, i, 0, 0, 0)),
        out_shape=jax.ShapeDtypeStruct((chan_size, own, 2, rows, size), F32),
        compiler_params=params(16),
        cost_estimate=cost(own * 4 * 4 * size**3, own * 5 * 4 * size * size),
    )(back, psi)
    result = lax.all_to_all(result.astype(jnp.float16), chan, 0, 0, tiled=True)
    whole = result.reshape(group_bins, 2, rows, size).astype(F32) * SCALE
    return jnp.swapaxes(whole, 2, 3)


def solution(mesh):
    freq_size, pairs = mesh.shape["freq"], mesh.shape["chan"] // 2
    split_mesh = jax.sharding.Mesh(
        mesh.devices.reshape(freq_size, 2, pairs), ("freq", "side", "pair")
    )
    in_specs = (
        P("freq", None, ("side", "pair"), None),
        P("freq", None, ("side", "pair"), None),
        P("freq"),
        P(),
    )
    out_specs = P("freq", None, None, ("side", "pair"))
    body = functools.partial(shards, freq_size, pairs)
    return jax.shard_map(
        body, mesh=split_mesh, in_specs=in_specs, out_specs=out_specs, check_vma=False
    )
```

```python
import functools
import math

import jax
import jax.numpy as jnp
from jax import lax
from jax.experimental import pallas as pl
from jax.experimental.pallas import tpu as pltpu
from jax.sharding import PartitionSpec as P

ITERS = 8
SCALE = 16.0
CHUNKS = 2
F32 = jnp.float32
BF16 = jnp.bfloat16
MIB = 1024 * 1024
NN = (((1,), (0,)), ((), ()))
NT = (((1,), (1,)), ((), ()))
TN = (((0,), (0,)), ((), ()))


def dot(left, right, dims=NN):
    return lax.dot_general(left, right, dims, preferred_element_type=F32)


def split(value):
    high = value.astype(BF16)
    return high, (value - high.astype(F32)).astype(BF16)


def cat(parts, axis):
    return jnp.concatenate(parts, axis=axis)


def dot3(left_high, left_low, right_high, right_low, dims=NN):
    rows = left_high.shape[0]
    both = dot(cat([left_high, left_low], 0), right_high, dims)
    return both[:rows] + (both[rows:] + dot(left_high, right_low, dims))


def eye(size):
    rows = lax.broadcasted_iota(jnp.int32, (size, size), 0)
    columns = lax.broadcasted_iota(jnp.int32, (size, size), 1)
    return jnp.where(rows == columns, 1.0, 0.0).astype(F32)


def place_rows(member, panels, out_ref):
    rows = panels[0].shape[-2]
    for index, panel in enumerate(panels):
        start = pl.multiple_of((member ^ index) * rows, rows)
        out_ref[..., pl.ds(start, rows), :] = panel[...]


def newton_kernel(member_ref, scale_ref, own_ref, one_ref, two_ref, three_ref, *refs):
    out_ref, psi_ref = refs[-2:]
    bins, _, size, _ = psi_ref.shape
    place_rows(member_ref[0], [own_ref.at[0], one_ref, two_ref, three_ref], psi_ref)
    identity = eye(size)
    state = []
    for item in range(bins):
        re, im = psi_ref[item, 0], psi_ref[item, 1]
        scale = scale_ref[pl.program_id(0) * bins + item]
        gram = dot(cat([re, im], 0), cat([cat([re, im], 1), cat([im, -re], 1)], 0), TN)
        sym = identity - scale * gram[:, :size]
        anti = -scale * gram[:, size:]
        state.append((sym, anti, None))
    for step in range(ITERS):
        after = []
        for sym, anti, total in state:
            left_high, left_low = split(cat([sym, anti], 1))
            if step == 0:
                total = identity + (sym + anti)
                right = cat([sym + anti, sym - anti], 0)
            elif step < ITERS - 1:
                right = cat([cat([sym + anti, total], 1), cat([sym - anti, total.T], 1)], 0)
            else:
                right = cat([total, total.T], 0)
            product = dot3(left_high, left_low, *split(right))
            if step > 0:
                total = total + product[:, -size:]
            if step < ITERS - 1:
                square = product[:, :size]
                square_t = square.T
                sym = 0.5 * (square + square_t)
                anti = 0.5 * (square - square_t)
            after.append((sym, anti, total))
        state = after
    for item in range(bins):
        total = state[item][2]
        total_t = total.T
        re, im = psi_ref[item, 0], psi_ref[item, 1]
        scale = scale_ref[pl.program_id(0) * bins + item]
        half = (0.5 * scale) * cat([total + total_t, total - total_t], 1)
        high, low = split(half)
        both = dot(cat([high, low], 0), cat([cat([re, im], 1), cat([-im, re], 1)], 0), NT)
        high, low = split(both[:size] + both[size:])
        out_ref[item, 0] = high
        out_ref[item, 1] = low


def middle_kernel(member_ref, inverse_ref, own_ref, one_ref, two_ref, three_ref, out_ref, packed_ref):
    bins, size = inverse_ref.shape[0], inverse_ref.shape[2]
    total_bins = pl.num_programs(0) * bins
    place_rows(member_ref[0], [own_ref.at[0], one_ref, two_ref, three_ref], packed_ref)
    identity = eye(size)
    rows = lax.broadcasted_iota(jnp.int32, (size, size), 0)
    columns = lax.broadcasted_iota(jnp.int32, (size, size), 1)

    def swapped(value):
        return cat([value, cat([value[:, size:], -value[:, :size]], 1)], 0)

    for item in range(bins):
        packed = packed_ref[item].astype(F32)
        packed_t = packed.T
        re = jnp.where(columns >= rows, packed, packed_t).astype(BF16)
        im = jnp.where(columns == rows, 0.0, jnp.where(columns < rows, packed, -packed_t)).astype(BF16)
        high, low = inverse_ref[item, 0], inverse_ref[item, 1]
        both = dot(cat([high, low], 0), cat([cat([re, im], 1), cat([-im, re], 1)], 0))
        left_high, left_low = split(both[:size] + both[size:])
        middle = dot3(left_high, left_low, swapped(high), swapped(low), NT)
        middle = middle[:, :size] - middle[:, size:]
        place = pl.program_id(0) * bins + item
        out_ref[pl.ds(place, size, stride=total_bins), :] = (middle + identity) * (1.0 / SCALE)


def causal_kernel(real_ref, imag_ref, values_ref, *refs):
    *out_refs, table_high, table_low = refs
    count = real_ref.shape[1]
    sources, kept, own, lanes = values_ref.shape

    @pl.when(pl.program_id(0) == 0)
    def _():
        for part, table_ref in enumerate((real_ref, imag_ref)):
            high, low = split(table_ref[...])
            table_high[part * count : (part + 1) * count] = high
            table_low[part * count : (part + 1) * count] = low

    values = cat([values_ref[:, item].reshape(count, lanes) for item in range(kept)], 1)
    high, low = split(values)
    whole = dot(table_high[...], high) + (dot(table_high[...], low) + dot(table_low[...], high))
    for item in range(kept):
        for part in range(2):
            piece = whole[part * count : (part + 1) * count, item * lanes : (item + 1) * lanes]
            piece = piece.reshape(sources, own, lanes)
            step = own // len(out_refs)
            for chunk, out_ref in enumerate(out_refs):
                out_ref[:, item, part] = piece[:, chunk * step : (chunk + 1) * step]


def product_kernel(causal_ref, psi_ref, out_ref):
    bins, _, size, _ = psi_ref.shape
    total_bins = causal_ref.shape[0] // (2 * size)
    shape = (out_ref.shape[0], out_ref.shape[3], size)
    for item in range(bins):
        re, im = psi_ref[item, 0], psi_ref[item, 1]
        place = pl.program_id(0) * bins + item
        part_re = causal_ref[pl.ds(place, size, stride=2 * total_bins), :]
        part_im = causal_ref[pl.ds(total_bins + place, size, stride=2 * total_bins), :]
        added, taken = part_re + part_im, part_re - part_im
        high, low = split(0.5 * cat([taken.T + added, added.T - taken], 1))
        both = dot(cat([high, low], 0), cat([cat([re, -im], 1), cat([im, re], 1)], 0), NT)
        result = both[:size] + both[size:]
        out_ref[:, item, 0] = result[:, :size].reshape(shape)
        out_ref[:, item, 1] = result[:, size:].reshape(shape)


def projection_table(lag_limit, count, freq_size, pairs):
    own = count // (freq_size * 2 * pairs)

    def bins(index):
        return index // own % freq_size * (own * 2 * pairs) + index // (own * freq_size) * own + index % own

    row = lax.broadcasted_iota(jnp.int32, (count, 1), 0)
    column = lax.broadcasted_iota(jnp.int32, (1, count), 1)
    shift = bins(column) - bins(row)
    unit = math.pi / count
    half_angle = shift.astype(F32) * unit
    turned = ((2 * lag_limit + 1) * shift) % (2 * count)
    turned = jnp.where(turned >= count, turned - 2 * count, turned)
    last_angle = turned.astype(F32) * unit
    below = jnp.where(shift == 0, 1.0, 2.0 * count * jnp.sin(half_angle))
    real = jnp.where(shift == 0, (lag_limit.astype(F32) + 0.5) / count, jnp.sin(last_angle) / below)
    imag = jnp.where(shift == 0, 0.0, (jnp.cos(half_angle) - jnp.cos(last_angle)) / below)
    return real, imag


def params(limit):
    return pltpu.CompilerParams(vmem_limit_bytes=limit * MIB)


def cost(flops, moved):
    return pl.CostEstimate(flops=flops, bytes_accessed=moved, transcendentals=0)


def after(value, *earlier):
    return lax.optimization_barrier((value,) + earlier)[0]


SWAP = ((0, 1), (1, 0))
FLIP = ((0, 3), (1, 2), (2, 1), (3, 0))


def swap(value, distance):
    if distance == 1:
        return lax.ppermute(value, "pair", SWAP)
    if distance == 2:
        return lax.ppermute(value, "side", SWAP)
    return lax.ppermute(value, ("side", "pair"), FLIP)


def call(kernel, steps, in_specs, out_specs, out_shape, scratch, flops, moved, aliases={}):
    return pl.pallas_call(
        kernel,
        grid_spec=pltpu.PrefetchScalarGridSpec(
            num_scalar_prefetch=1,
            grid=(steps,),
            in_specs=in_specs,
            out_specs=out_specs,
            scratch_shapes=scratch,
        ),
        out_shape=out_shape,
        input_output_aliases=aliases,
        compiler_params=params(16),
        cost_estimate=cost(flops, moved),
    )


def shards(freq_size, pairs, factor, spectrum, guess_scale, lag_cutoff):
    chan = ("side", "pair")
    chan_size = 2 * pairs
    group_bins, _, rows, size = factor.shape
    own = group_bins // chan_size
    count = group_bins * freq_size
    chunks = CHUNKS if own % (4 * CHUNKS) == 0 else 1
    part = own // chunks
    step = math.gcd(part, 4)
    column_parts = min(freq_size, rows)
    lane_parts = freq_size // column_parts
    kept = rows // column_parts
    lanes = size // lane_parts
    side, pair = lax.axis_index("side"), lax.axis_index("pair")
    member = side * pairs + pair
    members = member.reshape(1)
    devices = chan_size * freq_size
    distances = range(1, chan_size)

    factors = factor.reshape(chan_size, own, 2, rows, size)

    def rows_for(owner, first, length):
        return lax.dynamic_slice(
            factors, (owner, first, 0, 0, 0), (1, length, 2, rows, size)
        ).reshape(length, 2, rows, size)

    arrived = []
    for chunk in range(chunks):
        pieces = [rows_for(member ^ d, chunk * part, part) for d in distances]
        if arrived:
            pieces = lax.optimization_barrier((*pieces, arrived[-1][0]))[: len(pieces)]
        arrived.append([swap(piece, d) for piece, d in zip(pieces, distances)])
    row_index = lax.broadcasted_iota(jnp.int32, (rows, size), 0) + member * rows
    column_index = lax.broadcasted_iota(jnp.int32, (rows, size), 1)
    packed = jnp.where(column_index >= row_index, spectrum[:, 0], spectrum[:, 1])
    packed = packed.reshape(chan_size, own, rows, size)
    pieces = [lax.dynamic_index_in_dim(packed, member ^ d, 0, keepdims=False) for d in distances]
    table_re, table_im = projection_table(lag_cutoff[0], count, freq_size, pairs)

    local_block = lambda first: pl.BlockSpec(
        (1, step, 2, rows, size), lambda i, m: (m[0], i + first, 0, 0, 0)
    )
    other_block = pl.BlockSpec((step, 2, rows, size), lambda i, m: (i, 0, 0, 0))
    inverse_block = pl.BlockSpec((step, 2, size, 2 * size), lambda i, m: (i, 0, 0, 0))
    state, packed_arrived = [], []
    for chunk in range(chunks):
        scale = lax.dynamic_slice_in_dim(guess_scale, member * own + chunk * part, part, 0)
        offset = chunk * part // step
        state = call(
            newton_kernel,
            part // step,
            [pl.BlockSpec(memory_space=pltpu.SMEM), local_block(offset)]
            + [other_block] * 3
            + [pl.BlockSpec(memory_space=pl.ANY)] * len(state),
            [
                pl.BlockSpec(
                    (step, 2, size, 2 * size), lambda i, m, offset=offset: (i + offset, 0, 0, 0)
                ),
                pl.BlockSpec(
                    (step, 2, size, size), lambda i, m, offset=offset: (i + offset, 0, 0, 0)
                ),
            ],
            [
                jax.ShapeDtypeStruct((own, 2, size, 2 * size), BF16),
                jax.ShapeDtypeStruct((own, 2, size, size), BF16),
            ],
            [],
            part * 64 * 2 * 4 * size**3,
            part * 6 * 4 * size * size,
            {6 + index: index for index in range(len(state))},
        )(members, scale, factors, *arrived[chunk], *state)
        if chunk == 0:
            held = lax.optimization_barrier(tuple(pieces) + tuple(state))
            state = held[len(pieces) :]
            packed_arrived = [swap(piece, d) for piece, d in zip(held, distances)]
    inverse, psi = state

    other = pl.BlockSpec((step, rows, size), lambda i, m: (i, 0, 0))
    middle = call(
        middle_kernel,
        own // step,
        [inverse_block, pl.BlockSpec((1, step, rows, size), lambda i, m: (m[0], i, 0, 0))]
        + [other] * 3,
        pl.BlockSpec((size * own, size), lambda i, m: (0, 0)),
        jax.ShapeDtypeStruct((size * own, size), F32),
        [pltpu.VMEM((step, size, size), BF16)],
        own * 10 * 2 * 4 * size**3,
        own * 6 * 4 * size * size,
    )(members, inverse, packed, *packed_arrived)
    sent = middle.astype(jnp.float16)
    if lane_parts > 1:
        sent = sent.reshape(size, own, lane_parts, lanes).transpose(0, 2, 1, 3)
    sent = sent.reshape(devices, kept, own, lanes)
    values = lax.all_to_all(sent, chan + ("freq",), 0, 0, tiled=True).astype(F32)
    sources, own_rows = devices, own
    if own % 8:
        values = values.transpose(1, 0, 2, 3).reshape(1, kept, count, lanes)
        sources, own_rows = 1, count
    twice = math.gcd(kept, 2)
    table_block = pl.BlockSpec((count, count), lambda i: (0, 0))
    causal = pl.pallas_call(
        causal_kernel,
        grid=(kept // twice,),
        in_specs=[
            table_block,
            table_block,
            pl.BlockSpec((sources, twice, own_rows, lanes), lambda i: (0, i, 0, 0)),
        ],
        out_specs=[pl.BlockSpec((sources, twice, 2, own_rows, lanes), lambda i: (0, i, 0, 0, 0))],
        out_shape=[jax.ShapeDtypeStruct((sources, kept, 2, own_rows, lanes), F32)],
        scratch_shapes=[pltpu.VMEM((2 * count, count), BF16), pltpu.VMEM((2 * count, count), BF16)],
        compiler_params=params(24),
        cost_estimate=cost(kept * 12 * count * count * lanes, 12 * kept * count * lanes),
    )(table_re, table_im, values)[0].astype(jnp.float16)
    if own % 8:
        causal = causal.reshape(kept, 2, devices, own, lanes).transpose(2, 0, 1, 3, 4)
    back = lax.all_to_all(causal, chan + ("freq",), 0, 0, tiled=True).astype(F32)
    if lane_parts > 1:
        back = back.reshape(chan_size * column_parts, lane_parts, kept, 2, own, lanes)
        back = back.transpose(0, 2, 3, 4, 1, 5)
    back = back.reshape(size * 2 * own, size)
    result = pl.pallas_call(
        product_kernel,
        grid=(own // step,),
        in_specs=[
            pl.BlockSpec(back.shape, lambda i: (0, 0)),
            pl.BlockSpec((step, 2, size, size), lambda i: (i, 0, 0, 0)),
        ],
        out_specs=pl.BlockSpec((chan_size, step, 2, rows, size), lambda i: (0, i, 0, 0, 0)),
        out_shape=jax.ShapeDtypeStruct((chan_size, own, 2, rows, size), F32),
        compiler_params=params(16),
        cost_estimate=cost(own * 4 * 4 * size**3, own * 5 * 4 * size * size),
    )(back, psi)
    panels = [
        lax.dynamic_index_in_dim(result, member ^ d, 0, keepdims=False) for d in range(chan_size)
    ]
    panels[1:] = [swap(panels[d].astype(jnp.float16), d).astype(F32) for d in distances]
    owners = []
    for owner in range(chan_size):
        distance = member ^ owner
        low = jnp.where(distance % 2 == 0, panels[0], panels[1])
        high = jnp.where(distance % 2 == 0, panels[2], panels[3])
        owners.append(jnp.where(distance < 2, low, high))
    return jnp.swapaxes(cat(owners, 0) * SCALE, 2, 3)


def solution(mesh):
    freq_size, pairs = mesh.shape["freq"], mesh.shape["chan"] // 2
    split_mesh = jax.sharding.Mesh(
        mesh.devices.reshape(freq_size, 2, pairs), ("freq", "side", "pair")
    )
    in_specs = (
        P("freq", None, ("side", "pair"), None),
        P("freq", None, ("side", "pair"), None),
        P("freq"),
        P(),
    )
    out_specs = P("freq", None, None, ("side", "pair"))
    body = functools.partial(shards, freq_size, pairs)
    return jax.shard_map(
        body, mesh=split_mesh, in_specs=in_specs, out_specs=out_specs, check_vma=False
    )
```

```python
import functools
import math

import jax
import jax.numpy as jnp
from jax import lax
from jax.experimental import pallas as pl
from jax.experimental.pallas import tpu as pltpu
from jax.sharding import PartitionSpec as P

ITERS = 8
SCALE = 16.0
CHUNKS = 2
F32 = jnp.float32
BF16 = jnp.bfloat16
MIB = 1024 * 1024
NN = (((1,), (0,)), ((), ()))
NT = (((1,), (1,)), ((), ()))
TN = (((0,), (0,)), ((), ()))


def dot(left, right, dims=NN):
    return lax.dot_general(left, right, dims, preferred_element_type=F32)


def split(value):
    high = value.astype(BF16)
    return high, (value - high.astype(F32)).astype(BF16)


def cat(parts, axis):
    return jnp.concatenate(parts, axis=axis)


def dot3(left_high, left_low, right_high, right_low, dims=NN):
    rows = left_high.shape[0]
    both = dot(cat([left_high, left_low], 0), right_high, dims)
    return both[:rows] + (both[rows:] + dot(left_high, right_low, dims))


def eye(size):
    rows = lax.broadcasted_iota(jnp.int32, (size, size), 0)
    columns = lax.broadcasted_iota(jnp.int32, (size, size), 1)
    return jnp.where(rows == columns, 1.0, 0.0).astype(F32)


def place_rows(member, panels, out_ref):
    rows = panels[0].shape[-2]
    for index, panel in enumerate(panels):
        start = pl.multiple_of((member ^ index) * rows, rows)
        out_ref[..., pl.ds(start, rows), :] = panel[...]


def newton_kernel(member_ref, scale_ref, own_ref, one_ref, two_ref, three_ref, *refs):
    out_ref, psi_ref = refs[-2:]
    bins, _, size, _ = psi_ref.shape
    place_rows(member_ref[0], [own_ref.at[0], one_ref, two_ref, three_ref], psi_ref)
    identity = eye(size)
    state = []
    for item in range(bins):
        re, im = psi_ref[item, 0], psi_ref[item, 1]
        scale = scale_ref[pl.program_id(0) * bins + item]
        gram = dot(cat([re, im], 0), cat([cat([re, im], 1), cat([im, -re], 1)], 0), TN)
        sym = identity - scale * gram[:, :size]
        anti = -scale * gram[:, size:]
        state.append((sym, anti, None))
    for step in range(ITERS):
        after = []
        for sym, anti, total in state:
            left_high, left_low = split(cat([sym, anti], 1))
            if step == 0:
                total = identity + (sym + anti)
                right = cat([sym + anti, sym - anti], 0)
            elif step < ITERS - 1:
                right = cat([cat([sym + anti, total], 1), cat([sym - anti, total.T], 1)], 0)
            else:
                right = cat([total, total.T], 0)
            product = dot3(left_high, left_low, *split(right))
            if step > 0:
                total = total + product[:, -size:]
            if step < ITERS - 1:
                square = product[:, :size]
                square_t = square.T
                sym = 0.5 * (square + square_t)
                anti = 0.5 * (square - square_t)
            after.append((sym, anti, total))
        state = after
    for item in range(bins):
        total = state[item][2]
        total_t = total.T
        re, im = psi_ref[item, 0], psi_ref[item, 1]
        scale = scale_ref[pl.program_id(0) * bins + item]
        half = (0.5 * scale) * cat([total + total_t, total - total_t], 1)
        high, low = split(half)
        both = dot(cat([high, low], 0), cat([cat([re, im], 1), cat([-im, re], 1)], 0), NT)
        high, low = split(both[:size] + both[size:])
        out_ref[item, 0] = high
        out_ref[item, 1] = low


def middle_kernel(member_ref, inverse_ref, own_ref, one_ref, two_ref, three_ref, out_ref, packed_ref):
    bins, size = inverse_ref.shape[0], inverse_ref.shape[2]
    total_bins = pl.num_programs(0) * bins
    place_rows(member_ref[0], [own_ref.at[0], one_ref, two_ref, three_ref], packed_ref)
    identity = eye(size)
    rows = lax.broadcasted_iota(jnp.int32, (size, size), 0)
    columns = lax.broadcasted_iota(jnp.int32, (size, size), 1)

    def swapped(value):
        return cat([value, cat([value[:, size:], -value[:, :size]], 1)], 0)

    for item in range(bins):
        packed = packed_ref[item].astype(F32)
        packed_t = packed.T
        re = jnp.where(columns >= rows, packed, packed_t).astype(BF16)
        im = jnp.where(columns == rows, 0.0, jnp.where(columns < rows, packed, -packed_t)).astype(BF16)
        high, low = inverse_ref[item, 0], inverse_ref[item, 1]
        both = dot(cat([high, low], 0), cat([cat([re, im], 1), cat([-im, re], 1)], 0))
        left_high, left_low = split(both[:size] + both[size:])
        middle = dot3(left_high, left_low, swapped(high), swapped(low), NT)
        middle = middle[:, :size] - middle[:, size:]
        place = pl.program_id(0) * bins + item
        out_ref[pl.ds(place, size, stride=total_bins), :] = (middle + identity) * (1.0 / SCALE)


def causal_kernel(real_ref, imag_ref, values_ref, *refs):
    *out_refs, table_high, table_low = refs
    count = real_ref.shape[1]
    sources, kept, own, lanes = values_ref.shape

    @pl.when(pl.program_id(0) == 0)
    def _():
        for part, table_ref in enumerate((real_ref, imag_ref)):
            high, low = split(table_ref[...])
            table_high[part * count : (part + 1) * count] = high
            table_low[part * count : (part + 1) * count] = low

    values = cat([values_ref[:, item].reshape(count, lanes) for item in range(kept)], 1)
    high, low = split(values)
    whole = dot(table_high[...], high) + (dot(table_high[...], low) + dot(table_low[...], high))
    for item in range(kept):
        for part in range(2):
            piece = whole[part * count : (part + 1) * count, item * lanes : (item + 1) * lanes]
            piece = piece.reshape(sources, own, lanes)
            step = own // len(out_refs)
            for chunk, out_ref in enumerate(out_refs):
                out_ref[:, item, part] = piece[:, chunk * step : (chunk + 1) * step]


def product_kernel(member_ref, causal_ref, psi_ref, out_ref):
    bins, _, size, _ = psi_ref.shape
    total_bins = causal_ref.shape[0] // (2 * size)
    rows = out_ref.shape[3]
    for item in range(bins):
        re, im = psi_ref[item, 0], psi_ref[item, 1]
        place = pl.program_id(0) * bins + item
        part_re = causal_ref[pl.ds(place, size, stride=2 * total_bins), :]
        part_im = causal_ref[pl.ds(total_bins + place, size, stride=2 * total_bins), :]
        added, taken = part_re + part_im, part_re - part_im
        high, low = split(0.5 * cat([taken.T + added, added.T - taken], 1))
        both = dot(cat([high, low], 0), cat([cat([re, -im], 1), cat([im, re], 1)], 0), NT)
        result = both[:size] + both[size:]
        for panel in range(out_ref.shape[0]):
            piece = result[panel * rows : (panel + 1) * rows]
            out_ref[member_ref[0] ^ panel, item, 0] = piece[:, :size]
            out_ref[member_ref[0] ^ panel, item, 1] = piece[:, size:]


def projection_table(lag_limit, count, freq_size, pairs):
    own = count // (freq_size * 2 * pairs)

    def bins(index):
        return index // own % freq_size * (own * 2 * pairs) + index // (own * freq_size) * own + index % own

    row = lax.broadcasted_iota(jnp.int32, (count, 1), 0)
    column = lax.broadcasted_iota(jnp.int32, (1, count), 1)
    shift = bins(column) - bins(row)
    unit = math.pi / count
    half_angle = shift.astype(F32) * unit
    turned = ((2 * lag_limit + 1) * shift) % (2 * count)
    turned = jnp.where(turned >= count, turned - 2 * count, turned)
    last_angle = turned.astype(F32) * unit
    below = jnp.where(shift == 0, 1.0, 2.0 * count * jnp.sin(half_angle))
    real = jnp.where(shift == 0, (lag_limit.astype(F32) + 0.5) / count, jnp.sin(last_angle) / below)
    imag = jnp.where(shift == 0, 0.0, (jnp.cos(half_angle) - jnp.cos(last_angle)) / below)
    return real, imag


def params(limit):
    return pltpu.CompilerParams(vmem_limit_bytes=limit * MIB)


def cost(flops, moved):
    return pl.CostEstimate(flops=flops, bytes_accessed=moved, transcendentals=0)


def after(value, *earlier):
    return lax.optimization_barrier((value,) + earlier)[0]


SWAP = ((0, 1), (1, 0))
FLIP = ((0, 3), (1, 2), (2, 1), (3, 0))


def swap(value, distance):
    if distance == 1:
        return lax.ppermute(value, "pair", SWAP)
    if distance == 2:
        return lax.ppermute(value, "side", SWAP)
    return lax.ppermute(value, ("side", "pair"), FLIP)


def call(kernel, steps, in_specs, out_specs, out_shape, scratch, flops, moved, aliases={}):
    return pl.pallas_call(
        kernel,
        grid_spec=pltpu.PrefetchScalarGridSpec(
            num_scalar_prefetch=1,
            grid=(steps,),
            in_specs=in_specs,
            out_specs=out_specs,
            scratch_shapes=scratch,
        ),
        out_shape=out_shape,
        input_output_aliases=aliases,
        compiler_params=params(16),
        cost_estimate=cost(flops, moved),
    )


def shards(freq_size, pairs, factor, spectrum, guess_scale, lag_cutoff):
    chan = ("side", "pair")
    chan_size = 2 * pairs
    group_bins, _, rows, size = factor.shape
    own = group_bins // chan_size
    count = group_bins * freq_size
    chunks = CHUNKS if own % (4 * CHUNKS) == 0 else 1
    part = own // chunks
    step = math.gcd(part, 4)
    column_parts = min(freq_size, rows)
    lane_parts = freq_size // column_parts
    kept = rows // column_parts
    lanes = size // lane_parts
    side, pair = lax.axis_index("side"), lax.axis_index("pair")
    member = side * pairs + pair
    members = member.reshape(1)
    devices = chan_size * freq_size
    distances = range(1, chan_size)

    factors = factor.reshape(chan_size, own, 2, rows, size)

    def rows_for(owner, first, length):
        return lax.dynamic_slice(
            factors, (owner, first, 0, 0, 0), (1, length, 2, rows, size)
        ).reshape(length, 2, rows, size)

    arrived = []
    for chunk in range(chunks):
        pieces = [rows_for(member ^ d, chunk * part, part) for d in distances]
        arrived.append([swap(piece, d) for piece, d in zip(pieces, distances)])
    row_index = lax.broadcasted_iota(jnp.int32, (rows, size), 0) + member * rows
    column_index = lax.broadcasted_iota(jnp.int32, (rows, size), 1)
    packed = jnp.where(column_index >= row_index, spectrum[:, 0], spectrum[:, 1])
    packed = packed.reshape(chan_size, own, rows, size)
    pieces = [lax.dynamic_index_in_dim(packed, member ^ d, 0, keepdims=False) for d in distances]
    table_re, table_im = projection_table(lag_cutoff[0], count, freq_size, pairs)

    local_block = lambda first: pl.BlockSpec(
        (1, step, 2, rows, size), lambda i, m: (m[0], i + first, 0, 0, 0)
    )
    other_block = pl.BlockSpec((step, 2, rows, size), lambda i, m: (i, 0, 0, 0))
    inverse_block = pl.BlockSpec((step, 2, size, 2 * size), lambda i, m: (i, 0, 0, 0))
    state, packed_arrived = [], []
    for chunk in range(chunks):
        scale = lax.dynamic_slice_in_dim(guess_scale, member * own + chunk * part, part, 0)
        offset = chunk * part // step
        state = call(
            newton_kernel,
            part // step,
            [pl.BlockSpec(memory_space=pltpu.SMEM), local_block(offset)]
            + [other_block] * 3
            + [pl.BlockSpec(memory_space=pl.ANY)] * len(state),
            [
                pl.BlockSpec(
                    (step, 2, size, 2 * size), lambda i, m, offset=offset: (i + offset, 0, 0, 0)
                ),
                pl.BlockSpec(
                    (step, 2, size, size), lambda i, m, offset=offset: (i + offset, 0, 0, 0)
                ),
            ],
            [
                jax.ShapeDtypeStruct((own, 2, size, 2 * size), BF16),
                jax.ShapeDtypeStruct((own, 2, size, size), BF16),
            ],
            [],
            part * 64 * 2 * 4 * size**3,
            part * 6 * 4 * size * size,
            {6 + index: index for index in range(len(state))},
        )(members, scale, factors, *arrived[chunk], *state)
        if chunk == 0:
            held = lax.optimization_barrier(tuple(pieces) + tuple(state))
            state = held[len(pieces) :]
            packed_arrived = [swap(piece, d) for piece, d in zip(held, distances)]
    inverse, psi = state

    other = pl.BlockSpec((step, rows, size), lambda i, m: (i, 0, 0))
    middle = call(
        middle_kernel,
        own // step,
        [inverse_block, pl.BlockSpec((1, step, rows, size), lambda i, m: (m[0], i, 0, 0))]
        + [other] * 3,
        pl.BlockSpec((size * own, size), lambda i, m: (0, 0)),
        jax.ShapeDtypeStruct((size * own, size), F32),
        [pltpu.VMEM((step, size, size), BF16)],
        own * 10 * 2 * 4 * size**3,
        own * 6 * 4 * size * size,
    )(members, inverse, packed, *packed_arrived)
    sent = middle.astype(jnp.float16)
    if lane_parts > 1:
        sent = sent.reshape(size, own, lane_parts, lanes).transpose(0, 2, 1, 3)
    sent = sent.reshape(devices, kept, own, lanes)
    values = lax.all_to_all(sent, chan + ("freq",), 0, 0, tiled=True).astype(F32)
    sources, own_rows = devices, own
    if own % 8:
        values = values.transpose(1, 0, 2, 3).reshape(1, kept, count, lanes)
        sources, own_rows = 1, count
    twice = math.gcd(kept, 2)
    table_block = pl.BlockSpec((count, count), lambda i: (0, 0))
    causal = pl.pallas_call(
        causal_kernel,
        grid=(kept // twice,),
        in_specs=[
            table_block,
            table_block,
            pl.BlockSpec((sources, twice, own_rows, lanes), lambda i: (0, i, 0, 0)),
        ],
        out_specs=[pl.BlockSpec((sources, twice, 2, own_rows, lanes), lambda i: (0, i, 0, 0, 0))],
        out_shape=[jax.ShapeDtypeStruct((sources, kept, 2, own_rows, lanes), F32)],
        scratch_shapes=[pltpu.VMEM((2 * count, count), BF16), pltpu.VMEM((2 * count, count), BF16)],
        compiler_params=params(24),
        cost_estimate=cost(kept * 12 * count * count * lanes, 12 * kept * count * lanes),
    )(table_re, table_im, values)[0].astype(jnp.float16)
    if own % 8:
        causal = causal.reshape(kept, 2, devices, own, lanes).transpose(2, 0, 1, 3, 4)
    back = lax.all_to_all(causal, chan + ("freq",), 0, 0, tiled=True).astype(F32)
    if lane_parts > 1:
        back = back.reshape(chan_size * column_parts, lane_parts, kept, 2, own, lanes)
        back = back.transpose(0, 2, 3, 4, 1, 5)
    back = back.reshape(size * 2 * own, size)
    result = call(
        product_kernel,
        own // step,
        [
            pl.BlockSpec(back.shape, lambda i, m: (0, 0)),
            pl.BlockSpec((step, 2, size, size), lambda i, m: (i, 0, 0, 0)),
        ],
        pl.BlockSpec((chan_size, step, 2, rows, size), lambda i, m: (0, i, 0, 0, 0)),
        jax.ShapeDtypeStruct((chan_size, own, 2, rows, size), F32),
        [],
        own * 4 * 4 * size**3,
        own * 5 * 4 * size * size,
    )(members, back, psi)
    panels = [result[0]]
    panels += [swap(result[d].astype(jnp.float16), d).astype(F32) for d in distances]
    owners = []
    for owner in range(chan_size):
        distance = member ^ owner
        low = jnp.where(distance % 2 == 0, panels[0], panels[1])
        high = jnp.where(distance % 2 == 0, panels[2], panels[3])
        owners.append(jnp.where(distance < 2, low, high))
    return jnp.swapaxes(cat(owners, 0) * SCALE, 2, 3)


def solution(mesh):
    freq_size, pairs = mesh.shape["freq"], mesh.shape["chan"] // 2
    split_mesh = jax.sharding.Mesh(
        mesh.devices.reshape(freq_size, 2, pairs), ("freq", "side", "pair")
    )
    in_specs = (
        P("freq", None, ("side", "pair"), None),
        P("freq", None, ("side", "pair"), None),
        P("freq"),
        P(),
    )
    out_specs = P("freq", None, None, ("side", "pair"))
    body = functools.partial(shards, freq_size, pairs)
    return jax.shard_map(
        body, mesh=split_mesh, in_specs=in_specs, out_specs=out_specs, check_vma=False
    )
```

```python
import functools
import math

import jax
import jax.numpy as jnp
from jax import lax
from jax.experimental import pallas as pl
from jax.experimental.pallas import tpu as pltpu
from jax.sharding import PartitionSpec as P

ITERS = 8
SCALE = 16.0
CHUNKS = 2
F32 = jnp.float32
BF16 = jnp.bfloat16
MIB = 1024 * 1024
NN = (((1,), (0,)), ((), ()))
NT = (((1,), (1,)), ((), ()))
TN = (((0,), (0,)), ((), ()))


def dot(left, right, dims=NN):
    return lax.dot_general(left, right, dims, preferred_element_type=F32)


def split(value):
    high = value.astype(BF16)
    return high, (value - high.astype(F32)).astype(BF16)


def cat(parts, axis):
    return jnp.concatenate(parts, axis=axis)


def dot3(left_high, left_low, right_high, right_low, dims=NN):
    rows = left_high.shape[0]
    both = dot(cat([left_high, left_low], 0), right_high, dims)
    return both[:rows] + (both[rows:] + dot(left_high, right_low, dims))


def eye(size):
    rows = lax.broadcasted_iota(jnp.int32, (size, size), 0)
    columns = lax.broadcasted_iota(jnp.int32, (size, size), 1)
    return jnp.where(rows == columns, 1.0, 0.0).astype(F32)


def place_rows(member, panels, out_ref):
    rows = panels[0].shape[-2]
    for index, panel in enumerate(panels):
        start = pl.multiple_of((member ^ index) * rows, rows)
        out_ref[..., pl.ds(start, rows), :] = panel[...]


def newton_kernel(member_ref, scale_ref, own_ref, one_ref, two_ref, three_ref, *refs):
    out_ref, psi_ref = refs[-2:]
    bins, _, size, _ = psi_ref.shape
    place_rows(member_ref[0], [own_ref.at[0], one_ref, two_ref, three_ref], psi_ref)
    identity = eye(size)
    state = []
    for item in range(bins):
        re, im = psi_ref[item, 0], psi_ref[item, 1]
        scale = scale_ref[pl.program_id(0) * bins + item]
        gram = dot(cat([re, im], 0), cat([cat([re, im], 1), cat([im, -re], 1)], 0), TN)
        sym = identity - scale * gram[:, :size]
        anti = -scale * gram[:, size:]
        state.append((sym, anti, None))
    for step in range(ITERS):
        after = []
        for sym, anti, total in state:
            left_high, left_low = split(cat([sym, anti], 1))
            if step == 0:
                total = identity + (sym + anti)
                right = cat([sym + anti, sym - anti], 0)
            elif step < ITERS - 1:
                right = cat([cat([sym + anti, total], 1), cat([sym - anti, total.T], 1)], 0)
            else:
                right = cat([total, total.T], 0)
            product = dot3(left_high, left_low, *split(right))
            if step > 0:
                total = total + product[:, -size:]
            if step < ITERS - 1:
                square = product[:, :size]
                square_t = square.T
                sym = 0.5 * (square + square_t)
                anti = 0.5 * (square - square_t)
            after.append((sym, anti, total))
        state = after
    for item in range(bins):
        total = state[item][2]
        total_t = total.T
        re, im = psi_ref[item, 0], psi_ref[item, 1]
        scale = scale_ref[pl.program_id(0) * bins + item]
        half = (0.5 * scale) * cat([total + total_t, total - total_t], 1)
        high, low = split(half)
        both = dot(cat([high, low], 0), cat([cat([re, im], 1), cat([-im, re], 1)], 0), NT)
        high, low = split(both[:size] + both[size:])
        out_ref[item, 0] = high
        out_ref[item, 1] = low


def middle_kernel(member_ref, inverse_ref, own_ref, one_ref, two_ref, three_ref, out_ref, packed_ref):
    bins, size = inverse_ref.shape[0], inverse_ref.shape[2]
    total_bins = pl.num_programs(0) * bins
    place_rows(member_ref[0], [own_ref.at[0], one_ref, two_ref, three_ref], packed_ref)
    identity = eye(size)
    rows = lax.broadcasted_iota(jnp.int32, (size, size), 0)
    columns = lax.broadcasted_iota(jnp.int32, (size, size), 1)

    def swapped(value):
        return cat([value, cat([value[:, size:], -value[:, :size]], 1)], 0)

    for item in range(bins):
        packed = packed_ref[item].astype(F32)
        packed_t = packed.T
        re = jnp.where(columns >= rows, packed, packed_t).astype(BF16)
        im = jnp.where(columns == rows, 0.0, jnp.where(columns < rows, packed, -packed_t)).astype(BF16)
        high, low = inverse_ref[item, 0], inverse_ref[item, 1]
        both = dot(cat([high, low], 0), cat([cat([re, im], 1), cat([-im, re], 1)], 0))
        left_high, left_low = split(both[:size] + both[size:])
        middle = dot3(left_high, left_low, swapped(high), swapped(low), NT)
        middle = middle[:, :size] - middle[:, size:]
        place = pl.program_id(0) * bins + item
        out_ref[pl.ds(place, size, stride=total_bins), :] = (middle + identity) * (1.0 / SCALE)


def causal_kernel(real_ref, imag_ref, values_ref, *refs):
    *out_refs, table_high, table_low = refs
    count = real_ref.shape[1]
    sources, kept, own, lanes = values_ref.shape

    @pl.when(pl.program_id(0) == 0)
    def _():
        for part, table_ref in enumerate((real_ref, imag_ref)):
            high, low = split(table_ref[...])
            table_high[part * count : (part + 1) * count] = high
            table_low[part * count : (part + 1) * count] = low

    values = cat([values_ref[:, item].reshape(count, lanes) for item in range(kept)], 1)
    high, low = split(values)
    whole = dot(table_high[...], high) + (dot(table_high[...], low) + dot(table_low[...], high))
    for item in range(kept):
        for part in range(2):
            piece = whole[part * count : (part + 1) * count, item * lanes : (item + 1) * lanes]
            piece = piece.reshape(sources, own, lanes)
            step = own // len(out_refs)
            for chunk, out_ref in enumerate(out_refs):
                out_ref[:, item, part] = piece[:, chunk * step : (chunk + 1) * step]


def product_kernel(member_ref, causal_ref, psi_ref, out_ref):
    bins, _, size, _ = psi_ref.shape
    total_bins = causal_ref.shape[0] // (2 * size)
    rows = out_ref.shape[3]
    for item in range(bins):
        re, im = psi_ref[item, 0], psi_ref[item, 1]
        place = pl.program_id(0) * bins + item
        part_re = causal_ref[pl.ds(place, size, stride=2 * total_bins), :]
        part_im = causal_ref[pl.ds(total_bins + place, size, stride=2 * total_bins), :]
        added, taken = part_re + part_im, part_re - part_im
        high, low = split(0.5 * cat([taken.T + added, added.T - taken], 1))
        both = dot(cat([high, low], 0), cat([cat([re, -im], 1), cat([im, re], 1)], 0), NT)
        result = both[:size] + both[size:]
        for panel in range(out_ref.shape[0]):
            piece = result[panel * rows : (panel + 1) * rows]
            out_ref[member_ref[0] ^ panel, item, 0] = piece[:, :size]
            out_ref[member_ref[0] ^ panel, item, 1] = piece[:, size:]


def projection_table(lag_limit, count, freq_size, pairs):
    own = count // (freq_size * 2 * pairs)

    def bins(index):
        return index // own % freq_size * (own * 2 * pairs) + index // (own * freq_size) * own + index % own

    row = lax.broadcasted_iota(jnp.int32, (count, 1), 0)
    column = lax.broadcasted_iota(jnp.int32, (1, count), 1)
    shift = bins(column) - bins(row)
    unit = math.pi / count
    half_angle = shift.astype(F32) * unit
    turned = ((2 * lag_limit + 1) * shift) % (2 * count)
    turned = jnp.where(turned >= count, turned - 2 * count, turned)
    last_angle = turned.astype(F32) * unit
    below = jnp.where(shift == 0, 1.0, 2.0 * count * jnp.sin(half_angle))
    real = jnp.where(shift == 0, (lag_limit.astype(F32) + 0.5) / count, jnp.sin(last_angle) / below)
    imag = jnp.where(shift == 0, 0.0, (jnp.cos(half_angle) - jnp.cos(last_angle)) / below)
    return real, imag


def params(limit):
    return pltpu.CompilerParams(vmem_limit_bytes=limit * MIB)


def cost(flops, moved):
    return pl.CostEstimate(flops=flops, bytes_accessed=moved, transcendentals=0)


def after(value, *earlier):
    return lax.optimization_barrier((value,) + earlier)[0]


SWAP = ((0, 1), (1, 0))
FLIP = ((0, 3), (1, 2), (2, 1), (3, 0))


def swap(value, distance):
    if distance == 1:
        return lax.ppermute(value, "pair", SWAP)
    if distance == 2:
        return lax.ppermute(value, "side", SWAP)
    return lax.ppermute(value, ("side", "pair"), FLIP)


def call(kernel, steps, in_specs, out_specs, out_shape, scratch, flops, moved, aliases={}):
    return pl.pallas_call(
        kernel,
        grid_spec=pltpu.PrefetchScalarGridSpec(
            num_scalar_prefetch=1,
            grid=(steps,),
            in_specs=in_specs,
            out_specs=out_specs,
            scratch_shapes=scratch,
        ),
        out_shape=out_shape,
        input_output_aliases=aliases,
        compiler_params=params(16),
        cost_estimate=cost(flops, moved),
    )


def shards(freq_size, pairs, factor, spectrum, guess_scale, lag_cutoff):
    chan = ("side", "pair")
    chan_size = 2 * pairs
    group_bins, _, rows, size = factor.shape
    own = group_bins // chan_size
    count = group_bins * freq_size
    chunks = CHUNKS if own % (4 * CHUNKS) == 0 else 1
    part = own // chunks
    step = math.gcd(part, 4)
    column_parts = min(freq_size, rows)
    lane_parts = freq_size // column_parts
    kept = rows // column_parts
    lanes = size // lane_parts
    side, pair = lax.axis_index("side"), lax.axis_index("pair")
    member = side * pairs + pair
    members = member.reshape(1)
    devices = chan_size * freq_size
    distances = range(1, chan_size)

    factors = factor.reshape(chan_size, own, 2, rows, size)

    def rows_for(owner, first, length):
        return lax.dynamic_slice(
            factors, (owner, first, 0, 0, 0), (1, length, 2, rows, size)
        ).reshape(length, 2, rows, size)

    arrived = []
    for chunk in range(chunks):
        pieces = [rows_for(member ^ d, chunk * part, part) for d in distances]
        if arrived:
            pieces = lax.optimization_barrier((*pieces, *arrived[-1]))[: len(pieces)]
        arrived.append([swap(piece, d) for piece, d in zip(pieces, distances)])
    row_index = lax.broadcasted_iota(jnp.int32, (rows, size), 0) + member * rows
    column_index = lax.broadcasted_iota(jnp.int32, (rows, size), 1)
    packed = jnp.where(column_index >= row_index, spectrum[:, 0], spectrum[:, 1])
    packed = packed.reshape(chan_size, own, rows, size)
    pieces = [lax.dynamic_index_in_dim(packed, member ^ d, 0, keepdims=False) for d in distances]
    table_re, table_im = projection_table(lag_cutoff[0], count, freq_size, pairs)

    local_block = lambda first: pl.BlockSpec(
        (1, step, 2, rows, size), lambda i, m: (m[0], i + first, 0, 0, 0)
    )
    other_block = pl.BlockSpec((step, 2, rows, size), lambda i, m: (i, 0, 0, 0))
    inverse_block = pl.BlockSpec((step, 2, size, 2 * size), lambda i, m: (i, 0, 0, 0))
    state, packed_arrived = [], []
    for chunk in range(chunks):
        scale = lax.dynamic_slice_in_dim(guess_scale, member * own + chunk * part, part, 0)
        offset = chunk * part // step
        state = call(
            newton_kernel,
            part // step,
            [pl.BlockSpec(memory_space=pltpu.SMEM), local_block(offset)]
            + [other_block] * 3
            + [pl.BlockSpec(memory_space=pl.ANY)] * len(state),
            [
                pl.BlockSpec(
                    (step, 2, size, 2 * size), lambda i, m, offset=offset: (i + offset, 0, 0, 0)
                ),
                pl.BlockSpec(
                    (step, 2, size, size), lambda i, m, offset=offset: (i + offset, 0, 0, 0)
                ),
            ],
            [
                jax.ShapeDtypeStruct((own, 2, size, 2 * size), BF16),
                jax.ShapeDtypeStruct((own, 2, size, size), BF16),
            ],
            [],
            part * 64 * 2 * 4 * size**3,
            part * 6 * 4 * size * size,
            {6 + index: index for index in range(len(state))},
        )(members, scale, factors, *arrived[chunk], *state)
        if chunk == 0:
            held = lax.optimization_barrier(tuple(pieces) + tuple(state))
            state = held[len(pieces) :]
            packed_arrived = [swap(piece, d) for piece, d in zip(held, distances)]
    inverse, psi = state

    other = pl.BlockSpec((step, rows, size), lambda i, m: (i, 0, 0))
    middle = call(
        middle_kernel,
        own // step,
        [inverse_block, pl.BlockSpec((1, step, rows, size), lambda i, m: (m[0], i, 0, 0))]
        + [other] * 3,
        pl.BlockSpec((size * own, size), lambda i, m: (0, 0)),
        jax.ShapeDtypeStruct((size * own, size), F32),
        [pltpu.VMEM((step, size, size), BF16)],
        own * 10 * 2 * 4 * size**3,
        own * 6 * 4 * size * size,
    )(members, inverse, packed, *packed_arrived)
    sent = middle.astype(jnp.float16)
    if lane_parts > 1:
        sent = sent.reshape(size, own, lane_parts, lanes).transpose(0, 2, 1, 3)
    sent = sent.reshape(devices, kept, own, lanes)
    values = lax.all_to_all(sent, chan + ("freq",), 0, 0, tiled=True).astype(F32)
    sources, own_rows = devices, own
    if own % 8:
        values = values.transpose(1, 0, 2, 3).reshape(1, kept, count, lanes)
        sources, own_rows = 1, count
    twice = math.gcd(kept, 2)
    table_block = pl.BlockSpec((count, count), lambda i: (0, 0))
    causal = pl.pallas_call(
        causal_kernel,
        grid=(kept // twice,),
        in_specs=[
            table_block,
            table_block,
            pl.BlockSpec((sources, twice, own_rows, lanes), lambda i: (0, i, 0, 0)),
        ],
        out_specs=[pl.BlockSpec((sources, twice, 2, own_rows, lanes), lambda i: (0, i, 0, 0, 0))],
        out_shape=[jax.ShapeDtypeStruct((sources, kept, 2, own_rows, lanes), F32)],
        scratch_shapes=[pltpu.VMEM((2 * count, count), BF16), pltpu.VMEM((2 * count, count), BF16)],
        compiler_params=params(24),
        cost_estimate=cost(kept * 12 * count * count * lanes, 12 * kept * count * lanes),
    )(table_re, table_im, values)[0].astype(jnp.float16)
    if own % 8:
        causal = causal.reshape(kept, 2, devices, own, lanes).transpose(2, 0, 1, 3, 4)
    back = lax.all_to_all(causal, chan + ("freq",), 0, 0, tiled=True).astype(F32)
    if lane_parts > 1:
        back = back.reshape(chan_size * column_parts, lane_parts, kept, 2, own, lanes)
        back = back.transpose(0, 2, 3, 4, 1, 5)
    back = back.reshape(size * 2 * own, size)
    result = call(
        product_kernel,
        own // step,
        [
            pl.BlockSpec(back.shape, lambda i, m: (0, 0)),
            pl.BlockSpec((step, 2, size, size), lambda i, m: (i, 0, 0, 0)),
        ],
        pl.BlockSpec((chan_size, step, 2, rows, size), lambda i, m: (0, i, 0, 0, 0)),
        jax.ShapeDtypeStruct((chan_size, own, 2, rows, size), F32),
        [],
        own * 4 * 4 * size**3,
        own * 5 * 4 * size * size,
    )(members, back, psi)
    panels = [lax.optimization_barrier(result[0])]
    panels += [swap(result[d].astype(jnp.float16), d).astype(F32) for d in distances]
    owners = []
    for owner in range(chan_size):
        distance = member ^ owner
        low = jnp.where(distance % 2 == 0, panels[0], panels[1])
        high = jnp.where(distance % 2 == 0, panels[2], panels[3])
        owners.append(jnp.where(distance < 2, low, high))
    return jnp.swapaxes(cat(owners, 0) * SCALE, 2, 3)


def solution(mesh):
    freq_size, pairs = mesh.shape["freq"], mesh.shape["chan"] // 2
    split_mesh = jax.sharding.Mesh(
        mesh.devices.reshape(freq_size, 2, pairs), ("freq", "side", "pair")
    )
    in_specs = (
        P("freq", None, ("side", "pair"), None),
        P("freq", None, ("side", "pair"), None),
        P("freq"),
        P(),
    )
    out_specs = P("freq", None, None, ("side", "pair"))
    body = functools.partial(shards, freq_size, pairs)
    return jax.shard_map(
        body, mesh=split_mesh, in_specs=in_specs, out_specs=out_specs, check_vma=False
    )
```

```python
import functools
import math

import jax
import jax.numpy as jnp
from jax import lax
from jax.experimental import pallas as pl
from jax.experimental.pallas import tpu as pltpu
from jax.sharding import PartitionSpec as P

ITERS = 8
SCALE = 16.0
CHUNKS = 2
F32 = jnp.float32
BF16 = jnp.bfloat16
MIB = 1024 * 1024
NN = (((1,), (0,)), ((), ()))
NT = (((1,), (1,)), ((), ()))
TN = (((0,), (0,)), ((), ()))


def dot(left, right, dims=NN):
    return lax.dot_general(left, right, dims, preferred_element_type=F32)


def split(value):
    high = value.astype(BF16)
    return high, (value - high.astype(F32)).astype(BF16)


def cat(parts, axis):
    return jnp.concatenate(parts, axis=axis)


def dot3(left_high, left_low, right_high, right_low, dims=NN):
    rows = left_high.shape[0]
    both = dot(cat([left_high, left_low], 0), right_high, dims)
    return both[:rows] + (both[rows:] + dot(left_high, right_low, dims))


def eye(size):
    rows = lax.broadcasted_iota(jnp.int32, (size, size), 0)
    columns = lax.broadcasted_iota(jnp.int32, (size, size), 1)
    return jnp.where(rows == columns, 1.0, 0.0).astype(F32)


def place_rows(member, panels, out_ref):
    rows = panels[0].shape[-2]
    for index, panel in enumerate(panels):
        start = pl.multiple_of((member ^ index) * rows, rows)
        out_ref[..., pl.ds(start, rows), :] = panel[...]


def newton_kernel(member_ref, scale_ref, own_ref, one_ref, two_ref, three_ref, *refs):
    out_ref, psi_ref = refs[-2:]
    bins, _, size, _ = psi_ref.shape
    place_rows(member_ref[0], [own_ref.at[0], one_ref, two_ref, three_ref], psi_ref)
    identity = eye(size)
    state = []
    for item in range(bins):
        re, im = psi_ref[item, 0], psi_ref[item, 1]
        scale = scale_ref[pl.program_id(0) * bins + item]
        gram = dot(cat([re, im], 0), cat([cat([re, im], 1), cat([im, -re], 1)], 0), TN)
        sym = identity - scale * gram[:, :size]
        anti = -scale * gram[:, size:]
        state.append((sym, anti, None))
    for step in range(ITERS):
        after = []
        for sym, anti, total in state:
            left_high, left_low = split(cat([sym, anti], 1))
            if step == 0:
                total = identity + (sym + anti)
                right = cat([sym + anti, sym - anti], 0)
            elif step < ITERS - 1:
                right = cat([cat([sym + anti, total], 1), cat([sym - anti, total.T], 1)], 0)
            else:
                right = cat([total, total.T], 0)
            product = dot3(left_high, left_low, *split(right))
            if step > 0:
                total = total + product[:, -size:]
            if step < ITERS - 1:
                square = product[:, :size]
                square_t = square.T
                sym = 0.5 * (square + square_t)
                anti = 0.5 * (square - square_t)
            after.append((sym, anti, total))
        state = after
    for item in range(bins):
        total = state[item][2]
        total_t = total.T
        re, im = psi_ref[item, 0], psi_ref[item, 1]
        scale = scale_ref[pl.program_id(0) * bins + item]
        half = (0.5 * scale) * cat([total + total_t, total - total_t], 1)
        high, low = split(half)
        both = dot(cat([high, low], 0), cat([cat([re, im], 1), cat([-im, re], 1)], 0), NT)
        high, low = split(both[:size] + both[size:])
        out_ref[item, 0] = high
        out_ref[item, 1] = low


def middle_kernel(member_ref, inverse_ref, own_ref, one_ref, two_ref, three_ref, out_ref, packed_ref):
    bins, size = inverse_ref.shape[0], inverse_ref.shape[2]
    total_bins = pl.num_programs(0) * bins
    place_rows(member_ref[0], [own_ref.at[0], one_ref, two_ref, three_ref], packed_ref)
    identity = eye(size)
    rows = lax.broadcasted_iota(jnp.int32, (size, size), 0)
    columns = lax.broadcasted_iota(jnp.int32, (size, size), 1)

    def swapped(value):
        return cat([value, cat([value[:, size:], -value[:, :size]], 1)], 0)

    for item in range(bins):
        packed = packed_ref[item].astype(F32)
        packed_t = packed.T
        re = jnp.where(columns >= rows, packed, packed_t).astype(BF16)
        im = jnp.where(columns == rows, 0.0, jnp.where(columns < rows, packed, -packed_t)).astype(BF16)
        high, low = inverse_ref[item, 0], inverse_ref[item, 1]
        both = dot(cat([high, low], 0), cat([cat([re, im], 1), cat([-im, re], 1)], 0))
        left_high, left_low = split(both[:size] + both[size:])
        middle = dot3(left_high, left_low, swapped(high), swapped(low), NT)
        middle = middle[:, :size] - middle[:, size:]
        place = pl.program_id(0) * bins + item
        out_ref[pl.ds(place, size, stride=total_bins), :] = (middle + identity) * (1.0 / SCALE)


def causal_kernel(real_ref, imag_ref, values_ref, *refs):
    *out_refs, table_high, table_low = refs
    count = real_ref.shape[1]
    sources, kept, own, lanes = values_ref.shape

    @pl.when(pl.program_id(0) == 0)
    def _():
        for part, table_ref in enumerate((real_ref, imag_ref)):
            high, low = split(table_ref[...])
            table_high[part * count : (part + 1) * count] = high
            table_low[part * count : (part + 1) * count] = low

    values = cat([values_ref[:, item].reshape(count, lanes) for item in range(kept)], 1)
    high, low = split(values)
    whole = dot(table_high[...], high) + (dot(table_high[...], low) + dot(table_low[...], high))
    for item in range(kept):
        for part in range(2):
            piece = whole[part * count : (part + 1) * count, item * lanes : (item + 1) * lanes]
            piece = piece.reshape(sources, own, lanes)
            step = own // len(out_refs)
            for chunk, out_ref in enumerate(out_refs):
                out_ref[:, item, part] = piece[:, chunk * step : (chunk + 1) * step]


def product_kernel(member_ref, causal_ref, psi_ref, out_ref):
    bins, _, size, _ = psi_ref.shape
    total_bins = causal_ref.shape[0] // (2 * size)
    rows = out_ref.shape[3]
    for item in range(bins):
        re, im = psi_ref[item, 0], psi_ref[item, 1]
        place = pl.program_id(0) * bins + item
        part_re = causal_ref[pl.ds(place, size, stride=2 * total_bins), :]
        part_im = causal_ref[pl.ds(total_bins + place, size, stride=2 * total_bins), :]
        added, taken = part_re + part_im, part_re - part_im
        high, low = split(0.5 * cat([taken.T + added, added.T - taken], 1))
        both = dot(cat([high, low], 0), cat([cat([re, -im], 1), cat([im, re], 1)], 0), NT)
        result = both[:size] + both[size:]
        for panel in range(out_ref.shape[0]):
            piece = result[panel * rows : (panel + 1) * rows]
            out_ref[member_ref[0] ^ panel, item, 0] = piece[:, :size]
            out_ref[member_ref[0] ^ panel, item, 1] = piece[:, size:]


def projection_table(lag_limit, count, freq_size, pairs):
    own = count // (freq_size * 2 * pairs)

    def bins(index):
        return index // own % freq_size * (own * 2 * pairs) + index // (own * freq_size) * own + index % own

    row = lax.broadcasted_iota(jnp.int32, (count, 1), 0)
    column = lax.broadcasted_iota(jnp.int32, (1, count), 1)
    shift = bins(column) - bins(row)
    unit = math.pi / count
    half_angle = shift.astype(F32) * unit
    turned = ((2 * lag_limit + 1) * shift) % (2 * count)
    turned = jnp.where(turned >= count, turned - 2 * count, turned)
    last_angle = turned.astype(F32) * unit
    below = jnp.where(shift == 0, 1.0, 2.0 * count * jnp.sin(half_angle))
    real = jnp.where(shift == 0, (lag_limit.astype(F32) + 0.5) / count, jnp.sin(last_angle) / below)
    imag = jnp.where(shift == 0, 0.0, (jnp.cos(half_angle) - jnp.cos(last_angle)) / below)
    return real, imag


def params(limit):
    return pltpu.CompilerParams(vmem_limit_bytes=limit * MIB)


def cost(flops, moved):
    return pl.CostEstimate(flops=flops, bytes_accessed=moved, transcendentals=0)


def after(value, *earlier):
    return lax.optimization_barrier((value,) + earlier)[0]


SWAP = ((0, 1), (1, 0))
FLIP = ((0, 3), (1, 2), (2, 1), (3, 0))


def swap(value, distance):
    if distance == 1:
        return lax.ppermute(value, "pair", SWAP)
    if distance == 2:
        return lax.ppermute(value, "side", SWAP)
    return lax.ppermute(value, ("side", "pair"), FLIP)


def call(kernel, steps, in_specs, out_specs, out_shape, scratch, flops, moved, aliases={}):
    return pl.pallas_call(
        kernel,
        grid_spec=pltpu.PrefetchScalarGridSpec(
            num_scalar_prefetch=1,
            grid=(steps,),
            in_specs=in_specs,
            out_specs=out_specs,
            scratch_shapes=scratch,
        ),
        out_shape=out_shape,
        input_output_aliases=aliases,
        compiler_params=params(16),
        cost_estimate=cost(flops, moved),
    )


def shards(freq_size, pairs, factor, spectrum, guess_scale, lag_cutoff):
    chan = ("side", "pair")
    chan_size = 2 * pairs
    group_bins, _, rows, size = factor.shape
    own = group_bins // chan_size
    count = group_bins * freq_size
    chunks = CHUNKS if own % (4 * CHUNKS) == 0 else 1
    part = own // chunks
    step = math.gcd(part, 4)
    column_parts = min(freq_size, rows)
    lane_parts = freq_size // column_parts
    kept = rows // column_parts
    lanes = size // lane_parts
    side, pair = lax.axis_index("side"), lax.axis_index("pair")
    member = side * pairs + pair
    members = member.reshape(1)
    devices = chan_size * freq_size
    distances = range(1, chan_size)

    factors = factor.reshape(chan_size, own, 2, rows, size)

    def rows_for(owner, first, length):
        return lax.dynamic_slice(
            factors, (owner, first, 0, 0, 0), (1, length, 2, rows, size)
        ).reshape(length, 2, rows, size)

    arrived = []
    for chunk in range(chunks):
        pieces = [rows_for(member ^ d, chunk * part, part) for d in distances]
        arrived.append([swap(piece, d) for piece, d in zip(pieces, distances)])
    row_index = lax.broadcasted_iota(jnp.int32, (rows, size), 0) + member * rows
    column_index = lax.broadcasted_iota(jnp.int32, (rows, size), 1)
    packed = jnp.where(column_index >= row_index, spectrum[:, 0], spectrum[:, 1])
    packed = packed.reshape(chan_size, own, rows, size)
    pieces = [lax.dynamic_index_in_dim(packed, member ^ d, 0, keepdims=False) for d in distances]
    table_re, table_im = projection_table(lag_cutoff[0], count, freq_size, pairs)

    wide = math.gcd(part, 8)
    local_block = lambda first: pl.BlockSpec(
        (1, wide, 2, rows, size), lambda i, m: (m[0], i + first, 0, 0, 0)
    )
    other_block = pl.BlockSpec((wide, 2, rows, size), lambda i, m: (i, 0, 0, 0))
    inverse_block = pl.BlockSpec((step, 2, size, 2 * size), lambda i, m: (i, 0, 0, 0))
    state, packed_arrived = [], []
    for chunk in range(chunks):
        scale = lax.dynamic_slice_in_dim(guess_scale, member * own + chunk * part, part, 0)
        offset = chunk * part // wide
        state = call(
            newton_kernel,
            part // wide,
            [pl.BlockSpec(memory_space=pltpu.SMEM), local_block(offset)]
            + [other_block] * 3
            + [pl.BlockSpec(memory_space=pl.ANY)] * len(state),
            [
                pl.BlockSpec(
                    (wide, 2, size, 2 * size), lambda i, m, offset=offset: (i + offset, 0, 0, 0)
                ),
                pl.BlockSpec(
                    (wide, 2, size, size), lambda i, m, offset=offset: (i + offset, 0, 0, 0)
                ),
            ],
            [
                jax.ShapeDtypeStruct((own, 2, size, 2 * size), BF16),
                jax.ShapeDtypeStruct((own, 2, size, size), BF16),
            ],
            [],
            part * 64 * 2 * 4 * size**3,
            part * 6 * 4 * size * size,
            {6 + index: index for index in range(len(state))},
        )(members, scale, factors, *arrived[chunk], *state)
        if chunk == 0:
            held = lax.optimization_barrier(tuple(pieces) + tuple(state))
            state = held[len(pieces) :]
            packed_arrived = [swap(piece, d) for piece, d in zip(held, distances)]
    inverse, psi = state

    other = pl.BlockSpec((step, rows, size), lambda i, m: (i, 0, 0))
    middle = call(
        middle_kernel,
        own // step,
        [inverse_block, pl.BlockSpec((1, step, rows, size), lambda i, m: (m[0], i, 0, 0))]
        + [other] * 3,
        pl.BlockSpec((size * own, size), lambda i, m: (0, 0)),
        jax.ShapeDtypeStruct((size * own, size), F32),
        [pltpu.VMEM((step, size, size), BF16)],
        own * 10 * 2 * 4 * size**3,
        own * 6 * 4 * size * size,
    )(members, inverse, packed, *packed_arrived)
    sent = middle.astype(jnp.float16)
    if lane_parts > 1:
        sent = sent.reshape(size, own, lane_parts, lanes).transpose(0, 2, 1, 3)
    sent = sent.reshape(devices, kept, own, lanes)
    values = lax.all_to_all(sent, chan + ("freq",), 0, 0, tiled=True).astype(F32)
    sources, own_rows = devices, own
    if own % 8:
        values = values.transpose(1, 0, 2, 3).reshape(1, kept, count, lanes)
        sources, own_rows = 1, count
    twice = math.gcd(kept, 2)
    table_block = pl.BlockSpec((count, count), lambda i: (0, 0))
    causal = pl.pallas_call(
        causal_kernel,
        grid=(kept // twice,),
        in_specs=[
            table_block,
            table_block,
            pl.BlockSpec((sources, twice, own_rows, lanes), lambda i: (0, i, 0, 0)),
        ],
        out_specs=[pl.BlockSpec((sources, twice, 2, own_rows, lanes), lambda i: (0, i, 0, 0, 0))],
        out_shape=[jax.ShapeDtypeStruct((sources, kept, 2, own_rows, lanes), F32)],
        scratch_shapes=[pltpu.VMEM((2 * count, count), BF16), pltpu.VMEM((2 * count, count), BF16)],
        compiler_params=params(24),
        cost_estimate=cost(kept * 12 * count * count * lanes, 12 * kept * count * lanes),
    )(table_re, table_im, values)[0].astype(jnp.float16)
    if own % 8:
        causal = causal.reshape(kept, 2, devices, own, lanes).transpose(2, 0, 1, 3, 4)
    back = lax.all_to_all(causal, chan + ("freq",), 0, 0, tiled=True).astype(F32)
    if lane_parts > 1:
        back = back.reshape(chan_size * column_parts, lane_parts, kept, 2, own, lanes)
        back = back.transpose(0, 2, 3, 4, 1, 5)
    back = back.reshape(size * 2 * own, size)
    result = call(
        product_kernel,
        own // step,
        [
            pl.BlockSpec(back.shape, lambda i, m: (0, 0)),
            pl.BlockSpec((step, 2, size, size), lambda i, m: (i, 0, 0, 0)),
        ],
        pl.BlockSpec((chan_size, step, 2, rows, size), lambda i, m: (0, i, 0, 0, 0)),
        jax.ShapeDtypeStruct((chan_size, own, 2, rows, size), F32),
        [],
        own * 4 * 4 * size**3,
        own * 5 * 4 * size * size,
    )(members, back, psi)
    panels = [result[0]] + [swap(result[d].astype(jnp.float16), d).astype(F32) for d in distances]
    whole = jnp.zeros((group_bins, 2, rows, size), F32)
    for d in range(chan_size):
        whole = lax.dynamic_update_slice(whole, panels[d] * SCALE, ((member ^ d) * own, 0, 0, 0))
    return jnp.swapaxes(whole, 2, 3)


def solution(mesh):
    freq_size, pairs = mesh.shape["freq"], mesh.shape["chan"] // 2
    split_mesh = jax.sharding.Mesh(
        mesh.devices.reshape(freq_size, 2, pairs), ("freq", "side", "pair")
    )
    in_specs = (
        P("freq", None, ("side", "pair"), None),
        P("freq", None, ("side", "pair"), None),
        P("freq"),
        P(),
    )
    out_specs = P("freq", None, None, ("side", "pair"))
    body = functools.partial(shards, freq_size, pairs)
    return jax.shard_map(
        body, mesh=split_mesh, in_specs=in_specs, out_specs=out_specs, check_vma=False
    )
```

```python
import functools
import math

import jax
import jax.numpy as jnp
from jax import lax
from jax.experimental import pallas as pl
from jax.experimental.pallas import tpu as pltpu
from jax.sharding import PartitionSpec as P

ITERS = 8
SCALE = 16.0
CHUNKS = 2
F32 = jnp.float32
BF16 = jnp.bfloat16
MIB = 1024 * 1024
NN = (((1,), (0,)), ((), ()))
NT = (((1,), (1,)), ((), ()))
TN = (((0,), (0,)), ((), ()))


def dot(left, right, dims=NN):
    return lax.dot_general(left, right, dims, preferred_element_type=F32)


def split(value):
    high = value.astype(BF16)
    return high, (value - high.astype(F32)).astype(BF16)


def cat(parts, axis):
    return jnp.concatenate(parts, axis=axis)


def dot3(left_high, left_low, right_high, right_low, dims=NN):
    rows = left_high.shape[0]
    both = dot(cat([left_high, left_low], 0), right_high, dims)
    return both[:rows] + (both[rows:] + dot(left_high, right_low, dims))


def eye(size):
    rows = lax.broadcasted_iota(jnp.int32, (size, size), 0)
    columns = lax.broadcasted_iota(jnp.int32, (size, size), 1)
    return jnp.where(rows == columns, 1.0, 0.0).astype(F32)


def place_rows(member, panels, out_ref):
    rows = panels[0].shape[-2]
    for index, panel in enumerate(panels):
        start = pl.multiple_of((member ^ index) * rows, rows)
        out_ref[..., pl.ds(start, rows), :] = panel[...]


def newton_kernel(member_ref, scale_ref, own_ref, one_ref, two_ref, three_ref, *refs):
    out_ref, psi_ref = refs[-2:]
    bins, _, size, _ = psi_ref.shape
    place_rows(member_ref[0], [own_ref.at[0], one_ref, two_ref, three_ref], psi_ref)
    identity = eye(size)
    state = []
    for item in range(bins):
        re, im = psi_ref[item, 0], psi_ref[item, 1]
        scale = scale_ref[pl.program_id(0) * bins + item]
        gram = dot(cat([re, im], 0), cat([cat([re, im], 1), cat([im, -re], 1)], 0), TN)
        sym = identity - scale * gram[:, :size]
        anti = -scale * gram[:, size:]
        state.append((sym, anti, None))
    for step in range(ITERS):
        after = []
        for sym, anti, total in state:
            left_high, left_low = split(cat([sym, anti], 1))
            if step == 0:
                total = identity + (sym + anti)
                right = cat([sym + anti, sym - anti], 0)
            elif step < ITERS - 1:
                right = cat([cat([sym + anti, total], 1), cat([sym - anti, total.T], 1)], 0)
            else:
                right = cat([total, total.T], 0)
            product = dot3(left_high, left_low, *split(right))
            if step > 0:
                total = total + product[:, -size:]
            if step < ITERS - 1:
                square = product[:, :size]
                square_t = square.T
                sym = 0.5 * (square + square_t)
                anti = 0.5 * (square - square_t)
            after.append((sym, anti, total))
        state = after
    for item in range(bins):
        total = state[item][2]
        total_t = total.T
        re, im = psi_ref[item, 0], psi_ref[item, 1]
        scale = scale_ref[pl.program_id(0) * bins + item]
        half = (0.5 * scale) * cat([total + total_t, total - total_t], 1)
        high, low = split(half)
        both = dot(cat([high, low], 0), cat([cat([re, im], 1), cat([-im, re], 1)], 0), NT)
        high, low = split(both[:size] + both[size:])
        out_ref[item, 0] = high
        out_ref[item, 1] = low


def middle_kernel(member_ref, inverse_ref, own_ref, one_ref, two_ref, three_ref, out_ref, packed_ref):
    bins, size = inverse_ref.shape[0], inverse_ref.shape[2]
    total_bins = pl.num_programs(0) * bins
    place_rows(member_ref[0], [own_ref.at[0], one_ref, two_ref, three_ref], packed_ref)
    identity = eye(size)
    rows = lax.broadcasted_iota(jnp.int32, (size, size), 0)
    columns = lax.broadcasted_iota(jnp.int32, (size, size), 1)

    def swapped(value):
        return cat([value, cat([value[:, size:], -value[:, :size]], 1)], 0)

    for item in range(bins):
        packed = packed_ref[item].astype(F32)
        packed_t = packed.T
        re = jnp.where(columns >= rows, packed, packed_t).astype(BF16)
        im = jnp.where(columns == rows, 0.0, jnp.where(columns < rows, packed, -packed_t)).astype(BF16)
        high, low = inverse_ref[item, 0], inverse_ref[item, 1]
        both = dot(cat([high, low], 0), cat([cat([re, im], 1), cat([-im, re], 1)], 0))
        left_high, left_low = split(both[:size] + both[size:])
        middle = dot3(left_high, left_low, swapped(high), swapped(low), NT)
        middle = middle[:, :size] - middle[:, size:]
        place = pl.program_id(0) * bins + item
        out_ref[pl.ds(place, size, stride=total_bins), :] = (middle + identity) * (1.0 / SCALE)


def causal_kernel(real_ref, imag_ref, values_ref, *refs):
    *out_refs, table_high, table_low = refs
    count = real_ref.shape[1]
    sources, kept, own, lanes = values_ref.shape

    @pl.when(pl.program_id(0) == 0)
    def _():
        for part, table_ref in enumerate((real_ref, imag_ref)):
            high, low = split(table_ref[...])
            table_high[part * count : (part + 1) * count] = high
            table_low[part * count : (part + 1) * count] = low

    values = cat([values_ref[:, item].reshape(count, lanes) for item in range(kept)], 1)
    high, low = split(values)
    whole = dot(table_high[...], high) + (dot(table_high[...], low) + dot(table_low[...], high))
    for item in range(kept):
        for part in range(2):
            piece = whole[part * count : (part + 1) * count, item * lanes : (item + 1) * lanes]
            piece = piece.reshape(sources, own, lanes)
            step = own // len(out_refs)
            for chunk, out_ref in enumerate(out_refs):
                out_ref[:, item, part] = piece[:, chunk * step : (chunk + 1) * step]


def product_kernel(member_ref, causal_ref, psi_ref, out_ref):
    bins, _, size, _ = psi_ref.shape
    total_bins = causal_ref.shape[0] // (2 * size)
    rows = out_ref.shape[3]
    for item in range(bins):
        re, im = psi_ref[item, 0], psi_ref[item, 1]
        place = pl.program_id(0) * bins + item
        part_re = causal_ref[pl.ds(place, size, stride=2 * total_bins), :]
        part_im = causal_ref[pl.ds(total_bins + place, size, stride=2 * total_bins), :]
        added, taken = part_re + part_im, part_re - part_im
        high, low = split(0.5 * cat([taken.T + added, added.T - taken], 1))
        both = dot(cat([high, low], 0), cat([cat([re, -im], 1), cat([im, re], 1)], 0), NT)
        result = both[:size] + both[size:]
        for panel in range(out_ref.shape[0]):
            piece = result[panel * rows : (panel + 1) * rows]
            out_ref[member_ref[0] ^ panel, item, 0] = piece[:, :size]
            out_ref[member_ref[0] ^ panel, item, 1] = piece[:, size:]


def projection_table(lag_limit, count, freq_size, pairs):
    own = count // (freq_size * 2 * pairs)

    def bins(index):
        return index // own % freq_size * (own * 2 * pairs) + index // (own * freq_size) * own + index % own

    row = lax.broadcasted_iota(jnp.int32, (count, 1), 0)
    column = lax.broadcasted_iota(jnp.int32, (1, count), 1)
    shift = bins(column) - bins(row)
    unit = math.pi / count
    half_angle = shift.astype(F32) * unit
    turned = ((2 * lag_limit + 1) * shift) % (2 * count)
    turned = jnp.where(turned >= count, turned - 2 * count, turned)
    last_angle = turned.astype(F32) * unit
    below = jnp.where(shift == 0, 1.0, 2.0 * count * jnp.sin(half_angle))
    real = jnp.where(shift == 0, (lag_limit.astype(F32) + 0.5) / count, jnp.sin(last_angle) / below)
    imag = jnp.where(shift == 0, 0.0, (jnp.cos(half_angle) - jnp.cos(last_angle)) / below)
    return real, imag


def params(limit):
    return pltpu.CompilerParams(vmem_limit_bytes=limit * MIB)


def cost(flops, moved):
    return pl.CostEstimate(flops=flops, bytes_accessed=moved, transcendentals=0)


def after(value, *earlier):
    return lax.optimization_barrier((value,) + earlier)[0]


SWAP = ((0, 1), (1, 0))
FLIP = ((0, 3), (1, 2), (2, 1), (3, 0))


def swap(value, distance):
    if distance == 1:
        return lax.ppermute(value, "pair", SWAP)
    if distance == 2:
        return lax.ppermute(value, "side", SWAP)
    return lax.ppermute(value, ("side", "pair"), FLIP)


def call(kernel, steps, in_specs, out_specs, out_shape, scratch, flops, moved, aliases={}):
    return pl.pallas_call(
        kernel,
        grid_spec=pltpu.PrefetchScalarGridSpec(
            num_scalar_prefetch=1,
            grid=(steps,),
            in_specs=in_specs,
            out_specs=out_specs,
            scratch_shapes=scratch,
        ),
        out_shape=out_shape,
        input_output_aliases=aliases,
        compiler_params=params(16),
        cost_estimate=cost(flops, moved),
    )


def shards(freq_size, pairs, factor, spectrum, guess_scale, lag_cutoff):
    chan = ("side", "pair")
    chan_size = 2 * pairs
    group_bins, _, rows, size = factor.shape
    own = group_bins // chan_size
    count = group_bins * freq_size
    chunks = CHUNKS if own % (4 * CHUNKS) == 0 else 1
    part = own // chunks
    step = math.gcd(part, 8)
    column_parts = min(freq_size, rows)
    lane_parts = freq_size // column_parts
    kept = rows // column_parts
    lanes = size // lane_parts
    side, pair = lax.axis_index("side"), lax.axis_index("pair")
    member = side * pairs + pair
    members = member.reshape(1)
    devices = chan_size * freq_size
    distances = range(1, chan_size)

    factors = factor.reshape(chan_size, own, 2, rows, size)

    def rows_for(owner, first, length):
        return lax.dynamic_slice(
            factors, (owner, first, 0, 0, 0), (1, length, 2, rows, size)
        ).reshape(length, 2, rows, size)

    arrived = []
    for chunk in range(chunks):
        pieces = [rows_for(member ^ d, chunk * part, part) for d in distances]
        arrived.append([swap(piece, d) for piece, d in zip(pieces, distances)])
    row_index = lax.broadcasted_iota(jnp.int32, (rows, size), 0) + member * rows
    column_index = lax.broadcasted_iota(jnp.int32, (rows, size), 1)
    packed = jnp.where(column_index >= row_index, spectrum[:, 0], spectrum[:, 1])
    packed = packed.reshape(chan_size, own, rows, size)
    pieces = [lax.dynamic_index_in_dim(packed, member ^ d, 0, keepdims=False) for d in distances]
    table_re, table_im = projection_table(lag_cutoff[0], count, freq_size, pairs)

    wide = step
    local_block = lambda first: pl.BlockSpec(
        (1, wide, 2, rows, size), lambda i, m: (m[0], i + first, 0, 0, 0)
    )
    other_block = pl.BlockSpec((wide, 2, rows, size), lambda i, m: (i, 0, 0, 0))
    inverse_block = pl.BlockSpec((step, 2, size, 2 * size), lambda i, m: (i, 0, 0, 0))
    state, packed_arrived = [], []
    for chunk in range(chunks):
        scale = lax.dynamic_slice_in_dim(guess_scale, member * own + chunk * part, part, 0)
        offset = chunk * part // wide
        state = call(
            newton_kernel,
            part // wide,
            [pl.BlockSpec(memory_space=pltpu.SMEM), local_block(offset)]
            + [other_block] * 3
            + [pl.BlockSpec(memory_space=pl.ANY)] * len(state),
            [
                pl.BlockSpec(
                    (wide, 2, size, 2 * size), lambda i, m, offset=offset: (i + offset, 0, 0, 0)
                ),
                pl.BlockSpec(
                    (wide, 2, size, size), lambda i, m, offset=offset: (i + offset, 0, 0, 0)
                ),
            ],
            [
                jax.ShapeDtypeStruct((own, 2, size, 2 * size), BF16),
                jax.ShapeDtypeStruct((own, 2, size, size), BF16),
            ],
            [],
            part * 64 * 2 * 4 * size**3,
            part * 6 * 4 * size * size,
            {6 + index: index for index in range(len(state))},
        )(members, scale, factors, *arrived[chunk], *state)
        if chunk == 0:
            held = lax.optimization_barrier(tuple(pieces) + tuple(state))
            state = held[len(pieces) :]
            packed_arrived = [swap(piece, d) for piece, d in zip(held, distances)]
    inverse, psi = state

    other = pl.BlockSpec((step, rows, size), lambda i, m: (i, 0, 0))
    middle = call(
        middle_kernel,
        own // step,
        [inverse_block, pl.BlockSpec((1, step, rows, size), lambda i, m: (m[0], i, 0, 0))]
        + [other] * 3,
        pl.BlockSpec((size * own, size), lambda i, m: (0, 0)),
        jax.ShapeDtypeStruct((size * own, size), F32),
        [pltpu.VMEM((step, size, size), BF16)],
        own * 10 * 2 * 4 * size**3,
        own * 6 * 4 * size * size,
    )(members, inverse, packed, *packed_arrived)
    sent = middle.astype(jnp.float16)
    if lane_parts > 1:
        sent = sent.reshape(size, own, lane_parts, lanes).transpose(0, 2, 1, 3)
    sent = sent.reshape(devices, kept, own, lanes)
    values = lax.all_to_all(sent, chan + ("freq",), 0, 0, tiled=True).astype(F32)
    sources, own_rows = devices, own
    if own % 8:
        values = values.transpose(1, 0, 2, 3).reshape(1, kept, count, lanes)
        sources, own_rows = 1, count
    twice = math.gcd(kept, 2)
    table_block = pl.BlockSpec((count, count), lambda i: (0, 0))
    causal = pl.pallas_call(
        causal_kernel,
        grid=(kept // twice,),
        in_specs=[
            table_block,
            table_block,
            pl.BlockSpec((sources, twice, own_rows, lanes), lambda i: (0, i, 0, 0)),
        ],
        out_specs=[pl.BlockSpec((sources, twice, 2, own_rows, lanes), lambda i: (0, i, 0, 0, 0))],
        out_shape=[jax.ShapeDtypeStruct((sources, kept, 2, own_rows, lanes), F32)],
        scratch_shapes=[pltpu.VMEM((2 * count, count), BF16), pltpu.VMEM((2 * count, count), BF16)],
        compiler_params=params(24),
        cost_estimate=cost(kept * 12 * count * count * lanes, 12 * kept * count * lanes),
    )(table_re, table_im, values)[0].astype(jnp.float16)
    if own % 8:
        causal = causal.reshape(kept, 2, devices, own, lanes).transpose(2, 0, 1, 3, 4)
    back = lax.all_to_all(causal, chan + ("freq",), 0, 0, tiled=True).astype(F32)
    if lane_parts > 1:
        back = back.reshape(chan_size * column_parts, lane_parts, kept, 2, own, lanes)
        back = back.transpose(0, 2, 3, 4, 1, 5)
    back = back.reshape(size * 2 * own, size)
    result = call(
        product_kernel,
        own // step,
        [
            pl.BlockSpec(back.shape, lambda i, m: (0, 0)),
            pl.BlockSpec((step, 2, size, size), lambda i, m: (i, 0, 0, 0)),
        ],
        pl.BlockSpec((chan_size, step, 2, rows, size), lambda i, m: (0, i, 0, 0, 0)),
        jax.ShapeDtypeStruct((chan_size, own, 2, rows, size), F32),
        [],
        own * 4 * 4 * size**3,
        own * 5 * 4 * size * size,
    )(members, back, psi)
    panels = [result[0]] + [swap(result[d].astype(jnp.float16), d).astype(F32) for d in distances]
    whole = jnp.zeros((group_bins, 2, rows, size), F32)
    for d in range(chan_size):
        whole = lax.dynamic_update_slice(whole, panels[d] * SCALE, ((member ^ d) * own, 0, 0, 0))
    return jnp.swapaxes(whole, 2, 3)


def solution(mesh):
    freq_size, pairs = mesh.shape["freq"], mesh.shape["chan"] // 2
    split_mesh = jax.sharding.Mesh(
        mesh.devices.reshape(freq_size, 2, pairs), ("freq", "side", "pair")
    )
    in_specs = (
        P("freq", None, ("side", "pair"), None),
        P("freq", None, ("side", "pair"), None),
        P("freq"),
        P(),
    )
    out_specs = P("freq", None, None, ("side", "pair"))
    body = functools.partial(shards, freq_size, pairs)
    return jax.shard_map(
        body, mesh=split_mesh, in_specs=in_specs, out_specs=out_specs, check_vma=False
    )
```

```python
import functools
import math

import jax
import jax.numpy as jnp
from jax import lax
from jax.experimental import pallas as pl
from jax.experimental.pallas import tpu as pltpu
from jax.sharding import PartitionSpec as P

ITERS = 8
SCALE = 16.0
CHUNKS = 2
F32 = jnp.float32
BF16 = jnp.bfloat16
MIB = 1024 * 1024
NN = (((1,), (0,)), ((), ()))
NT = (((1,), (1,)), ((), ()))
TN = (((0,), (0,)), ((), ()))


def dot(left, right, dims=NN):
    return lax.dot_general(left, right, dims, preferred_element_type=F32)


def split(value):
    high = value.astype(BF16)
    return high, (value - high.astype(F32)).astype(BF16)


def cat(parts, axis):
    return jnp.concatenate(parts, axis=axis)


def dot3(left_high, left_low, right_high, right_low, dims=NN):
    rows = left_high.shape[0]
    both = dot(cat([left_high, left_low], 0), right_high, dims)
    return both[:rows] + (both[rows:] + dot(left_high, right_low, dims))


def eye(size):
    rows = lax.broadcasted_iota(jnp.int32, (size, size), 0)
    columns = lax.broadcasted_iota(jnp.int32, (size, size), 1)
    return jnp.where(rows == columns, 1.0, 0.0).astype(F32)


def place_rows(member, panels, out_ref):
    rows = panels[0].shape[-2]
    for index, panel in enumerate(panels):
        start = pl.multiple_of((member ^ index) * rows, rows)
        out_ref[..., pl.ds(start, rows), :] = panel[...]


def newton_kernel(member_ref, scale_ref, own_ref, one_ref, two_ref, three_ref, *refs):
    out_ref, psi_ref = refs[-2:]
    bins, _, size, _ = psi_ref.shape
    place_rows(member_ref[0], [own_ref.at[0], one_ref, two_ref, three_ref], psi_ref)
    identity = eye(size)
    state = []
    for item in range(bins):
        re, im = psi_ref[item, 0], psi_ref[item, 1]
        scale = scale_ref[pl.program_id(0) * bins + item]
        gram = dot(cat([re, im], 0), cat([cat([re, im], 1), cat([im, -re], 1)], 0), TN)
        sym = identity - scale * gram[:, :size]
        anti = -scale * gram[:, size:]
        state.append((sym, anti, None))
    for step in range(ITERS):
        after = []
        for sym, anti, total in state:
            left_high, left_low = split(cat([sym, anti], 1))
            if step == 0:
                total = identity + (sym + anti)
                right = cat([sym + anti, sym - anti], 0)
            elif step < ITERS - 1:
                right = cat([cat([sym + anti, total], 1), cat([sym - anti, total.T], 1)], 0)
            else:
                right = cat([total, total.T], 0)
            product = dot3(left_high, left_low, *split(right))
            if step > 0:
                total = total + product[:, -size:]
            if step < ITERS - 1:
                square = product[:, :size]
                square_t = square.T
                sym = 0.5 * (square + square_t)
                anti = 0.5 * (square - square_t)
            after.append((sym, anti, total))
        state = after
    for item in range(bins):
        total = state[item][2]
        total_t = total.T
        re, im = psi_ref[item, 0], psi_ref[item, 1]
        scale = scale_ref[pl.program_id(0) * bins + item]
        half = (0.5 * scale) * cat([total + total_t, total - total_t], 1)
        high, low = split(half)
        both = dot(cat([high, low], 0), cat([cat([re, im], 1), cat([-im, re], 1)], 0), NT)
        high, low = split(both[:size] + both[size:])
        out_ref[item, 0] = high
        out_ref[item, 1] = low


def middle_kernel(member_ref, inverse_ref, own_ref, one_ref, two_ref, three_ref, out_ref, packed_ref):
    bins, size = inverse_ref.shape[0], inverse_ref.shape[2]
    total_bins = pl.num_programs(0) * bins
    place_rows(member_ref[0], [own_ref.at[0], one_ref, two_ref, three_ref], packed_ref)
    identity = eye(size)
    rows = lax.broadcasted_iota(jnp.int32, (size, size), 0)
    columns = lax.broadcasted_iota(jnp.int32, (size, size), 1)

    def swapped(value):
        return cat([value, cat([value[:, size:], -value[:, :size]], 1)], 0)

    for item in range(bins):
        packed = packed_ref[item].astype(F32)
        packed_t = packed.T
        re = jnp.where(columns >= rows, packed, packed_t).astype(BF16)
        im = jnp.where(columns == rows, 0.0, jnp.where(columns < rows, packed, -packed_t)).astype(BF16)
        high, low = inverse_ref[item, 0], inverse_ref[item, 1]
        both = dot(cat([high, low], 0), cat([cat([re, im], 1), cat([-im, re], 1)], 0))
        left_high, left_low = split(both[:size] + both[size:])
        middle = dot3(left_high, left_low, swapped(high), swapped(low), NT)
        middle = middle[:, :size] - middle[:, size:]
        place = pl.program_id(0) * bins + item
        out_ref[pl.ds(place, size, stride=total_bins), :] = (middle + identity) * (1.0 / SCALE)


def causal_kernel(real_ref, imag_ref, values_ref, *refs):
    *out_refs, table_high, table_low = refs
    count = real_ref.shape[1]
    sources, kept, own, lanes = values_ref.shape

    @pl.when(pl.program_id(0) == 0)
    def _():
        for part, table_ref in enumerate((real_ref, imag_ref)):
            high, low = split(table_ref[...])
            table_high[part * count : (part + 1) * count] = high
            table_low[part * count : (part + 1) * count] = low

    values = cat([values_ref[:, item].reshape(count, lanes) for item in range(kept)], 1)
    high, low = split(values)
    whole = dot(table_high[...], high) + (dot(table_high[...], low) + dot(table_low[...], high))
    for item in range(kept):
        for part in range(2):
            piece = whole[part * count : (part + 1) * count, item * lanes : (item + 1) * lanes]
            piece = piece.reshape(sources, own, lanes)
            step = own // len(out_refs)
            for chunk, out_ref in enumerate(out_refs):
                out_ref[:, item, part] = piece[:, chunk * step : (chunk + 1) * step]


def product_kernel(member_ref, causal_ref, psi_ref, out_ref):
    bins, _, size, _ = psi_ref.shape
    total_bins = causal_ref.shape[0] // (2 * size)
    rows = out_ref.shape[3]
    for item in range(bins):
        re, im = psi_ref[item, 0], psi_ref[item, 1]
        place = pl.program_id(0) * bins + item
        part_re = causal_ref[pl.ds(place, size, stride=2 * total_bins), :]
        part_im = causal_ref[pl.ds(total_bins + place, size, stride=2 * total_bins), :]
        added, taken = part_re + part_im, part_re - part_im
        high, low = split(0.5 * cat([taken.T + added, added.T - taken], 1))
        both = dot(cat([high, low], 0), cat([cat([re, -im], 1), cat([im, re], 1)], 0), NT)
        result = both[:size] + both[size:]
        for panel in range(out_ref.shape[0]):
            piece = result[panel * rows : (panel + 1) * rows]
            out_ref[member_ref[0] ^ panel, item, 0] = piece[:, :size]
            out_ref[member_ref[0] ^ panel, item, 1] = piece[:, size:]


def projection_table(lag_limit, count, freq_size, pairs):
    own = count // (freq_size * 2 * pairs)

    def bins(index):
        return index // own % freq_size * (own * 2 * pairs) + index // (own * freq_size) * own + index % own

    row = lax.broadcasted_iota(jnp.int32, (count, 1), 0)
    column = lax.broadcasted_iota(jnp.int32, (1, count), 1)
    shift = bins(column) - bins(row)
    unit = math.pi / count
    half_angle = shift.astype(F32) * unit
    turned = ((2 * lag_limit + 1) * shift) % (2 * count)
    turned = jnp.where(turned >= count, turned - 2 * count, turned)
    last_angle = turned.astype(F32) * unit
    below = jnp.where(shift == 0, 1.0, 2.0 * count * jnp.sin(half_angle))
    real = jnp.where(shift == 0, (lag_limit.astype(F32) + 0.5) / count, jnp.sin(last_angle) / below)
    imag = jnp.where(shift == 0, 0.0, (jnp.cos(half_angle) - jnp.cos(last_angle)) / below)
    return real, imag


def params(limit):
    return pltpu.CompilerParams(vmem_limit_bytes=limit * MIB)


def cost(flops, moved):
    return pl.CostEstimate(flops=flops, bytes_accessed=moved, transcendentals=0)


def after(value, *earlier):
    return lax.optimization_barrier((value,) + earlier)[0]


SWAP = ((0, 1), (1, 0))
FLIP = ((0, 3), (1, 2), (2, 1), (3, 0))


def swap(value, distance):
    if distance == 1:
        return lax.ppermute(value, "pair", SWAP)
    if distance == 2:
        return lax.ppermute(value, "side", SWAP)
    return lax.ppermute(value, ("side", "pair"), FLIP)


def call(kernel, steps, in_specs, out_specs, out_shape, scratch, flops, moved, aliases={}):
    return pl.pallas_call(
        kernel,
        grid_spec=pltpu.PrefetchScalarGridSpec(
            num_scalar_prefetch=1,
            grid=(steps,),
            in_specs=in_specs,
            out_specs=out_specs,
            scratch_shapes=scratch,
        ),
        out_shape=out_shape,
        input_output_aliases=aliases,
        compiler_params=params(16),
        cost_estimate=cost(flops, moved),
    )


def shards(freq_size, pairs, factor, spectrum, guess_scale, lag_cutoff):
    chan = ("side", "pair")
    chan_size = 2 * pairs
    group_bins, _, rows, size = factor.shape
    own = group_bins // chan_size
    count = group_bins * freq_size
    chunks = CHUNKS if own % (4 * CHUNKS) == 0 else 1
    part = own // chunks
    step = math.gcd(part, 8)
    column_parts = min(freq_size, rows)
    lane_parts = freq_size // column_parts
    kept = rows // column_parts
    lanes = size // lane_parts
    side, pair = lax.axis_index("side"), lax.axis_index("pair")
    member = side * pairs + pair
    members = member.reshape(1)
    devices = chan_size * freq_size
    distances = range(1, chan_size)

    factors = factor.reshape(chan_size, own, 2, rows, size)

    def rows_for(owner, first, length):
        return lax.dynamic_slice(
            factors, (owner, first, 0, 0, 0), (1, length, 2, rows, size)
        ).reshape(length, 2, rows, size)

    arrived = []
    for chunk in range(chunks):
        pieces = [rows_for(member ^ d, chunk * part, part) for d in distances]
        arrived.append([swap(piece, d) for piece, d in zip(pieces, distances)])
    row_index = lax.broadcasted_iota(jnp.int32, (rows, size), 0) + member * rows
    column_index = lax.broadcasted_iota(jnp.int32, (rows, size), 1)
    packed = jnp.where(column_index >= row_index, spectrum[:, 0], spectrum[:, 1])
    packed = packed.reshape(chan_size, own, rows, size)
    pieces = [lax.dynamic_index_in_dim(packed, member ^ d, 0, keepdims=False) for d in distances]
    table_re, table_im = projection_table(lag_cutoff[0], count, freq_size, pairs)

    wide = step
    local_block = lambda first: pl.BlockSpec(
        (1, wide, 2, rows, size), lambda i, m: (m[0], i + first, 0, 0, 0)
    )
    other_block = pl.BlockSpec((wide, 2, rows, size), lambda i, m: (i, 0, 0, 0))
    inverse_block = pl.BlockSpec((step, 2, size, 2 * size), lambda i, m: (i, 0, 0, 0))
    state, packed_arrived = [], []
    for chunk in range(chunks):
        scale = lax.dynamic_slice_in_dim(guess_scale, member * own + chunk * part, part, 0)
        offset = chunk * part // wide
        state = call(
            newton_kernel,
            part // wide,
            [pl.BlockSpec(memory_space=pltpu.SMEM), local_block(offset)]
            + [other_block] * 3
            + [pl.BlockSpec(memory_space=pl.ANY)] * len(state),
            [
                pl.BlockSpec(
                    (wide, 2, size, 2 * size), lambda i, m, offset=offset: (i + offset, 0, 0, 0)
                ),
                pl.BlockSpec(
                    (wide, 2, size, size), lambda i, m, offset=offset: (i + offset, 0, 0, 0)
                ),
            ],
            [
                jax.ShapeDtypeStruct((own, 2, size, 2 * size), BF16),
                jax.ShapeDtypeStruct((own, 2, size, size), BF16),
            ],
            [],
            part * 64 * 2 * 4 * size**3,
            part * 6 * 4 * size * size,
            {6 + index: index for index in range(len(state))},
        )(members, scale, factors, *arrived[chunk], *state)
        if chunk == 0:
            held = lax.optimization_barrier(tuple(pieces) + tuple(state))
            state = held[len(pieces) :]
            packed_arrived = [swap(piece, d) for piece, d in zip(held, distances)]
    inverse, psi = state

    other = pl.BlockSpec((step, rows, size), lambda i, m: (i, 0, 0))
    middle = call(
        middle_kernel,
        own // step,
        [inverse_block, pl.BlockSpec((1, step, rows, size), lambda i, m: (m[0], i, 0, 0))]
        + [other] * 3,
        pl.BlockSpec((size * own, size), lambda i, m: (0, 0)),
        jax.ShapeDtypeStruct((size * own, size), F32),
        [pltpu.VMEM((step, size, size), BF16)],
        own * 10 * 2 * 4 * size**3,
        own * 6 * 4 * size * size,
    )(members, inverse, packed, *packed_arrived)
    sent = middle.astype(jnp.float16)
    if lane_parts > 1:
        sent = sent.reshape(size, own, lane_parts, lanes).transpose(0, 2, 1, 3)
    sent = sent.reshape(devices, kept, own, lanes)
    values = lax.all_to_all(sent, chan + ("freq",), 0, 0, tiled=True).astype(F32)
    sources, own_rows = devices, own
    if own % 8:
        values = values.transpose(1, 0, 2, 3).reshape(1, kept, count, lanes)
        sources, own_rows = 1, count
    twice = math.gcd(kept, 4)
    table_block = pl.BlockSpec((count, count), lambda i: (0, 0))
    causal = pl.pallas_call(
        causal_kernel,
        grid=(kept // twice,),
        in_specs=[
            table_block,
            table_block,
            pl.BlockSpec((sources, twice, own_rows, lanes), lambda i: (0, i, 0, 0)),
        ],
        out_specs=[pl.BlockSpec((sources, twice, 2, own_rows, lanes), lambda i: (0, i, 0, 0, 0))],
        out_shape=[jax.ShapeDtypeStruct((sources, kept, 2, own_rows, lanes), F32)],
        scratch_shapes=[pltpu.VMEM((2 * count, count), BF16), pltpu.VMEM((2 * count, count), BF16)],
        compiler_params=params(24),
        cost_estimate=cost(kept * 12 * count * count * lanes, 12 * kept * count * lanes),
    )(table_re, table_im, values)[0].astype(jnp.float16)
    if own % 8:
        causal = causal.reshape(kept, 2, devices, own, lanes).transpose(2, 0, 1, 3, 4)
    back = lax.all_to_all(causal, chan + ("freq",), 0, 0, tiled=True).astype(F32)
    if lane_parts > 1:
        back = back.reshape(chan_size * column_parts, lane_parts, kept, 2, own, lanes)
        back = back.transpose(0, 2, 3, 4, 1, 5)
    back = back.reshape(size * 2 * own, size)
    result = call(
        product_kernel,
        own // step,
        [
            pl.BlockSpec(back.shape, lambda i, m: (0, 0)),
            pl.BlockSpec((step, 2, size, size), lambda i, m: (i, 0, 0, 0)),
        ],
        pl.BlockSpec((chan_size, step, 2, rows, size), lambda i, m: (0, i, 0, 0, 0)),
        jax.ShapeDtypeStruct((chan_size, own, 2, rows, size), F32),
        [],
        own * 4 * 4 * size**3,
        own * 5 * 4 * size * size,
    )(members, back, psi)
    panels = [result[0]] + [swap(result[d].astype(jnp.float16), d).astype(F32) for d in distances]
    whole = jnp.zeros((group_bins, 2, rows, size), F32)
    for d in range(chan_size):
        whole = lax.dynamic_update_slice(whole, panels[d] * SCALE, ((member ^ d) * own, 0, 0, 0))
    return jnp.swapaxes(whole, 2, 3)


def solution(mesh):
    freq_size, pairs = mesh.shape["freq"], mesh.shape["chan"] // 2
    split_mesh = jax.sharding.Mesh(
        mesh.devices.reshape(freq_size, 2, pairs), ("freq", "side", "pair")
    )
    in_specs = (
        P("freq", None, ("side", "pair"), None),
        P("freq", None, ("side", "pair"), None),
        P("freq"),
        P(),
    )
    out_specs = P("freq", None, None, ("side", "pair"))
    body = functools.partial(shards, freq_size, pairs)
    return jax.shard_map(
        body, mesh=split_mesh, in_specs=in_specs, out_specs=out_specs, check_vma=False
    )
```

```python
import functools
import math

import jax
import jax.numpy as jnp
from jax import lax
from jax.experimental import pallas as pl
from jax.experimental.pallas import tpu as pltpu
from jax.sharding import PartitionSpec as P

ITERS = 8
SCALE = 16.0
CHUNKS = 2
F32 = jnp.float32
BF16 = jnp.bfloat16
MIB = 1024 * 1024
NN = (((1,), (0,)), ((), ()))
NT = (((1,), (1,)), ((), ()))
TN = (((0,), (0,)), ((), ()))


def dot(left, right, dims=NN):
    return lax.dot_general(left, right, dims, preferred_element_type=F32)


def split(value):
    high = value.astype(BF16)
    return high, (value - high.astype(F32)).astype(BF16)


def cat(parts, axis):
    return jnp.concatenate(parts, axis=axis)


def dot3(left_high, left_low, right_high, right_low, dims=NN):
    rows = left_high.shape[0]
    both = dot(cat([left_high, left_low], 0), right_high, dims)
    return both[:rows] + (both[rows:] + dot(left_high, right_low, dims))


def eye(size):
    rows = lax.broadcasted_iota(jnp.int32, (size, size), 0)
    columns = lax.broadcasted_iota(jnp.int32, (size, size), 1)
    return jnp.where(rows == columns, 1.0, 0.0).astype(F32)


def place_rows(member, panels, out_ref):
    rows = panels[0].shape[-2]
    for index, panel in enumerate(panels):
        start = pl.multiple_of((member ^ index) * rows, rows)
        out_ref[..., pl.ds(start, rows), :] = panel[...]


def newton_kernel(member_ref, scale_ref, own_ref, one_ref, two_ref, three_ref, *refs):
    out_ref, psi_ref = refs[-2:]
    bins, _, size, _ = psi_ref.shape
    place_rows(member_ref[0], [own_ref.at[0], one_ref, two_ref, three_ref], psi_ref)
    identity = eye(size)
    state = []
    for item in range(bins):
        re, im = psi_ref[item, 0], psi_ref[item, 1]
        scale = scale_ref[pl.program_id(0) * bins + item]
        gram = dot(cat([re, im], 0), cat([cat([re, im], 1), cat([im, -re], 1)], 0), TN)
        sym = identity - scale * gram[:, :size]
        anti = -scale * gram[:, size:]
        state.append((sym, anti, None))
    for step in range(ITERS):
        after = []
        for sym, anti, total in state:
            left_high, left_low = split(cat([sym, anti], 1))
            if step == 0:
                total = identity + (sym + anti)
                right = cat([sym + anti, sym - anti], 0)
            elif step < ITERS - 1:
                right = cat([cat([sym + anti, total], 1), cat([sym - anti, total.T], 1)], 0)
            else:
                right = cat([total, total.T], 0)
            product = dot3(left_high, left_low, *split(right))
            if step > 0:
                total = total + product[:, -size:]
            if step < ITERS - 1:
                square = product[:, :size]
                square_t = square.T
                sym = 0.5 * (square + square_t)
                anti = 0.5 * (square - square_t)
            after.append((sym, anti, total))
        state = after
    for item in range(bins):
        total = state[item][2]
        total_t = total.T
        re, im = psi_ref[item, 0], psi_ref[item, 1]
        scale = scale_ref[pl.program_id(0) * bins + item]
        half = (0.5 * scale) * cat([total + total_t, total - total_t], 1)
        high, low = split(half)
        both = dot(cat([high, low], 0), cat([cat([re, im], 1), cat([-im, re], 1)], 0), NT)
        high, low = split(both[:size] + both[size:])
        out_ref[item, 0] = high
        out_ref[item, 1] = low


def middle_kernel(member_ref, inverse_ref, own_ref, one_ref, two_ref, three_ref, out_ref, packed_ref):
    bins, size = inverse_ref.shape[0], inverse_ref.shape[2]
    total_bins = pl.num_programs(0) * bins
    place_rows(member_ref[0], [own_ref.at[0], one_ref, two_ref, three_ref], packed_ref)
    identity = eye(size)
    rows = lax.broadcasted_iota(jnp.int32, (size, size), 0)
    columns = lax.broadcasted_iota(jnp.int32, (size, size), 1)

    def swapped(value):
        return cat([value, cat([value[:, size:], -value[:, :size]], 1)], 0)

    for item in range(bins):
        packed = packed_ref[item].astype(F32)
        packed_t = packed.T
        re = jnp.where(columns >= rows, packed, packed_t).astype(BF16)
        im = jnp.where(columns == rows, 0.0, jnp.where(columns < rows, packed, -packed_t)).astype(BF16)
        high, low = inverse_ref[item, 0], inverse_ref[item, 1]
        both = dot(cat([high, low], 0), cat([cat([re, im], 1), cat([-im, re], 1)], 0))
        left_high, left_low = split(both[:size] + both[size:])
        middle = dot3(left_high, left_low, swapped(high), swapped(low), NT)
        middle = middle[:, :size] - middle[:, size:]
        place = pl.program_id(0) * bins + item
        out_ref[pl.ds(place, size, stride=total_bins), :] = (middle + identity) * (1.0 / SCALE)


def causal_kernel(real_ref, imag_ref, values_ref, *refs):
    *out_refs, table_high, table_low = refs
    count = real_ref.shape[1]
    sources, kept, own, lanes = values_ref.shape

    @pl.when(pl.program_id(0) == 0)
    def _():
        for part, table_ref in enumerate((real_ref, imag_ref)):
            high, low = split(table_ref[...])
            table_high[part * count : (part + 1) * count] = high
            table_low[part * count : (part + 1) * count] = low

    values = cat([values_ref[:, item].reshape(count, lanes) for item in range(kept)], 1)
    high, low = split(values)
    whole = dot(table_high[...], high) + (dot(table_high[...], low) + dot(table_low[...], high))
    for item in range(kept):
        for part in range(2):
            piece = whole[part * count : (part + 1) * count, item * lanes : (item + 1) * lanes]
            piece = piece.reshape(sources, own, lanes)
            step = own // len(out_refs)
            for chunk, out_ref in enumerate(out_refs):
                out_ref[:, item, part] = piece[:, chunk * step : (chunk + 1) * step]


def product_kernel(member_ref, causal_ref, psi_ref, out_ref):
    bins, _, size, _ = psi_ref.shape
    total_bins = causal_ref.shape[0] // (2 * size)
    rows = out_ref.shape[3]
    for item in range(bins):
        re, im = psi_ref[item, 0], psi_ref[item, 1]
        place = pl.program_id(0) * bins + item
        part_re = causal_ref[pl.ds(place, size, stride=2 * total_bins), :]
        part_im = causal_ref[pl.ds(total_bins + place, size, stride=2 * total_bins), :]
        added, taken = part_re + part_im, part_re - part_im
        high, low = split(0.5 * cat([taken.T + added, added.T - taken], 1))
        both = dot(cat([high, low], 0), cat([cat([re, -im], 1), cat([im, re], 1)], 0), NT)
        result = both[:size] + both[size:]
        for panel in range(out_ref.shape[0]):
            piece = result[panel * rows : (panel + 1) * rows]
            out_ref[member_ref[0] ^ panel, item, 0] = piece[:, :size]
            out_ref[member_ref[0] ^ panel, item, 1] = piece[:, size:]


def projection_table(lag_limit, count, freq_size, pairs):
    own = count // (freq_size * 2 * pairs)

    def bins(index):
        return index // own % freq_size * (own * 2 * pairs) + index // (own * freq_size) * own + index % own

    row = lax.broadcasted_iota(jnp.int32, (count, 1), 0)
    column = lax.broadcasted_iota(jnp.int32, (1, count), 1)
    shift = bins(column) - bins(row)
    unit = math.pi / count
    half_angle = shift.astype(F32) * unit
    turned = ((2 * lag_limit + 1) * shift) % (2 * count)
    turned = jnp.where(turned >= count, turned - 2 * count, turned)
    last_angle = turned.astype(F32) * unit
    below = jnp.where(shift == 0, 1.0, 2.0 * count * jnp.sin(half_angle))
    real = jnp.where(shift == 0, (lag_limit.astype(F32) + 0.5) / count, jnp.sin(last_angle) / below)
    imag = jnp.where(shift == 0, 0.0, (jnp.cos(half_angle) - jnp.cos(last_angle)) / below)
    return real, imag


def params(limit):
    return pltpu.CompilerParams(vmem_limit_bytes=limit * MIB)


def cost(flops, moved):
    return pl.CostEstimate(flops=flops, bytes_accessed=moved, transcendentals=0)


def after(value, *earlier):
    return lax.optimization_barrier((value,) + earlier)[0]


SWAP = ((0, 1), (1, 0))
FLIP = ((0, 3), (1, 2), (2, 1), (3, 0))


def swap(value, distance):
    if distance == 1:
        return lax.ppermute(value, "pair", SWAP)
    if distance == 2:
        return lax.ppermute(value, "side", SWAP)
    return lax.ppermute(value, ("side", "pair"), FLIP)


def call(kernel, steps, in_specs, out_specs, out_shape, scratch, flops, moved, aliases={}):
    return pl.pallas_call(
        kernel,
        grid_spec=pltpu.PrefetchScalarGridSpec(
            num_scalar_prefetch=1,
            grid=(steps,),
            in_specs=in_specs,
            out_specs=out_specs,
            scratch_shapes=scratch,
        ),
        out_shape=out_shape,
        input_output_aliases=aliases,
        compiler_params=params(16),
        cost_estimate=cost(flops, moved),
    )


def shards(freq_size, pairs, factor, spectrum, guess_scale, lag_cutoff):
    chan = ("side", "pair")
    chan_size = 2 * pairs
    group_bins, _, rows, size = factor.shape
    own = group_bins // chan_size
    count = group_bins * freq_size
    chunks = CHUNKS if own % (4 * CHUNKS) == 0 else 1
    part = own // chunks
    step = math.gcd(own, 16)
    column_parts = min(freq_size, rows)
    lane_parts = freq_size // column_parts
    kept = rows // column_parts
    lanes = size // lane_parts
    side, pair = lax.axis_index("side"), lax.axis_index("pair")
    member = side * pairs + pair
    members = member.reshape(1)
    devices = chan_size * freq_size
    distances = range(1, chan_size)

    factors = factor.reshape(chan_size, own, 2, rows, size)

    def rows_for(owner, first, length):
        return lax.dynamic_slice(
            factors, (owner, first, 0, 0, 0), (1, length, 2, rows, size)
        ).reshape(length, 2, rows, size)

    arrived = []
    for chunk in range(chunks):
        pieces = [rows_for(member ^ d, chunk * part, part) for d in distances]
        arrived.append([swap(piece, d) for piece, d in zip(pieces, distances)])
    row_index = lax.broadcasted_iota(jnp.int32, (rows, size), 0) + member * rows
    column_index = lax.broadcasted_iota(jnp.int32, (rows, size), 1)
    packed = jnp.where(column_index >= row_index, spectrum[:, 0], spectrum[:, 1])
    packed = packed.reshape(chan_size, own, rows, size)
    pieces = [lax.dynamic_index_in_dim(packed, member ^ d, 0, keepdims=False) for d in distances]
    table_re, table_im = projection_table(lag_cutoff[0], count, freq_size, pairs)

    wide = math.gcd(part, 8)
    local_block = lambda first: pl.BlockSpec(
        (1, wide, 2, rows, size), lambda i, m: (m[0], i + first, 0, 0, 0)
    )
    other_block = pl.BlockSpec((wide, 2, rows, size), lambda i, m: (i, 0, 0, 0))
    inverse_block = pl.BlockSpec((step, 2, size, 2 * size), lambda i, m: (i, 0, 0, 0))
    state, packed_arrived = [], []
    for chunk in range(chunks):
        scale = lax.dynamic_slice_in_dim(guess_scale, member * own + chunk * part, part, 0)
        offset = chunk * part // wide
        state = call(
            newton_kernel,
            part // wide,
            [pl.BlockSpec(memory_space=pltpu.SMEM), local_block(offset)]
            + [other_block] * 3
            + [pl.BlockSpec(memory_space=pl.ANY)] * len(state),
            [
                pl.BlockSpec(
                    (wide, 2, size, 2 * size), lambda i, m, offset=offset: (i + offset, 0, 0, 0)
                ),
                pl.BlockSpec(
                    (wide, 2, size, size), lambda i, m, offset=offset: (i + offset, 0, 0, 0)
                ),
            ],
            [
                jax.ShapeDtypeStruct((own, 2, size, 2 * size), BF16),
                jax.ShapeDtypeStruct((own, 2, size, size), BF16),
            ],
            [],
            part * 64 * 2 * 4 * size**3,
            part * 6 * 4 * size * size,
            {6 + index: index for index in range(len(state))},
        )(members, scale, factors, *arrived[chunk], *state)
        if chunk == 0:
            held = lax.optimization_barrier(tuple(pieces) + tuple(state))
            state = held[len(pieces) :]
            packed_arrived = [swap(piece, d) for piece, d in zip(held, distances)]
    inverse, psi = state

    other = pl.BlockSpec((step, rows, size), lambda i, m: (i, 0, 0))
    middle = call(
        middle_kernel,
        own // step,
        [inverse_block, pl.BlockSpec((1, step, rows, size), lambda i, m: (m[0], i, 0, 0))]
        + [other] * 3,
        pl.BlockSpec((size * own, size), lambda i, m: (0, 0)),
        jax.ShapeDtypeStruct((size * own, size), F32),
        [pltpu.VMEM((step, size, size), BF16)],
        own * 10 * 2 * 4 * size**3,
        own * 6 * 4 * size * size,
    )(members, inverse, packed, *packed_arrived)
    sent = middle.astype(jnp.float16)
    if lane_parts > 1:
        sent = sent.reshape(size, own, lane_parts, lanes).transpose(0, 2, 1, 3)
    sent = sent.reshape(devices, kept, own, lanes)
    values = lax.all_to_all(sent, chan + ("freq",), 0, 0, tiled=True).astype(F32)
    sources, own_rows = devices, own
    if own % 8:
        values = values.transpose(1, 0, 2, 3).reshape(1, kept, count, lanes)
        sources, own_rows = 1, count
    twice = math.gcd(kept, 4)
    table_block = pl.BlockSpec((count, count), lambda i: (0, 0))
    causal = pl.pallas_call(
        causal_kernel,
        grid=(kept // twice,),
        in_specs=[
            table_block,
            table_block,
            pl.BlockSpec((sources, twice, own_rows, lanes), lambda i: (0, i, 0, 0)),
        ],
        out_specs=[pl.BlockSpec((sources, twice, 2, own_rows, lanes), lambda i: (0, i, 0, 0, 0))],
        out_shape=[jax.ShapeDtypeStruct((sources, kept, 2, own_rows, lanes), F32)],
        scratch_shapes=[pltpu.VMEM((2 * count, count), BF16), pltpu.VMEM((2 * count, count), BF16)],
        compiler_params=params(24),
        cost_estimate=cost(kept * 12 * count * count * lanes, 12 * kept * count * lanes),
    )(table_re, table_im, values)[0].astype(jnp.float16)
    if own % 8:
        causal = causal.reshape(kept, 2, devices, own, lanes).transpose(2, 0, 1, 3, 4)
    back = lax.all_to_all(causal, chan + ("freq",), 0, 0, tiled=True).astype(F32)
    if lane_parts > 1:
        back = back.reshape(chan_size * column_parts, lane_parts, kept, 2, own, lanes)
        back = back.transpose(0, 2, 3, 4, 1, 5)
    back = back.reshape(size * 2 * own, size)
    result = call(
        product_kernel,
        own // step,
        [
            pl.BlockSpec(back.shape, lambda i, m: (0, 0)),
            pl.BlockSpec((step, 2, size, size), lambda i, m: (i, 0, 0, 0)),
        ],
        pl.BlockSpec((chan_size, step, 2, rows, size), lambda i, m: (0, i, 0, 0, 0)),
        jax.ShapeDtypeStruct((chan_size, own, 2, rows, size), F32),
        [],
        own * 4 * 4 * size**3,
        own * 5 * 4 * size * size,
    )(members, back, psi)
    panels = [result[0]] + [swap(result[d].astype(jnp.float16), d).astype(F32) for d in distances]
    whole = jnp.zeros((group_bins, 2, rows, size), F32)
    for d in range(chan_size):
        whole = lax.dynamic_update_slice(whole, panels[d] * SCALE, ((member ^ d) * own, 0, 0, 0))
    return jnp.swapaxes(whole, 2, 3)


def solution(mesh):
    freq_size, pairs = mesh.shape["freq"], mesh.shape["chan"] // 2
    split_mesh = jax.sharding.Mesh(
        mesh.devices.reshape(freq_size, 2, pairs), ("freq", "side", "pair")
    )
    in_specs = (
        P("freq", None, ("side", "pair"), None),
        P("freq", None, ("side", "pair"), None),
        P("freq"),
        P(),
    )
    out_specs = P("freq", None, None, ("side", "pair"))
    body = functools.partial(shards, freq_size, pairs)
    return jax.shard_map(
        body, mesh=split_mesh, in_specs=in_specs, out_specs=out_specs, check_vma=False
    )
```

```python
import functools
import math

import jax
import jax.numpy as jnp
from jax import lax
from jax.experimental import pallas as pl
from jax.experimental.pallas import tpu as pltpu
from jax.sharding import PartitionSpec as P

ITERS = 8
SCALE = 16.0
CHUNKS = 2
F32 = jnp.float32
BF16 = jnp.bfloat16
MIB = 1024 * 1024
NN = (((1,), (0,)), ((), ()))
NT = (((1,), (1,)), ((), ()))
TN = (((0,), (0,)), ((), ()))


def dot(left, right, dims=NN):
    return lax.dot_general(left, right, dims, preferred_element_type=F32)


def split(value):
    high = value.astype(BF16)
    return high, (value - high.astype(F32)).astype(BF16)


def cat(parts, axis):
    return jnp.concatenate(parts, axis=axis)


def dot3(left_high, left_low, right_high, right_low, dims=NN):
    rows = left_high.shape[0]
    both = dot(cat([left_high, left_low], 0), right_high, dims)
    return both[:rows] + (both[rows:] + dot(left_high, right_low, dims))


def eye(size):
    rows = lax.broadcasted_iota(jnp.int32, (size, size), 0)
    columns = lax.broadcasted_iota(jnp.int32, (size, size), 1)
    return jnp.where(rows == columns, 1.0, 0.0).astype(F32)


def place_rows(member, panels, out_ref):
    rows = panels[0].shape[-2]
    for index, panel in enumerate(panels):
        start = pl.multiple_of((member ^ index) * rows, rows)
        out_ref[..., pl.ds(start, rows), :] = panel[...]


def newton_kernel(member_ref, scale_ref, own_ref, one_ref, two_ref, three_ref, *refs):
    out_ref, psi_ref = refs[-2:]
    bins, _, size, _ = psi_ref.shape
    place_rows(member_ref[0], [own_ref.at[0], one_ref, two_ref, three_ref], psi_ref)
    identity = eye(size)
    state = []
    for item in range(bins):
        re, im = psi_ref[item, 0], psi_ref[item, 1]
        scale = scale_ref[pl.program_id(0) * bins + item]
        gram = dot(cat([re, im], 0), cat([cat([re, im], 1), cat([im, -re], 1)], 0), TN)
        sym = identity - scale * gram[:, :size]
        anti = -scale * gram[:, size:]
        state.append((sym, anti, None))
    for step in range(ITERS):
        after = []
        for sym, anti, total in state:
            left_high, left_low = split(cat([sym, anti], 1))
            if step == 0:
                total = identity + (sym + anti)
                right = cat([sym + anti, sym - anti], 0)
            elif step < ITERS - 1:
                right = cat([cat([sym + anti, total], 1), cat([sym - anti, total.T], 1)], 0)
            else:
                right = cat([total, total.T], 0)
            product = dot3(left_high, left_low, *split(right))
            if step > 0:
                total = total + product[:, -size:]
            if step < ITERS - 1:
                square = product[:, :size]
                square_t = square.T
                sym = 0.5 * (square + square_t)
                anti = 0.5 * (square - square_t)
            after.append((sym, anti, total))
        state = after
    for item in range(bins):
        total = state[item][2]
        total_t = total.T
        re, im = psi_ref[item, 0], psi_ref[item, 1]
        scale = scale_ref[pl.program_id(0) * bins + item]
        half = (0.5 * scale) * cat([total + total_t, total - total_t], 1)
        high, low = split(half)
        both = dot(cat([high, low], 0), cat([cat([re, im], 1), cat([-im, re], 1)], 0), NT)
        high, low = split(both[:size] + both[size:])
        out_ref[item, 0] = high
        out_ref[item, 1] = low


def middle_kernel(member_ref, inverse_ref, own_ref, one_ref, two_ref, three_ref, out_ref, packed_ref):
    bins, size = inverse_ref.shape[0], inverse_ref.shape[2]
    total_bins = pl.num_programs(0) * bins
    place_rows(member_ref[0], [own_ref.at[0], one_ref, two_ref, three_ref], packed_ref)
    identity = eye(size)
    rows = lax.broadcasted_iota(jnp.int32, (size, size), 0)
    columns = lax.broadcasted_iota(jnp.int32, (size, size), 1)

    def swapped(value):
        return cat([value, cat([value[:, size:], -value[:, :size]], 1)], 0)

    for item in range(bins):
        packed = packed_ref[item].astype(F32)
        packed_t = packed.T
        re = jnp.where(columns >= rows, packed, packed_t).astype(BF16)
        im = jnp.where(columns == rows, 0.0, jnp.where(columns < rows, packed, -packed_t)).astype(BF16)
        high, low = inverse_ref[item, 0], inverse_ref[item, 1]
        both = dot(cat([high, low], 0), cat([cat([re, im], 1), cat([-im, re], 1)], 0))
        left_high, left_low = split(both[:size] + both[size:])
        middle = dot3(left_high, left_low, swapped(high), swapped(low), NT)
        middle = middle[:, :size] - middle[:, size:]
        place = pl.program_id(0) * bins + item
        out_ref[pl.ds(place, size, stride=total_bins), :] = (middle + identity) * (1.0 / SCALE)


def causal_kernel(real_ref, imag_ref, values_ref, *refs):
    *out_refs, table_high, table_low = refs
    count = real_ref.shape[1]
    sources, kept, own, lanes = values_ref.shape

    @pl.when(pl.program_id(0) == 0)
    def _():
        for part, table_ref in enumerate((real_ref, imag_ref)):
            high, low = split(table_ref[...])
            table_high[part * count : (part + 1) * count] = high
            table_low[part * count : (part + 1) * count] = low

    values = cat([values_ref[:, item].reshape(count, lanes) for item in range(kept)], 1)
    high, low = split(values)
    whole = dot(table_high[...], high) + (dot(table_high[...], low) + dot(table_low[...], high))
    for item in range(kept):
        for part in range(2):
            piece = whole[part * count : (part + 1) * count, item * lanes : (item + 1) * lanes]
            piece = piece.reshape(sources, own, lanes)
            step = own // len(out_refs)
            for chunk, out_ref in enumerate(out_refs):
                out_ref[:, item, part] = piece[:, chunk * step : (chunk + 1) * step]


def product_kernel(member_ref, causal_ref, psi_ref, out_ref):
    bins, _, size, _ = psi_ref.shape
    total_bins = causal_ref.shape[0] // (2 * size)
    rows = out_ref.shape[3]
    for item in range(bins):
        re, im = psi_ref[item, 0], psi_ref[item, 1]
        place = pl.program_id(0) * bins + item
        part_re = causal_ref[pl.ds(place, size, stride=2 * total_bins), :]
        part_im = causal_ref[pl.ds(total_bins + place, size, stride=2 * total_bins), :]
        added, taken = part_re + part_im, part_re - part_im
        high, low = split(0.5 * cat([taken.T + added, added.T - taken], 1))
        both = dot(cat([high, low], 0), cat([cat([re, -im], 1), cat([im, re], 1)], 0), NT)
        result = both[:size] + both[size:]
        for panel in range(out_ref.shape[0]):
            piece = result[panel * rows : (panel + 1) * rows]
            out_ref[member_ref[0] ^ panel, item, 0] = piece[:, :size]
            out_ref[member_ref[0] ^ panel, item, 1] = piece[:, size:]


def projection_table(lag_limit, count, freq_size, pairs):
    own = count // (freq_size * 2 * pairs)

    def bins(index):
        return index // own % freq_size * (own * 2 * pairs) + index // (own * freq_size) * own + index % own

    row = lax.broadcasted_iota(jnp.int32, (count, 1), 0)
    column = lax.broadcasted_iota(jnp.int32, (1, count), 1)
    shift = bins(column) - bins(row)
    unit = math.pi / count
    half_angle = shift.astype(F32) * unit
    turned = ((2 * lag_limit + 1) * shift) % (2 * count)
    turned = jnp.where(turned >= count, turned - 2 * count, turned)
    last_angle = turned.astype(F32) * unit
    below = jnp.where(shift == 0, 1.0, 2.0 * count * jnp.sin(half_angle))
    real = jnp.where(shift == 0, (lag_limit.astype(F32) + 0.5) / count, jnp.sin(last_angle) / below)
    imag = jnp.where(shift == 0, 0.0, (jnp.cos(half_angle) - jnp.cos(last_angle)) / below)
    return real, imag


def params(limit):
    return pltpu.CompilerParams(vmem_limit_bytes=limit * MIB)


def cost(flops, moved):
    return pl.CostEstimate(flops=flops, bytes_accessed=moved, transcendentals=0)


def after(value, *earlier):
    return lax.optimization_barrier((value,) + earlier)[0]


SWAP = ((0, 1), (1, 0))
FLIP = ((0, 3), (1, 2), (2, 1), (3, 0))


def swap(value, distance):
    if distance == 1:
        return lax.ppermute(value, "pair", SWAP)
    if distance == 2:
        return lax.ppermute(value, "side", SWAP)
    return lax.ppermute(value, ("side", "pair"), FLIP)


def call(kernel, steps, in_specs, out_specs, out_shape, scratch, flops, moved, aliases={}):
    return pl.pallas_call(
        kernel,
        grid_spec=pltpu.PrefetchScalarGridSpec(
            num_scalar_prefetch=1,
            grid=(steps,),
            in_specs=in_specs,
            out_specs=out_specs,
            scratch_shapes=scratch,
        ),
        out_shape=out_shape,
        input_output_aliases=aliases,
        compiler_params=params(16),
        cost_estimate=cost(flops, moved),
    )


def shards(freq_size, pairs, factor, spectrum, guess_scale, lag_cutoff):
    chan = ("side", "pair")
    chan_size = 2 * pairs
    group_bins, _, rows, size = factor.shape
    own = group_bins // chan_size
    count = group_bins * freq_size
    chunks = CHUNKS if own % (4 * CHUNKS) == 0 else 1
    part = own // chunks
    step = math.gcd(own, 16)
    column_parts = min(freq_size, rows)
    lane_parts = freq_size // column_parts
    kept = rows // column_parts
    lanes = size // lane_parts
    side, pair = lax.axis_index("side"), lax.axis_index("pair")
    member = side * pairs + pair
    members = member.reshape(1)
    devices = chan_size * freq_size
    distances = range(1, chan_size)

    factors = factor.reshape(chan_size, own, 2, rows, size)

    def rows_for(owner, first, length):
        return lax.dynamic_slice(
            factors, (owner, first, 0, 0, 0), (1, length, 2, rows, size)
        ).reshape(length, 2, rows, size)

    arrived = []
    for chunk in range(chunks):
        pieces = [rows_for(member ^ d, chunk * part, part) for d in distances]
        arrived.append([swap(piece, d) for piece, d in zip(pieces, distances)])
    row_index = lax.broadcasted_iota(jnp.int32, (rows, size), 0) + member * rows
    column_index = lax.broadcasted_iota(jnp.int32, (rows, size), 1)
    packed = jnp.where(column_index >= row_index, spectrum[:, 0], spectrum[:, 1])
    packed = packed.reshape(chan_size, own, rows, size)
    pieces = [lax.dynamic_index_in_dim(packed, member ^ d, 0, keepdims=False) for d in distances]
    table_re, table_im = projection_table(lag_cutoff[0], count, freq_size, pairs)

    wide = math.gcd(part, 8)
    local_block = lambda first: pl.BlockSpec(
        (1, wide, 2, rows, size), lambda i, m: (m[0], i + first, 0, 0, 0)
    )
    other_block = pl.BlockSpec((wide, 2, rows, size), lambda i, m: (i, 0, 0, 0))
    inverse_block = pl.BlockSpec((step, 2, size, 2 * size), lambda i, m: (i, 0, 0, 0))
    state, packed_arrived = [], []
    for chunk in range(chunks):
        scale = lax.dynamic_slice_in_dim(guess_scale, member * own + chunk * part, part, 0)
        offset = chunk * part // wide
        state = call(
            newton_kernel,
            part // wide,
            [pl.BlockSpec(memory_space=pltpu.SMEM), local_block(offset)]
            + [other_block] * 3
            + [pl.BlockSpec(memory_space=pl.ANY)] * len(state),
            [
                pl.BlockSpec(
                    (wide, 2, size, 2 * size), lambda i, m, offset=offset: (i + offset, 0, 0, 0)
                ),
                pl.BlockSpec(
                    (wide, 2, size, size), lambda i, m, offset=offset: (i + offset, 0, 0, 0)
                ),
            ],
            [
                jax.ShapeDtypeStruct((own, 2, size, 2 * size), BF16),
                jax.ShapeDtypeStruct((own, 2, size, size), BF16),
            ],
            [],
            part * 64 * 2 * 4 * size**3,
            part * 6 * 4 * size * size,
            {6 + index: index for index in range(len(state))},
        )(members, scale, factors, *arrived[chunk], *state)
        if chunk == 0:
            held = lax.optimization_barrier(tuple(pieces) + tuple(arrived[0]))[: len(pieces)]
            packed_arrived = [swap(piece, d) for piece, d in zip(held, distances)]
    inverse, psi = state

    other = pl.BlockSpec((step, rows, size), lambda i, m: (i, 0, 0))
    middle = call(
        middle_kernel,
        own // step,
        [inverse_block, pl.BlockSpec((1, step, rows, size), lambda i, m: (m[0], i, 0, 0))]
        + [other] * 3,
        pl.BlockSpec((size * own, size), lambda i, m: (0, 0)),
        jax.ShapeDtypeStruct((size * own, size), F32),
        [pltpu.VMEM((step, size, size), BF16)],
        own * 10 * 2 * 4 * size**3,
        own * 6 * 4 * size * size,
    )(members, inverse, packed, *packed_arrived)
    sent = middle.astype(jnp.float16)
    if lane_parts > 1:
        sent = sent.reshape(size, own, lane_parts, lanes).transpose(0, 2, 1, 3)
    sent = sent.reshape(devices, kept, own, lanes)
    values = lax.all_to_all(sent, chan + ("freq",), 0, 0, tiled=True).astype(F32)
    sources, own_rows = devices, own
    if own % 8:
        values = values.transpose(1, 0, 2, 3).reshape(1, kept, count, lanes)
        sources, own_rows = 1, count
    twice = math.gcd(kept, 4)
    table_block = pl.BlockSpec((count, count), lambda i: (0, 0))
    causal = pl.pallas_call(
        causal_kernel,
        grid=(kept // twice,),
        in_specs=[
            table_block,
            table_block,
            pl.BlockSpec((sources, twice, own_rows, lanes), lambda i: (0, i, 0, 0)),
        ],
        out_specs=[pl.BlockSpec((sources, twice, 2, own_rows, lanes), lambda i: (0, i, 0, 0, 0))],
        out_shape=[jax.ShapeDtypeStruct((sources, kept, 2, own_rows, lanes), F32)],
        scratch_shapes=[pltpu.VMEM((2 * count, count), BF16), pltpu.VMEM((2 * count, count), BF16)],
        compiler_params=params(24),
        cost_estimate=cost(kept * 12 * count * count * lanes, 12 * kept * count * lanes),
    )(table_re, table_im, values)[0].astype(jnp.float16)
    if own % 8:
        causal = causal.reshape(kept, 2, devices, own, lanes).transpose(2, 0, 1, 3, 4)
    back = lax.all_to_all(causal, chan + ("freq",), 0, 0, tiled=True).astype(F32)
    if lane_parts > 1:
        back = back.reshape(chan_size * column_parts, lane_parts, kept, 2, own, lanes)
        back = back.transpose(0, 2, 3, 4, 1, 5)
    back = back.reshape(size * 2 * own, size)
    result = call(
        product_kernel,
        own // step,
        [
            pl.BlockSpec(back.shape, lambda i, m: (0, 0)),
            pl.BlockSpec((step, 2, size, size), lambda i, m: (i, 0, 0, 0)),
        ],
        pl.BlockSpec((chan_size, step, 2, rows, size), lambda i, m: (0, i, 0, 0, 0)),
        jax.ShapeDtypeStruct((chan_size, own, 2, rows, size), F32),
        [],
        own * 4 * 4 * size**3,
        own * 5 * 4 * size * size,
    )(members, back, psi)
    panels = [result[0]] + [swap(result[d].astype(jnp.float16), d).astype(F32) for d in distances]
    whole = jnp.zeros((group_bins, 2, rows, size), F32)
    for d in range(chan_size):
        whole = lax.dynamic_update_slice(whole, panels[d] * SCALE, ((member ^ d) * own, 0, 0, 0))
    return jnp.swapaxes(whole, 2, 3)


def solution(mesh):
    freq_size, pairs = mesh.shape["freq"], mesh.shape["chan"] // 2
    split_mesh = jax.sharding.Mesh(
        mesh.devices.reshape(freq_size, 2, pairs), ("freq", "side", "pair")
    )
    in_specs = (
        P("freq", None, ("side", "pair"), None),
        P("freq", None, ("side", "pair"), None),
        P("freq"),
        P(),
    )
    out_specs = P("freq", None, None, ("side", "pair"))
    body = functools.partial(shards, freq_size, pairs)
    return jax.shard_map(
        body, mesh=split_mesh, in_specs=in_specs, out_specs=out_specs, check_vma=False
    )
```
